256 devices in a mesh: dp: 16 (over y_hi, z), mp: 16 (over y_lo, x, core).
Axes of the slice: x: 4, y: 4 (y_hi: 2, y_lo: 2; y = y_hi * 2 + y_lo), z: 8, core: 2. Of those that a mesh axis runs over, the one named last changes fastest.
Arguments:
- tokens: bfloat16 [64, 257, 1664], P('dp', None, 'mp'), may hold values from -12 to 12
- up_ckpts: bfloat16 [2, 10, 1664, 8192], P(None, None, 'dp', 'mp'), may hold values from -0.3125 to 0.3125
- up_bias_ckpts: float32 [2, 10, 8192], P(None, None, 'mp'), may hold values from -3 to 3
- down_ckpts: bfloat16 [2, 10, 8192, 1664], P(None, None, 'mp', 'dp'), may hold values from -0.125 to 0.125
- down_bias_ckpts: float32 [2, 10, 1664], replicated, may hold values from -1.75 to 1.75
- norm_ckpts: float32 [2, 10, 1664], replicated, may hold values from 0.25 to 1.75
- soup_mask: int32 [10], replicated, may hold values from 0 to 1, as said below
- final_gain: float32 [1664], replicated, may hold values from 0.25 to 1.75
- projection: bfloat16 [1664, 1280], replicated, may hold values from -0.15625 to 0.15625
- class_embed: bfloat16 [22528, 1280], P('dp', 'mp'), may hold values from -0.0625 to 0.0625
- labels: int32 [64], P('dp'), may hold values from 0 to 22527
Outputs:
- logits: float32 [64, 22528], P('dp')
- label_logit: float32 [64], P('dp')
The draws below stay inside these ranges and needn't reach their ends.
Inputs may be any that keep to these rules, and one draw needn't show every extreme that they name: `soup_mask`: every entry is 0 or 1, and at least one checkpoint is in the soup.
All inputs are finite; a program needn't handle non-finite values.
Results may differ from the reference program's by a relative error of at most 0.025.
Values may be sent and summed in bfloat16 or wider, within the bound.
A program may use at most 128 MiB of HBM per device.

```python
import math
import jax
import jax.numpy as jnp
from jax import lax

D = 1664
FF = 8192
EMB = 1280
TOKS = 257
CKPT = 10
LAYERS = 2
CLASSES = 22528
IMAGES = 64
N_MP = 16


def draw_tokens(key, part):
    key = jax.random.fold_in(key, 5)
    first, second, third, fourth = jax.random.split(key, 4)
    image_part = jax.random.normal(first, (IMAGES, 1, D), jnp.float32)
    token_part = jax.random.normal(second, (IMAGES, TOKS, D), jnp.float32)
    column_scale = jnp.exp(jax.random.uniform(third, (1, 1, D), jnp.float32, math.log(0.5), math.log(2.0)))
    row_scale = jnp.exp(jax.random.uniform(fourth, (IMAGES, TOKS, 1), jnp.float32, math.log(0.5), math.log(2.0)))
    values = 0.7 * column_scale * row_scale * (image_part + token_part)
    return jnp.clip(values, -12.0, 12.0).astype(jnp.bfloat16)


def draw_soup_mask(key, part):
    key = jax.random.fold_in(key, 11)
    first, second = jax.random.split(key)
    picks = jax.random.randint(first, (CKPT,), 0, 2)
    chosen = jax.random.randint(second, (), 0, CKPT)
    forced = (jnp.arange(CKPT) == chosen).astype(jnp.int32)
    return jnp.maximum(picks, forced).astype(jnp.int32)


def plant(values, rng, least, top_value):
    longest = values.shape.index(max(values.shape))
    spots = []
    for shift in (0, 1):
        where = [jax.random.randint(jax.random.fold_in(rng, axis), (), 0, length) for axis, length in enumerate(values.shape)]
        where[longest] = (where[longest] + shift) % values.shape[longest]
        spots.append(tuple(where))
    return values.at[spots[0]].set(least).at[spots[1]].set(top_value)


def shard_levels(own_key, dims, shards, least, high):
    loudness, own = 1.0, jax.random.fold_in(own_key, 6)
    for axis_at, parts in shards:
        heights = jnp.exp(jax.random.uniform(jax.random.fold_in(own, axis_at), (parts,), jnp.float32, least / len(shards), high / len(shards)))
        loudness = loudness * jnp.repeat(heights, dims[axis_at] // parts).reshape([-1 if axis == axis_at else 1 for axis in range(len(dims))])
    return loudness


def centred(rng, dims, deviation, most, pieces=(), dtype=jnp.bfloat16):
    level = shard_levels(rng, dims, pieces, -0.22, 0.18) if pieces else 1.0
    drawn = jax.random.normal(rng, dims, jnp.float32) * deviation * level
    return jnp.minimum(jnp.maximum(drawn, -most), most).astype(dtype)


def setup_inputs(seed: int = 0) -> dict:
    keys = jax.random.split(jax.random.key(seed), 12)
    tokens = draw_tokens(jax.random.fold_in(keys[11], 71), 0)
    up_ckpts = centred(keys[1], (LAYERS, CKPT, D, FF), (D // 4) ** -0.5, 0.3125, ((2, 16), (3, 16)))
    up_bias_ckpts = centred(keys[2], (LAYERS, CKPT, FF), 0.5, 3.0, ((2, 16),), jnp.float32)
    down_ckpts = centred(keys[3], (LAYERS, CKPT, FF, D), (FF // 4) ** -0.5, 0.125, ((2, 16), (3, 16)))
    down_bias_ckpts = centred(keys[4], (LAYERS, CKPT, D), 0.3, 1.75, (), jnp.float32)
    norm_ckpts = jnp.clip(1.0 + 0.15 * jax.random.normal(keys[5], (LAYERS, CKPT, D), jnp.float32), 0.25, 1.75)
    soup_mask = draw_soup_mask(jax.random.fold_in(keys[11], 71), 0)
    final_gain = jnp.clip(1.0 + 0.15 * jax.random.normal(keys[7], (D,), jnp.float32), 0.25, 1.75)
    projection = centred(keys[8], (D, EMB), D ** -0.5, 0.15625)
    class_embed = centred(keys[9], (CLASSES, EMB), 0.01, 0.0625, ((0, 16), (1, 16)))
    labels = plant(jax.random.randint(keys[10], (IMAGES,), 0, CLASSES), jax.random.fold_in(keys[10], 1), 0, CLASSES - 1).astype(jnp.int32)
    return {"tokens": tokens, "up_ckpts": up_ckpts, "up_bias_ckpts": up_bias_ckpts, "down_ckpts": down_ckpts, "down_bias_ckpts": down_bias_ckpts, "norm_ckpts": norm_ckpts, "soup_mask": soup_mask, "final_gain": final_gain, "projection": projection, "class_embed": class_embed, "labels": labels}


def soup_average(ckpts, share):
    total = jnp.zeros(ckpts.shape[1:], jnp.float32)
    for which in range(ckpts.shape[0]):
        total = total + share[which] * ckpts[which].astype(jnp.float32)
    return total

def layer_norm(values, gain):
    center = values - lax.optimization_barrier(jnp.mean(values, axis=-1, keepdims=True))
    spread = lax.optimization_barrier(jnp.mean(center * center, axis=-1, keepdims=True))
    return center * lax.rsqrt(spread + 1e-05) * gain

def reference(tokens, up_ckpts, up_bias_ckpts, down_ckpts, down_bias_ckpts, norm_ckpts, soup_mask, final_gain, projection, class_embed, labels):
    mask_float = soup_mask.astype(jnp.float32)
    share = mask_float / jnp.sum(mask_float)
    state = tokens.reshape(IMAGES * TOKS, D)
    block_units = FF // N_MP
    final = None
    for layer_index in range(LAYERS):
        norm_gain = soup_average(norm_ckpts[layer_index], share)
        up_weight = soup_average(up_ckpts[layer_index], share).astype(jnp.bfloat16)
        up_bias = soup_average(up_bias_ckpts[layer_index], share)
        down_weight = soup_average(down_ckpts[layer_index], share).astype(jnp.bfloat16)
        down_bias = soup_average(down_bias_ckpts[layer_index], share)
        normed = layer_norm(state.astype(jnp.float32), norm_gain).astype(jnp.bfloat16)
        hidden = jax.nn.gelu(jnp.dot(normed, up_weight, preferred_element_type=jnp.float32) + up_bias, approximate=False).astype(jnp.bfloat16)
        summed = jnp.zeros((IMAGES * TOKS, D), jnp.float32)
        for block_index in range(N_MP):
            lower = block_index * block_units
            piece = jnp.dot(hidden[:, lower:lower + block_units], down_weight[lower:lower + block_units], preferred_element_type=jnp.float32)
            piece = lax.optimization_barrier(piece.astype(jnp.bfloat16))
            summed = summed + piece.astype(jnp.float32)
        result = state.astype(jnp.float32) + down_bias + summed
        if layer_index < LAYERS - 1:
            state = result.astype(jnp.bfloat16)
        else:
            final = result
    pooled = lax.optimization_barrier(jnp.mean(final.reshape(IMAGES, TOKS, D), axis=1)).astype(jnp.bfloat16)
    pooled_norm = layer_norm(pooled.astype(jnp.float32), final_gain).astype(jnp.bfloat16)
    embedding = jnp.dot(pooled_norm, projection, preferred_element_type=jnp.float32)
    unit = (embedding * lax.rsqrt(lax.optimization_barrier(jnp.sum(embedding * embedding, axis=1, keepdims=True)) + 1e-06)).astype(jnp.bfloat16)
    logits = jnp.dot(unit, class_embed.T, preferred_element_type=jnp.float32) * 100.0
    label_logit = jnp.take_along_axis(logits, labels[:, None].astype(jnp.int32), axis=1)[:, 0]
    return (logits, label_logit)
```

```python
import functools

import jax
import jax.numpy as jnp
from jax import lax
from jax.experimental import pallas as pl
from jax.experimental.pallas import tpu as pltpu
from jax.sharding import PartitionSpec as P

MESH = pl.DeviceIdType.MESH
F32 = jnp.float32
BF16 = jnp.bfloat16

CKPT = 10
D = 1664
DB = 104
FFB = 512
EMB = 1280
EMBB = 80
TOKS = 257
ROWS = 1040
OWN = 80
CHUNK = 208
HALF = 528
CLS_BLOCKS = 11
UP1, DOWN1, UP2, DOWN2 = 0, 1, 2, 3


def layer_norm(values, gain):
    center = values - jnp.mean(values, axis=-1, keepdims=True)
    spread = jnp.mean(center * center, axis=-1, keepdims=True)
    return center * lax.rsqrt(spread + 1e-05) * gain


def gelu(values):
    return 0.5 * values * (1.0 + lax.erf(values * 0.7071067811865476))


def kernel(
    mask, tok, up_ck, down_ck, up_b, down_b, norm_g, final_gain, proj_hbm, cet, labels,
    out, lab_out,
    a2a, state, x1, x2, gath, w_up1, w_dn1, w_up2, w_dn2, hid, p_sib, s_sib, t_own, red,
    tsp, part, part_r, pooled_all, bias2, proj, unit_b, unit_g, unit_f, cls, lg, lgf, lr, ob,
    s_a2a, r_a2a, s_ag, r_ag, s_sb, r_sb, s_ring, r_ring, s_rs, r_rs, s_half, r_half,
    s_pr, r_pr, s_pf, r_pf, s_cl, r_cl, s_un, r_un, s_lg, r_lg, s_ob, r_ob, s_ob2, r_ob2, proj_sem,
):
    dp = lax.axis_index("dp")
    mp = lax.axis_index("mp")
    yh, z = lax.div(dp, 8), lax.rem(dp, 8)
    core = lax.rem(mp, 2)
    chip = lax.div(mp, 2)
    other_yh = 1 - yh
    block = core * 8 + chip
    last = block == 15
    sibling = chip * 2 + (1 - core)

    def copy(src, dst, ssem, rsem, to_dp, to_mp):
        return pltpu.make_async_remote_copy(
            src_ref=src, dst_ref=dst, send_sem=ssem, recv_sem=rsem,
            device_id={"dp": to_dp, "mp": to_mp}, device_id_type=MESH,
        )

    def got(ref, rsem):
        copy(ref, ref, s_half.at[0], rsem, dp, sibling).wait_recv()

    def sent(ref, ssem):
        copy(ref, ref, ssem, r_half.at[0], dp, sibling).wait_send()

    def loop(lo, hi, body):
        def step(k, carry):
            body(k)
            return carry

        lax.fori_loop(lo, hi, step, 0)

    red[:, 64:80, :] = jnp.zeros((8, 16, D), BF16)
    barrier = pltpu.get_barrier_semaphore()

    def greet(k):
        pl.semaphore_signal(
            barrier, inc=1, device_id={"dp": dp, "mp": lax.rem(mp + k, 16)}, device_id_type=MESH
        )
        pl.semaphore_signal(
            barrier, inc=1, device_id={"dp": lax.rem(dp + k, 16), "mp": mp}, device_id_type=MESH
        )

    loop(1, 16, greet)

    proj_copy = pltpu.make_async_copy(proj_hbm, proj, proj_sem)
    proj_copy.start()

    mask_f = [mask[i].astype(F32) for i in range(CKPT)]
    total = mask_f[0]
    for i in range(1, CKPT):
        total = total + mask_f[i]
    total_v = jnp.full((1, 128), total, F32)
    share_v = [jnp.full((1, 128), v, F32) / total_v for v in mask_f]

    def soup_vec(ref, layer, width):
        acc = jnp.zeros((1, width), F32)
        for i in range(CKPT):
            acc = acc + jnp.tile(share_v[i], (1, width // 128)) * ref[layer, i : i + 1, :]
        return acc

    def soup_up(layer, cs):
        acc = jnp.zeros((DB, 128), F32)
        for i in range(CKPT):
            acc = acc + share_v[i] * up_ck[layer, i, :, 128 * cs : 128 * cs + 128].astype(F32)
        return acc

    def soup_down(layer, cs):
        acc = jnp.zeros((128, DB), F32)
        for i in range(CKPT):
            acc = acc + share_v[i][:, :DB] * down_ck[layer, i, 128 * cs : 128 * cs + 128, :].astype(F32)
        tsp[:, :DB] = acc
        return tsp[...].T[:DB]

    def own_shard(t, soup, layer):
        for h in range(2):
            both = jnp.concatenate([soup(layer, h), soup(layer, 2 + h)], axis=0)
            gath[t, dp, :, 128 * h : 128 * h + 128] = both.astype(BF16)

    z_next, z_prev = yh * 8 + lax.rem(z + 1, 8), yh * 8 + lax.rem(z + 7, 8)

    def slot(which_yh, shift):
        return which_yh * 8 + lax.rem(z + shift + 8, 8)

    def ring_push(t, s, n, to):
        copy(gath.at[t, s], gath.at[t, s], s_ring.at[t, n], r_ring.at[t, n], to, mp).start()

    def ring_got(t, s, n):
        got(gath.at[t, s], r_ring.at[t, n])

    def ring(t, step):
        if step == 0:
            ring_push(t, dp, 14, other_yh * 8 + z)
            ring_push(t, dp, 0, z_next)
            ring_push(t, dp, 7, z_prev)
        elif step == 1:
            s = slot(other_yh, 0)
            ring_got(t, s, 14)
            ring_push(t, s, 1, z_next)
            ring_push(t, s, 8, z_prev)
        elif step < 8:
            n = step - 2
            dist = n // 2 + 1
            which = yh if n % 2 == 0 else other_yh
            sl, sr = slot(which, -dist), slot(which, dist)
            ring_got(t, sl, n)
            if n < 5:
                ring_push(t, sl, n + 2, z_next)
            ring_got(t, sr, 7 + n)
            if n < 4:
                ring_push(t, sr, 7 + n + 2, z_prev)
            elif n == 5:
                ring_push(t, sr, 7 + 6, z_prev)
        else:
            ring_got(t, slot(yh, 4), 6)
            ring_got(t, slot(other_yh, 4), 13)

    def compact(t, dst):
        def pair(j):
            g0 = gath[t, 2 * j].astype(F32)
            g1 = gath[t, 2 * j + 1].astype(F32)
            rows = pl.ds(pl.multiple_of(208 * j, 16), 208)
            dst[rows, 0:256] = jnp.concatenate([g0[:DB], g1[:DB]], axis=0).astype(BF16)
            dst[rows, 256:512] = jnp.concatenate([g0[DB:], g1[DB:]], axis=0).astype(BF16)

        loop(0, 8, pair)

    def owner_rows(c, p):
        return pl.multiple_of(512 * c + 64 * p, 16)

    def to_chip(k):
        return lax.rem(chip + k, 8)

    def from_chip(k):
        return lax.rem(chip + 8 - k, 8)

    def ag_start(lay, x):
        mine = x.at[pl.ds(owner_rows(core, chip), 64)]

        def push(k):
            copy(mine, mine, s_ag.at[lay, k], r_ag.at[lay, k], dp, to_chip(k) * 2 + core).start()

        loop(1, 8, push)
        copy(mine, mine, s_sb.at[lay, 0], r_sb.at[lay, 0], dp, sibling).start()
        extra = x.at[pl.ds(1024, 16)]

        @pl.when(last)
        def _():
            def push_extra(k):
                copy(
                    extra, extra, s_ag.at[lay, 8 + k], r_ag.at[lay, 8], dp, to_chip(k) * 2 + core
                ).start()

            loop(1, 8, push_extra)
            copy(extra, extra, s_sb.at[lay, 8], r_sb.at[lay, 8], dp, sibling).start()

    def ag_step(lay, x, k):
        rows = x.at[pl.ds(owner_rows(core, from_chip(k)), 64)]
        got(rows, r_ag.at[lay, k])
        copy(rows, rows, s_sb.at[lay, k], r_sb.at[lay, k], dp, sibling).start()

    def ag_extra(lay, x):
        extra = x.at[pl.ds(1024, 16)]

        @pl.when(jnp.logical_and(core == 1, chip != 7))
        def _():
            got(extra, r_ag.at[lay, 8])
            copy(extra, extra, s_sb.at[lay, 8], r_sb.at[lay, 8], dp, sibling).start()

    def ag_finish(lay, x):
        def step(k):
            got(x.at[pl.ds(owner_rows(1 - core, from_chip(k)), 64)], r_sb.at[lay, k])

        loop(0, 8, step)

        @pl.when(core == 0)
        def _():
            got(x.at[pl.ds(1024, 16)], r_sb.at[lay, 8])

    def ag_sent(lay, x):
        rows = x.at[pl.ds(0, 64)]
        extra = x.at[pl.ds(1024, 16)]

        def step(k):
            sent(rows, s_ag.at[lay, k])

        loop(1, 8, step)

        def step_sb(k):
            sent(rows, s_sb.at[lay, k])

        loop(0, 8, step_sb)

        @pl.when(last)
        def _():
            def step_extra(k):
                sent(extra, s_ag.at[lay, 8 + k])

            loop(1, 8, step_extra)

        @pl.when(core == 1)
        def _():
            sent(extra, s_sb.at[lay, 8])

    def normed_rows(x, gain):
        rows = layer_norm(state[...], gain).astype(BF16)
        x[pl.ds(owner_rows(core, chip), 64), :] = rows[:64]

        @pl.when(last)
        def _():
            x[1024:1040, :] = rows[64:]

    def up_chunk(x, w, bias, ch):
        rows = pl.ds(CHUNK * ch, CHUNK)
        return gelu(jnp.dot(x[rows, :], w[...], preferred_element_type=F32) + bias).astype(BF16)

    def down_chunk(first):
        return lax.dot_general(
            hid[pl.ds(pl.multiple_of(first, 16), 176), :], w_dn1[...],
            (((1,), (1,)), ((), ())), preferred_element_type=F32,
        )

    own_shard(UP1, soup_up, 0)
    pl.semaphore_wait(barrier, 30)

    def send_tokens(k):
        m2 = lax.rem(mp + k, 16)
        src = tok.at[pl.ds(owner_rows(lax.rem(m2, 2), lax.div(m2, 2)), OWN)]
        copy(src, a2a.at[mp], s_a2a.at[k], r_a2a.at[k], dp, m2).start()

    loop(1, 16, send_tokens)
    ring(UP1, 0)
    a2a[mp] = tok[pl.ds(owner_rows(core, chip), OWN), :]
    own_shard(DOWN1, soup_down, 0)
    ring(UP1, 1)
    ring(DOWN1, 0)
    gain1 = soup_vec(norm_g, 0, D)
    ring(UP1, 2)

    def wait_tokens(k):
        got(a2a.at[lax.rem(mp + 16 - k, 16)], r_a2a.at[k])

    loop(1, 16, wait_tokens)
    for j in range(16):
        state[:, DB * j : DB * j + DB] = a2a[j, :, :DB].astype(F32)
    normed_rows(x1, gain1)
    ag_start(0, x1)
    ring(UP1, 3)
    own_shard(UP2, soup_up, 1)
    ring(UP1, 4)
    own_shard(DOWN2, soup_down, 1)
    ring(UP1, 5)
    ring(DOWN1, 1)
    ring(UP1, 6)
    def send_cls(k):
        @pl.when(k != mp)
        def _():
            src = cet.at[:, pl.ds(pl.multiple_of(128 * k, 128), 128)]
            copy(src, cls.at[mp], s_cl.at[k], r_cl.at[mp], dp, k).start()

        @pl.when(k == mp)
        def _():
            cls[mp] = cet[:, pl.ds(pl.multiple_of(128 * k, 128), 128)]

    ag_step(0, x1, 1)
    ag_step(0, x1, 7)
    ring(UP1, 7)
    ring(DOWN1, 2)
    ag_step(0, x1, 2)
    ag_step(0, x1, 6)
    ring(UP1, 8)
    compact(UP1, w_up1)
    ring(DOWN1, 3)
    ag_step(0, x1, 3)
    ag_step(0, x1, 5)
    ring(DOWN1, 4)
    ag_step(0, x1, 4)
    ag_extra(0, x1)
    ring(DOWN1, 5)
    bias_up1 = soup_vec(up_b, 0, FFB)
    ag_finish(0, x1)
    for ch in range(5):
        hid[CHUNK * ch : CHUNK * ch + CHUNK, :] = up_chunk(x1, w_up1, bias_up1, ch)
        if ch == 1:
            ring(DOWN1, 6)
        if ch == 3:
            ring(DOWN1, 7)
    ring(UP2, 0)
    ring(DOWN1, 8)
    compact(DOWN1, w_dn1)
    ring(UP2, 1)

    for i in range(3):
        rows = pl.ds(176 * i, 176)
        p_sib[rows, :] = down_chunk(512 * (1 - core) + 176 * i).astype(BF16)
        copy(
            p_sib.at[rows], s_sib.at[rows], s_half.at[i], r_half.at[i], dp, sibling
        ).start()
    ring(UP2, 2)
    done = 0
    for i in range(3):
        rows = pl.ds(176 * i, 176)
        term = down_chunk(512 * core + 176 * i)
        got(s_sib.at[rows], r_half.at[i])
        t_own[rows, :] = (term + s_sib[rows, :].astype(F32)).astype(BF16)
        upto = min((176 * (i + 1)) // 64, 8)
        for q in range(done, upto):
            @pl.when(chip != q)
            def _(q=q):
                copy(
                    t_own.at[pl.ds(64 * q, 64)], red.at[chip, pl.ds(0, 64)],
                    s_rs.at[q], r_rs.at[chip], dp, q * 2 + core,
                ).start()
        done = upto

    @pl.when(jnp.logical_and(core == 1, chip != 7))
    def _():
        copy(
            t_own.at[pl.ds(512, 16)], red.at[chip, pl.ds(64, 16)],
            s_rs.at[8], r_rs.at[8 + chip], dp, 15,
        ).start()

    red[chip] = t_own[pl.ds(pl.multiple_of(64 * chip, 16), OWN), :]
    ring(UP2, 3)
    loop(0, CLS_BLOCKS, send_cls)
    gain2 = soup_vec(norm_g, 1, D)
    bias_down1 = soup_vec(down_b, 0, D)
    bias_up2 = soup_vec(up_b, 1, FFB)
    bias_down2 = soup_vec(down_b, 1, D)
    for k in range(13):
        bias2[k] = jnp.broadcast_to(bias_down2[:, 128 * k : 128 * k + 128], (8, 128))
    ring(UP2, 4)
    ring(UP2, 5)
    ring(UP2, 6)
    for q in range(8):
        @pl.when(chip != q)
        def _(q=q):
            got(red.at[q, pl.ds(0, 64)], r_rs.at[q])

        if q < 7:
            @pl.when(last)
            def _(q=q):
                got(red.at[q, pl.ds(64, 16)], r_rs.at[8 + q])

    summed = red[0].astype(F32)
    for q in range(1, 8):
        summed = summed + red[q].astype(F32)
    state[...] = (state[...] + bias_down1 + summed).astype(BF16).astype(F32)
    normed_rows(x2, gain2)
    ag_start(1, x2)
    ring(UP2, 7)

    row = lax.broadcasted_iota(jnp.int32, (16, OWN), 1)
    img = lax.broadcasted_iota(jnp.int32, (16, OWN), 0)
    real = owner_rows(core, chip) + row
    inside = (real >= TOKS * img) & (real < TOKS * (img + 1)) & (img < 4)
    inside = inside & ((row < 64) | jnp.broadcast_to(last, (16, OWN)))
    state_sum = jnp.dot(
        jnp.where(inside, 1.0, 0.0).astype(BF16), state[...].astype(BF16), preferred_element_type=F32
    )[:8]
    ring(UP2, 8)
    ring(DOWN2, 0)
    compact(UP2, w_up2)
    ring(DOWN2, 1)
    ring(DOWN2, 2)
    ag_step(1, x2, 1)
    ag_step(1, x2, 7)
    ring(DOWN2, 3)
    ag_step(1, x2, 2)
    ag_step(1, x2, 6)
    ring(DOWN2, 4)
    ag_step(1, x2, 3)
    ag_step(1, x2, 5)
    ring(DOWN2, 5)
    ag_step(1, x2, 4)
    ag_extra(1, x2)
    ring(DOWN2, 6)
    ag_finish(1, x2)
    hsum = jnp.zeros((16, FFB), F32)
    for ch in range(5):
        h = up_chunk(x2, w_up2, bias_up2, ch)
        row = lax.broadcasted_iota(jnp.int32, (16, CHUNK), 1) + CHUNK * ch
        img = lax.broadcasted_iota(jnp.int32, (16, CHUNK), 0)
        inside = (row >= TOKS * img) & (row < TOKS * (img + 1)) & (img < 4)
        hsum = hsum + jnp.dot(
            jnp.where(inside, 1.0, 0.0).astype(BF16), h, preferred_element_type=F32
        )
        if ch == 1:
            ring(DOWN2, 7)
    ring(DOWN2, 8)
    compact(DOWN2, w_dn2)

    hmean = hsum[:8] * (1.0 / TOKS)
    high = hmean.astype(BF16)
    low = (hmean - high.astype(F32)).astype(BF16)
    both = lax.dot_general(
        jnp.concatenate([high.astype(F32), low.astype(F32)], axis=0).astype(BF16), w_dn2[...],
        (((1,), (1,)), ((), ())), preferred_element_type=F32,
    )
    partial = both[:8] + both[8:] + state_sum * (1.0 / TOKS)
    for k in range(13):
        part[k] = partial[:, 128 * k : 128 * k + 128]

    def send_part(k):
        @pl.when(k != mp)
        def _():
            copy(part.at[k], part_r.at[mp], s_pr.at[k], r_pr.at[mp], dp, k).start()

        @pl.when(k == mp)
        def _():
            part_r[mp] = part[k]

    loop(0, 13, send_part)

    @pl.when(mp < 13)
    def _():
        def wait_part(k):
            @pl.when(k != mp)
            def _():
                got(part_r.at[k], r_pr.at[k])

        loop(0, 16, wait_part)
        pooled = part_r[0]
        for k in range(1, 16):
            pooled = pooled + part_r[k]
        pooled_all[mp] = (pooled + bias2[mp]).astype(BF16).astype(F32)

        def send_pooled(k):
            copy(
                pooled_all.at[mp], pooled_all.at[mp], s_pf.at[k], r_pf.at[mp], dp,
                lax.rem(mp + k, 16),
            ).start()

        loop(1, 16, send_pooled)

    def wait_pooled(k):
        @pl.when(k != mp)
        def _():
            got(pooled_all.at[k], r_pf.at[k])

    proj_copy.wait()
    loop(0, 13, wait_pooled)
    pooled = jnp.concatenate([pooled_all[k] for k in range(13)], axis=1)
    pooled_norm = layer_norm(pooled, final_gain[...])
    pooled_norm = jnp.concatenate([pooled_norm, jnp.zeros_like(pooled_norm)], axis=0).astype(BF16)
    embedding = jnp.dot(pooled_norm, proj[...], preferred_element_type=F32)[:8]
    unit = embedding * lax.rsqrt(jnp.sum(embedding * embedding, axis=1, keepdims=True) + 1e-06)
    unit_b[40:48, :] = jnp.zeros((8, 128), F32)
    for j in range(10):
        unit_b[4 * j : 4 * j + 4, :] = unit[:4, 128 * j : 128 * j + 128]
    unit_g[dp] = unit_b[...].astype(BF16)

    def send_unit(k):
        copy(
            unit_g.at[dp], unit_g.at[dp], s_un.at[k], r_un.at[k], lax.rem(dp + k, 16), mp
        ).start()

    loop(1, 16, send_unit)

    def wait_cls(k):
        @pl.when(k != mp)
        def _():
            got(cls.at[k], r_cl.at[k])

    @pl.when(mp < CLS_BLOCKS)
    def _():
        loop(0, 16, wait_cls)

    def wait_unit(k):
        got(unit_g.at[lax.rem(dp + 16 - k, 16)], r_un.at[k])

    loop(1, 16, wait_unit)

    @pl.when(mp < CLS_BLOCKS)
    def _():
        for k in range(16):
            unit_f[48 * k : 48 * k + 48, :] = unit_g[k].astype(F32)
        columns = []
        for j in range(10):
            columns.append(
                jnp.concatenate(
                    [unit_f[pl.ds(4 * j + i, 16, stride=48), :] for i in range(4)], axis=0
                )
            )
        lhs = jnp.concatenate(columns, axis=1).astype(BF16)
        rhs = jnp.concatenate([cls[k] for k in range(16)], axis=0)
        lgf[...] = jnp.dot(lhs, rhs, preferred_element_type=F32) * 100.0
        for k in range(16):
            lg[k] = lgf[pl.ds(k, 4, stride=16), :]
        lr[dp] = lg[dp]

        def send_logits(k):
            to = lax.rem(dp + k, 16)
            copy(lg.at[to], lr.at[dp], s_lg.at[k], r_lg.at[k], to, mp).start()

        loop(1, 16, send_logits)

        def wait_logits(k):
            got(lr.at[lax.rem(dp + 16 - k, 16)], r_lg.at[k])

        loop(1, 16, wait_logits)
        for k in range(16):
            lgf[4 * k : 4 * k + 4, :] = lr[k]
        ob[mp] = lgf[...].astype(BF16)

        def send_ob(k):
            copy(
                ob.at[mp], ob.at[mp], s_ob.at[k], r_ob.at[mp], dp, to_chip(k) * 2 + core
            ).start()

        loop(1, 8, send_ob)
        copy(ob.at[mp], ob.at[mp], s_ob2.at[mp], r_ob2.at[mp], dp, sibling).start()

    for k in range(CLS_BLOCKS):
        @pl.when(jnp.logical_and(core == k % 2, mp != k))
        def _(k=k):
            got(ob.at[k], r_ob.at[k])
            copy(ob.at[k], ob.at[k], s_ob2.at[k], r_ob2.at[k], dp, sibling).start()

    for k in range(CLS_BLOCKS):
        @pl.when(core != k % 2)
        def _(k=k):
            got(ob.at[k], r_ob2.at[k])

    found = jnp.zeros((4, 128), F32)
    lane = lax.broadcasted_iota(jnp.int32, (4, 128), 1)
    label = labels[...]
    for k in range(CLS_BLOCKS):
        vals = ob[k].astype(F32)
        for g in range(16):
            first = (g * CLS_BLOCKS + k) * 128
            piece = vals[4 * g : 4 * g + 4]
            out[:, first : first + 128] = piece
            found = found + jnp.where(lane + first == label, piece, 0.0)
    lab_out[...] = jnp.broadcast_to(jnp.sum(found, axis=1, keepdims=True), (4, 128))

    def sent_a2a(k):
        sent(tok.at[pl.ds(0, OWN)], s_a2a.at[k])
        sent(unit_g.at[0], s_un.at[k])

    loop(1, 16, sent_a2a)

    def sent_ring(t):
        def step(n):
            sent(gath.at[t, 0], s_ring.at[t, n])

        loop(0, 15, step)

    loop(0, 4, sent_ring)
    ag_sent(0, x1)
    ag_sent(1, x2)
    for i in range(3):
        sent(p_sib.at[pl.ds(0, 176)], s_half.at[i])

    for q in range(8):
        @pl.when(chip != q)
        def _(q=q):
            sent(t_own.at[pl.ds(0, 64)], s_rs.at[q])

    @pl.when(jnp.logical_and(core == 1, chip != 7))
    def _():
        sent(t_own.at[pl.ds(0, 16)], s_rs.at[8])

    def sent_cls(k):
        @pl.when(k != mp)
        def _():
            sent(cls.at[0], s_cl.at[k])

    loop(0, CLS_BLOCKS, sent_cls)

    def sent_part(k):
        @pl.when(k != mp)
        def _():
            sent(part.at[0], s_pr.at[k])

    loop(0, 13, sent_part)

    @pl.when(mp < 13)
    def _():
        loop(1, 16, lambda k: sent(part.at[0], s_pf.at[k]))

    @pl.when(mp < CLS_BLOCKS)
    def _():
        loop(1, 16, lambda k: sent(lg.at[0], s_lg.at[k]))
        loop(1, 8, lambda k: sent(ob.at[0], s_ob.at[k]))

    for k in range(CLS_BLOCKS):
        @pl.when(core == k % 2)
        def _(k=k):
            sent(ob.at[0], s_ob2.at[k])


def per_device(
    tokens, up_ckpts, up_bias_ckpts, down_ckpts, down_bias_ckpts, norm_ckpts, soup_mask,
    final_gain, projection, class_embed, labels,
):
    images, token_count, feature_cols = tokens.shape
    rows = images * token_count
    tok = jnp.pad(tokens.reshape(rows, feature_cols), ((0, ROWS - rows), (0, 128 - feature_cols)))
    vm = pl.BlockSpec(memory_space=pltpu.VMEM)
    dma = pltpu.SemaphoreType.DMA
    logits, label_logit = pl.pallas_call(
        kernel,
        out_shape=(
            jax.ShapeDtypeStruct((4, 16 * CLS_BLOCKS * 128), F32),
            jax.ShapeDtypeStruct((4, 128), F32),
        ),
        in_specs=[pl.BlockSpec(memory_space=pltpu.SMEM)]
        + [vm] * 7
        + [pl.BlockSpec(memory_space=pl.ANY)]
        + [vm] * 2,
        out_specs=(vm, vm),
        scratch_shapes=[
            pltpu.VMEM((16, OWN, 128), BF16),
            pltpu.VMEM((OWN, D), F32),
            pltpu.VMEM((ROWS, D), BF16),
            pltpu.VMEM((ROWS, D), BF16),
            pltpu.VMEM((4, 16, 2 * DB, 256), BF16),
            pltpu.VMEM((D, FFB), BF16),
            pltpu.VMEM((D, FFB), BF16),
            pltpu.VMEM((D, FFB), BF16),
            pltpu.VMEM((D, FFB), BF16),
            pltpu.VMEM((ROWS, FFB), BF16),
            pltpu.VMEM((HALF, D), BF16),
            pltpu.VMEM((HALF, D), BF16),
            pltpu.VMEM((HALF, D), BF16),
            pltpu.VMEM((8, OWN, D), BF16),
            pltpu.VMEM((128, 128), F32),
            pltpu.VMEM((13, 8, 128), F32),
            pltpu.VMEM((16, 8, 128), F32),
            pltpu.VMEM((13, 8, 128), F32),
            pltpu.VMEM((13, 8, 128), F32),
            pltpu.VMEM((D, EMB), BF16),
            pltpu.VMEM((48, 128), F32),
            pltpu.VMEM((16, 48, 128), BF16),
            pltpu.VMEM((768, 128), F32),
            pltpu.VMEM((16, EMBB, 128), BF16),
            pltpu.VMEM((16, 4, 128), F32),
            pltpu.VMEM((64, 128), F32),
            pltpu.VMEM((16, 4, 128), F32),
            pltpu.VMEM((CLS_BLOCKS, 64, 128), BF16),
            dma((16,)), dma((16,)),
            dma((2, 16)), dma((2, 16)),
            dma((2, 9)), dma((2, 9)),
            dma((4, 15)), dma((4, 15)),
            dma((9,)), dma((16,)),
            dma((3,)), dma((3,)),
            dma((16,)), dma((16,)),
            dma((16,)), dma((16,)),
            dma((16,)), dma((16,)),
            dma((16,)), dma((16,)),
            dma((16,)), dma((16,)),
            dma((8,)), dma((16,)),
            dma((16,)), dma((16,)),
            dma(()),
        ],
        compiler_params=pltpu.CompilerParams(
            collective_id=0, has_side_effects=True, vmem_limit_bytes=60 * 2**20
        ),
    )(
        soup_mask, tok, up_ckpts, down_ckpts, up_bias_ckpts, down_bias_ckpts, norm_ckpts,
        final_gain[None, :], projection, class_embed.T, labels[:, None],
    )
    return (logits, label_logit[:, 0])


def solution(mesh):
    placed = (
        P("dp", None, "mp"),
        P(None, None, "dp", "mp"),
        P(None, None, "mp"),
        P(None, None, "mp", "dp"),
        P(),
        P(),
        P(),
        P(),
        P(),
        P("dp", "mp"),
        P("dp"),
    )
    return jax.shard_map(
        per_device, mesh=mesh, in_specs=placed, out_specs=(P("dp", None), P("dp")), check_vma=False
    )
```

```python
import functools

import jax
import jax.numpy as jnp
from jax import lax
from jax.experimental import pallas as pl
from jax.experimental.pallas import tpu as pltpu
from jax.sharding import PartitionSpec as P

MESH = pl.DeviceIdType.MESH
F32 = jnp.float32
BF16 = jnp.bfloat16

CKPT = 10
D = 1664
DB = 104
FFB = 512
EMB = 1280
EMBB = 80
TOKS = 257
ROWS = 1040
OWN = 80
CHUNK = 208
CLS_BLOCKS = 11
UP1, DOWN1, UP2, DOWN2 = 0, 1, 2, 3
PLACES = ((-1, 0), (1, 0), (0, 1), (-1, 1), (1, 1), (2, 0), (2, 1), (0, 0))
STEPS = (2, -1, 1, 0)


def layer_norm(values, gain):
    center = values - jnp.mean(values, axis=-1, keepdims=True)
    spread = jnp.mean(center * center, axis=-1, keepdims=True)
    return center * lax.rsqrt(spread + 1e-05) * gain


def gelu(values):
    return 0.5 * values * (1.0 + lax.erf(values * 0.7071067811865476))


def kernel(
    mask, tok, up_hbm, down_hbm, up_b, down_b, norm_g, final_gain, proj_hbm, cet,
    ob_out,
    up_ck, down_ck, a2a, state, x1, x2, gath, w_up1, w_dn1, w_up2, w_dn2, hid, p_sib, s_sib, t_own,
    red, extra_s, extra_r, part, part_r, pooled_all, bias2, proj, unit_g, cls, lg, lr, ob,
    s_a2a, r_a2a, s_ag, r_ag, s_sb, r_sb, s_ring, r_ring, s_rs, r_rs, s_half, r_half, s_ex, r_ex,
    s_pr, r_pr, s_pf, r_pf, s_cl, r_cl, s_un, r_un, s_us, r_us, s_lg, r_lg, s_ob, r_ob, s_ob2, r_ob2,
    proj_sem, ck_sem,
):
    dp = lax.axis_index("dp")
    mp = lax.axis_index("mp")
    yh, z = lax.div(dp, 8), lax.rem(dp, 8)
    core = lax.rem(mp, 2)
    chip = lax.div(mp, 2)
    yl, xc = lax.div(mp, 8), lax.rem(chip, 4)
    other_yh = 1 - yh
    block = core * 8 + xc * 2 + yl
    last = block == 15
    extra_src = jnp.logical_and(core == 1, block != 15)
    sibling = chip * 2 + (1 - core)

    def device(y, dx):
        return y * 8 + lax.rem(xc + dx + 4, 4) * 2 + core

    right, left, across = device(yl, 1), device(yl, -1), device(1 - yl, 0)

    def copy(src, dst, ssem, rsem, to_dp, to_mp):
        return pltpu.make_async_remote_copy(
            src_ref=src, dst_ref=dst, send_sem=ssem, recv_sem=rsem,
            device_id={"dp": to_dp, "mp": to_mp}, device_id_type=MESH,
        )

    def got(ref, rsem):
        copy(ref, ref, s_half.at[0], rsem, dp, sibling).wait_recv()

    def sent(ref, ssem):
        copy(ref, ref, ssem, r_half.at[0], dp, sibling).wait_send()

    def loop(lo, hi, body):
        def step(k, carry):
            body(k)
            return carry

        lax.fori_loop(lo, hi, step, 0)

    loads = [
        pltpu.make_async_copy(src.at[layer], dst.at[layer], ck_sem.at[n])
        for n, (src, dst, layer) in enumerate(
            ((up_hbm, up_ck, 0), (down_hbm, down_ck, 0), (up_hbm, up_ck, 1), (down_hbm, down_ck, 1))
        )
    ]
    for load in loads:
        load.start()
    proj_copy = pltpu.make_async_copy(proj_hbm, proj, proj_sem)
    proj_copy.start()

    state[64:80, :] = jnp.zeros((16, D), F32)
    extra_r[...] = jnp.zeros((8, 16, D), BF16)
    barrier = pltpu.get_barrier_semaphore()

    def greet(k):
        pl.semaphore_signal(
            barrier, inc=1, device_id={"dp": dp, "mp": lax.rem(mp + k, 16)}, device_id_type=MESH
        )
        pl.semaphore_signal(
            barrier, inc=1, device_id={"dp": lax.rem(dp + k, 16), "mp": mp}, device_id_type=MESH
        )

    loop(1, 16, greet)

    mask_f = [mask[i].astype(F32) for i in range(CKPT)]
    total = mask_f[0]
    for i in range(1, CKPT):
        total = total + mask_f[i]
    total_v = jnp.full((1, 128), total, F32)
    share_v = [jnp.full((1, 128), v, F32) / total_v for v in mask_f]

    def soup_vec(ref, layer, width):
        acc = jnp.zeros((1, width), F32)
        for i in range(CKPT):
            acc = acc + jnp.tile(share_v[i], (1, width // 128)) * ref[i, layer : layer + 1, :]
        return acc

    def soup(ref, layer, cs):
        acc = jnp.zeros((DB, 128), F32)
        for i in range(CKPT):
            acc = acc + share_v[i] * ref[layer, i, :, 128 * cs : 128 * cs + 128].astype(F32)
        return acc

    def own_shard(t, ref, layer):
        loads[t].wait()
        for h in range(2):
            both = jnp.concatenate([soup(ref, layer, h), soup(ref, layer, 2 + h)], axis=0)
            gath[t, dp, :, 128 * h : 128 * h + 128] = both.astype(BF16)

    z_next, z_prev = yh * 8 + lax.rem(z + 1, 8), yh * 8 + lax.rem(z + 7, 8)

    def slot(which_yh, shift):
        return which_yh * 8 + lax.rem(z + shift + 8, 8)

    def ring_push(t, s, n, to):
        copy(gath.at[t, s], gath.at[t, s], s_ring.at[t, n], r_ring.at[t, n], to, mp).start()

    def ring_got(t, s, n):
        got(gath.at[t, s], r_ring.at[t, n])

    def ring(t, step):
        if step == 0:
            ring_push(t, dp, 14, other_yh * 8 + z)
            ring_push(t, dp, 0, z_next)
            ring_push(t, dp, 7, z_prev)
        elif step == 1:
            s = slot(other_yh, 0)
            ring_got(t, s, 14)
            ring_push(t, s, 1, z_next)
            ring_push(t, s, 8, z_prev)
        elif step < 8:
            n = step - 2
            dist = n // 2 + 1
            which = yh if n % 2 == 0 else other_yh
            sl, sr = slot(which, -dist), slot(which, dist)
            ring_got(t, sl, n)
            if n < 5:
                ring_push(t, sl, n + 2, z_next)
            ring_got(t, sr, 7 + n)
            if n < 4:
                ring_push(t, sr, 7 + n + 2, z_prev)
            elif n == 5:
                ring_push(t, sr, 7 + 6, z_prev)
        else:
            ring_got(t, slot(yh, 4), 6)
            ring_got(t, slot(other_yh, 4), 13)

    def compact(t, dst):
        def pair(j):
            g0 = gath[t, 2 * j].astype(F32)
            g1 = gath[t, 2 * j + 1].astype(F32)
            rows = pl.ds(pl.multiple_of(208 * j, 16), 208)
            dst[rows, 0:256] = jnp.concatenate([g0[:DB], g1[:DB]], axis=0).astype(BF16)
            dst[rows, 256:512] = jnp.concatenate([g0[DB:], g1[DB:]], axis=0).astype(BF16)

        loop(0, 8, pair)

    def block_rows(c, dx, y):
        return pl.multiple_of(512 * c + 128 * lax.rem(xc + dx + 4, 4) + 64 * y, 16)

    def half_rows(x, c, idx, h):
        dx, other = PLACES[idx]
        y = 1 - yl if other else yl
        return x.at[pl.ds(block_rows(c, dx, y) + 32 * h, 32)]

    def ag_push(lay, x, idx_here, idx, h, to):
        rows = half_rows(x, core, idx_here, h)
        n = 2 * idx + h
        copy(rows, rows, s_ag.at[lay, n], r_ag.at[lay, n], dp, to).start()

    def ag_sib(lay, x, idx, h):
        rows = half_rows(x, core, idx, h)
        n = 2 * idx + h
        copy(rows, rows, s_sb.at[lay, n], r_sb.at[lay, n], dp, sibling).start()

    def ag_start(lay, x):
        for h in range(2):
            ag_push(lay, x, 7, 0, h, right)
            ag_push(lay, x, 7, 1, h, left)
            ag_push(lay, x, 7, 2, h, across)
        for h in range(2):
            ag_sib(lay, x, 7, h)
        extra = x.at[pl.ds(1024, 16)]

        @pl.when(last)
        def _():
            def push_extra(k):
                copy(
                    extra, extra, s_ex.at[lay, k], r_ex.at[lay], dp, lax.rem(chip + k, 8) * 2 + core
                ).start()

            loop(1, 8, push_extra)
            copy(extra, extra, s_sb.at[lay, 16], r_sb.at[lay, 16], dp, sibling).start()

    def ag_recv(lay, x, idx, h):
        got(half_rows(x, core, idx, h), r_ag.at[lay, 2 * idx + h])
        if idx == 0:
            ag_push(lay, x, 0, 5, h, right)
            if h == 1:
                ag_push(lay, x, 0, 3, h, across)
        elif idx == 1 and h == 1:
            ag_push(lay, x, 1, 4, h, across)
        elif idx == 2 and h == 0:
            ag_push(lay, x, 2, 3, h, right)
            ag_push(lay, x, 2, 4, h, left)
        elif idx == 4:
            ag_push(lay, x, 4, 6, h, left)
        ag_sib(lay, x, idx, h)

    def ag_extra(lay, x):
        extra = x.at[pl.ds(1024, 16)]

        @pl.when(extra_src)
        def _():
            got(extra, r_ex.at[lay])
            copy(extra, extra, s_sb.at[lay, 16], r_sb.at[lay, 16], dp, sibling).start()

    def ag_finish(lay, x):
        for idx in range(8):
            for h in range(2):
                got(half_rows(x, 1 - core, idx, h), r_sb.at[lay, 2 * idx + h])

        @pl.when(core == 0)
        def _():
            got(x.at[pl.ds(1024, 16)], r_sb.at[lay, 16])

    def ag_sent(lay, x):
        rows = x.at[pl.ds(0, 32)]
        extra = x.at[pl.ds(1024, 16)]
        loop(0, 14, lambda n: sent(rows, s_ag.at[lay, n]))
        loop(0, 16, lambda n: sent(rows, s_sb.at[lay, n]))

        @pl.when(last)
        def _():
            loop(1, 8, lambda k: sent(extra, s_ex.at[lay, k]))

        @pl.when(core == 1)
        def _():
            sent(extra, s_sb.at[lay, 16])

    def normed_rows(x, gain):
        rows = layer_norm(state[...], gain).astype(BF16)
        x[pl.ds(block_rows(core, 0, yl), 64), :] = rows[:64]

        @pl.when(last)
        def _():
            x[1024:1040, :] = rows[64:]

    def up_chunk(x, w, bias, ch):
        rows = pl.ds(CHUNK * ch, CHUNK)
        return gelu(jnp.dot(x[rows, :], w[...], preferred_element_type=F32) + bias).astype(BF16)

    def down_product(rows):
        return lax.dot_general(
            rows, w_dn1[...], (((1,), (1,)), ((), ())), preferred_element_type=F32
        )

    def rs_rows(o, y, h):
        return t_own.at[o, pl.ds(pl.multiple_of(64 * y + 32 * h, 16), 32)]

    def rs_push(o, y, kind, h, to):
        n = 2 * kind + h
        copy(rs_rows(o, y, h), red.at[kind, h], s_rs.at[n], r_rs.at[n], dp, to).start()

    def rs_add(o, y, h, *kinds):
        rows = rs_rows(o, y, h)
        acc = rows[...].astype(F32)
        for kind in kinds:
            got(red.at[kind, h], r_rs.at[2 * kind + h])
            acc = acc + red[kind, h].astype(F32)
        rows[...] = acc.astype(BF16)

    own_shard(UP1, up_ck, 0)
    pl.semaphore_wait(barrier, 30)

    def send_tokens(k):
        m2 = lax.rem(mp + k, 16)
        b2 = lax.rem(m2, 2) * 8 + lax.rem(lax.div(m2, 2), 4) * 2 + lax.div(m2, 8)
        src = tok.at[pl.ds(16 * b2, 17)]
        copy(src, a2a.at[mp], s_a2a.at[k], r_a2a.at[k], dp, m2).start()

    loop(1, 16, send_tokens)
    ring(UP1, 0)
    a2a[mp] = tok[pl.ds(16 * block, 17)]
    own_shard(DOWN1, down_ck, 0)
    ring(DOWN1, 0)
    gain1 = soup_vec(norm_g, 0, D)
    ring(UP1, 1)

    def wait_tokens(k):
        got(a2a.at[lax.rem(mp + 16 - k, 16)], r_a2a.at[k])

    loop(1, 16, wait_tokens)
    for j in range(16):
        state[:68, DB * j : DB * j + DB] = a2a[j].astype(F32).reshape(68, DB)
    normed_rows(x1, gain1)
    ag_start(0, x1)
    ring(UP1, 2)
    own_shard(UP2, up_ck, 1)
    ring(UP1, 3)
    for idx in range(3):
        ag_recv(0, x1, idx, 0)
    ring(UP1, 4)
    for idx in range(3):
        ag_recv(0, x1, idx, 1)
    ring(UP1, 5)
    ag_recv(0, x1, 3, 0)
    ag_recv(0, x1, 4, 0)
    ring(UP1, 6)
    ring(DOWN1, 1)
    ag_recv(0, x1, 3, 1)
    ag_recv(0, x1, 4, 1)
    ag_recv(0, x1, 5, 0)
    ring(UP1, 7)
    ring(DOWN1, 2)
    ag_recv(0, x1, 5, 1)
    ag_recv(0, x1, 6, 0)
    ag_recv(0, x1, 6, 1)
    ag_extra(0, x1)
    own_shard(DOWN2, down_ck, 1)
    ring(UP1, 8)
    ring(DOWN1, 3)
    compact(UP1, w_up1)
    bias_up1 = soup_vec(up_b, 0, FFB)
    ag_finish(0, x1)
    for ch in range(5):
        hid[CHUNK * ch : CHUNK * ch + CHUNK, :] = up_chunk(x1, w_up1, bias_up1, ch)
        if ch == 0:
            ring(DOWN1, 4)
        if ch == 2:
            ring(DOWN1, 5)
        if ch == 4:
            ring(DOWN1, 6)

    def send_cls(k):
        @pl.when(k != mp)
        def _():
            src = cet.at[:, pl.ds(pl.multiple_of(128 * k, 128), 128)]
            copy(src, cls.at[mp], s_cl.at[k], r_cl.at[mp], dp, k).start()

        @pl.when(k == mp)
        def _():
            cls[mp] = cet[:, pl.ds(pl.multiple_of(128 * k, 128), 128)]

    loop(0, CLS_BLOCKS, send_cls)
    gain2 = soup_vec(norm_g, 1, D)
    bias_down1 = soup_vec(down_b, 0, D)
    bias_up2 = soup_vec(up_b, 1, FFB)
    bias_down2 = soup_vec(down_b, 1, D)
    for k in range(13):
        bias2[k] = jnp.broadcast_to(bias_down2[:, 128 * k : 128 * k + 128], (8, 128))
    ring(DOWN1, 7)
    ring(UP2, 0)
    ring(UP2, 1)
    ring(DOWN1, 8)
    compact(DOWN1, w_dn1)

    def own_chunk(o):
        dx = STEPS[o]
        size = 144 if dx == 0 else 128
        rows = pl.ds(0, size)
        for c in (1 - core, core):
            lhs = hid[pl.ds(block_rows(c, dx, 0), 128), :]
            if dx == 0:
                lhs = jnp.concatenate([lhs, hid[1024:1040, :]], axis=0)
            term = down_product(lhs)
            if c is not core:
                p_sib[o, rows, :] = term.astype(BF16)
                copy(
                    p_sib.at[o, rows], s_sib.at[o, rows], s_half.at[o], r_half.at[o], dp, sibling
                ).start()
        got(s_sib.at[o, rows], r_half.at[o])
        t_own[o, rows, :] = (term + s_sib[o, rows, :].astype(F32)).astype(BF16)

    own_chunk(0)
    for h in range(2):
        rs_push(0, yl, 0, h, left)
        rs_push(0, 1 - yl, 1, h, right)
    own_chunk(1)
    for h in range(2):
        rs_push(1, 1 - yl, 2, h, left)
    own_chunk(2)
    for h in range(2):
        rs_add(2, 1 - yl, h, 1)
        rs_push(2, 1 - yl, 3, h, right)
        rs_add(1, yl, h, 0)
        rs_push(1, yl, 4, h, left)
    for h in range(2):
        rs_push(2, yl, 5, h, right)
    ring(UP2, 2)
    own_chunk(3)

    @pl.when(extra_src)
    def _():
        copy(
            t_own.at[3, pl.ds(128, 16)], extra_r.at[chip], s_ex.at[0, 0], r_ex.at[2 + chip], dp, 15
        ).start()

    ring(UP2, 3)
    ring(DOWN2, 0)
    for h in range(2):
        rs_add(3, 1 - yl, h, 3, 2)
        rs_push(3, 1 - yl, 6, h, across)
    ring(UP2, 4)
    ring(UP2, 5)
    ring(DOWN2, 1)
    for h in range(2):
        rs_add(3, yl, h, 4, 5, 6)

    @pl.when(last)
    def _():
        extra = t_own[3, 128:144, :].astype(F32)
        for q in range(7):
            got(extra_r.at[q], r_ex.at[2 + q])
            extra = extra + extra_r[q].astype(F32)
        extra_s[...] = extra

    @pl.when(jnp.logical_not(last))
    def _():
        extra_s[...] = jnp.zeros((16, D), F32)

    summed = jnp.concatenate(
        [t_own[3, pl.ds(pl.multiple_of(64 * yl, 16), 64), :].astype(F32), extra_s[...]], axis=0
    )
    state[...] = (state[...] + bias_down1 + summed).astype(BF16).astype(F32)
    normed_rows(x2, gain2)
    ag_start(1, x2)
    ring(UP2, 6)

    row = lax.broadcasted_iota(jnp.int32, (16, OWN), 1)
    img = lax.broadcasted_iota(jnp.int32, (16, OWN), 0)
    inside = ((row & 3) == img) & (row < jnp.where(last, 68, 64))
    state_sum = jnp.dot(
        jnp.where(inside, 1.0, 0.0).astype(BF16), state[...].astype(BF16), preferred_element_type=F32
    )[:8]
    ring(UP2, 7)
    ring(DOWN2, 2)
    for idx in range(3):
        ag_recv(1, x2, idx, 0)
    ring(UP2, 8)
    for idx in range(3):
        ag_recv(1, x2, idx, 1)
    ring(DOWN2, 3)
    ag_recv(1, x2, 3, 0)
    ag_recv(1, x2, 4, 0)
    ring(DOWN2, 4)
    compact(UP2, w_up2)
    ag_recv(1, x2, 3, 1)
    ag_recv(1, x2, 4, 1)
    ag_recv(1, x2, 5, 0)
    ring(DOWN2, 5)
    ag_recv(1, x2, 5, 1)
    ag_recv(1, x2, 6, 0)
    ag_recv(1, x2, 6, 1)
    ag_extra(1, x2)
    ring(DOWN2, 6)
    ag_finish(1, x2)
    hsum = jnp.zeros((16, FFB), F32)
    for ch in range(5):
        h = up_chunk(x2, w_up2, bias_up2, ch)
        row = lax.broadcasted_iota(jnp.int32, (16, CHUNK), 1) + CHUNK * ch
        img = lax.broadcasted_iota(jnp.int32, (16, CHUNK), 0)
        inside = ((row & 3) == img) & (row < 4 * TOKS)
        hsum = hsum + jnp.dot(
            jnp.where(inside, 1.0, 0.0).astype(BF16), h, preferred_element_type=F32
        )
        if ch == 1:
            ring(DOWN2, 7)
    ring(DOWN2, 8)
    compact(DOWN2, w_dn2)

    hmean = hsum[:8] * (1.0 / TOKS)
    high = hmean.astype(BF16)
    low = (hmean - high.astype(F32)).astype(BF16)
    both = lax.dot_general(
        jnp.concatenate([high.astype(F32), low.astype(F32)], axis=0).astype(BF16), w_dn2[...],
        (((1,), (1,)), ((), ())), preferred_element_type=F32,
    )
    partial = both[:8] + both[8:] + state_sum * (1.0 / TOKS)
    for k in range(13):
        part[k] = partial[:, 128 * k : 128 * k + 128]

    def send_part(k):
        @pl.when(k != mp)
        def _():
            copy(part.at[k], part_r.at[mp], s_pr.at[k], r_pr.at[mp], dp, k).start()

        @pl.when(k == mp)
        def _():
            part_r[mp] = part[k]

    loop(0, 13, send_part)

    @pl.when(mp < 13)
    def _():
        def wait_part(k):
            @pl.when(k != mp)
            def _():
                got(part_r.at[k], r_pr.at[k])

        loop(0, 16, wait_part)
        pooled = part_r[0]
        for k in range(1, 16):
            pooled = pooled + part_r[k]
        pooled_all[mp] = (pooled + bias2[mp]).astype(BF16).astype(F32)

        def send_pooled(k):
            copy(
                pooled_all.at[mp], pooled_all.at[mp], s_pf.at[k], r_pf.at[mp], dp,
                lax.rem(mp + k, 16),
            ).start()

        loop(1, 16, send_pooled)

    def wait_pooled(k):
        @pl.when(k != mp)
        def _():
            got(pooled_all.at[k], r_pf.at[k])

    proj_copy.wait()
    loop(0, 13, wait_pooled)
    pooled = jnp.concatenate([pooled_all[k] for k in range(13)], axis=1)
    pooled_norm = layer_norm(pooled, final_gain[...].reshape(1, D))
    pooled_norm = jnp.concatenate([pooled_norm, jnp.zeros_like(pooled_norm)], axis=0).astype(BF16)
    embedding = jnp.dot(pooled_norm, proj[...], preferred_element_type=F32)[:8]
    unit = embedding * lax.rsqrt(jnp.sum(embedding * embedding, axis=1, keepdims=True) + 1e-06)
    cols = pl.ds(pl.multiple_of(640 * core, 128), 640)
    rest = pl.ds(pl.multiple_of(640 * (1 - core), 128), 640)
    unit_g[dp] = unit[:4].astype(BF16)

    def send_unit(k):
        mine = unit_g.at[dp, :, cols]
        copy(mine, mine, s_un.at[k], r_un.at[k], lax.rem(dp + k, 16), mp).start()

    loop(1, 16, send_unit)

    def wait_cls(k):
        @pl.when(k != mp)
        def _():
            got(cls.at[k], r_cl.at[k])

    @pl.when(mp < CLS_BLOCKS)
    def _():
        loop(0, 16, wait_cls)

    def wait_unit(k):
        theirs = unit_g.at[lax.rem(dp + 16 - k, 16), :, cols]
        got(theirs, r_un.at[k])
        copy(theirs, theirs, s_us.at[k], r_us.at[k], dp, sibling).start()

    loop(1, 16, wait_unit)

    def wait_rest(k):
        got(unit_g.at[lax.rem(dp + 16 - k, 16), :, rest], r_us.at[k])

    loop(1, 16, wait_rest)

    @pl.when(mp < CLS_BLOCKS)
    def _():
        lhs = unit_g[...].astype(F32).reshape(64, EMB).astype(BF16)
        rhs = jnp.concatenate([cls[k] for k in range(16)], axis=0)
        scores = jnp.dot(lhs, rhs, preferred_element_type=F32) * 100.0
        lg[...] = scores.reshape(16, 4, 128)
        lr[dp] = lg[dp]

        def send_logits(k):
            to = lax.rem(dp + k, 16)
            copy(lg.at[to], lr.at[dp], s_lg.at[k], r_lg.at[k], to, mp).start()

        loop(1, 16, send_logits)

        def wait_logits(k):
            got(lr.at[lax.rem(dp + 16 - k, 16)], r_lg.at[k])

        loop(1, 16, wait_logits)
        ob[mp] = lr[...].reshape(64, 128).astype(BF16)

        def send_ob(k):
            copy(
                ob.at[mp], ob.at[mp], s_ob.at[k], r_ob.at[mp], dp, lax.rem(chip + k, 8) * 2 + core
            ).start()

        loop(1, 8, send_ob)
        copy(ob.at[mp], ob.at[mp], s_ob2.at[mp], r_ob2.at[mp], dp, sibling).start()

    for k in range(CLS_BLOCKS):
        @pl.when(jnp.logical_and(core == k % 2, mp != k))
        def _(k=k):
            got(ob.at[k], r_ob.at[k])
            copy(ob.at[k], ob.at[k], s_ob2.at[k], r_ob2.at[k], dp, sibling).start()

    for k in range(CLS_BLOCKS):
        @pl.when(core != k % 2)
        def _(k=k):
            got(ob.at[k], r_ob2.at[k])

    ob_out[...] = ob[...]

    def sent_a2a(k):
        sent(tok.at[pl.ds(0, 17)], s_a2a.at[k])
        sent(unit_g.at[0, :, cols], s_un.at[k])
        sent(unit_g.at[0, :, cols], s_us.at[k])

    loop(1, 16, sent_a2a)

    def sent_ring(t):
        def step(n):
            sent(gath.at[t, 0], s_ring.at[t, n])

        loop(0, 15, step)

    loop(0, 4, sent_ring)
    ag_sent(0, x1)
    ag_sent(1, x2)
    for o in range(4):
        sent(p_sib.at[o, pl.ds(0, 144 if o == 3 else 128)], s_half.at[o])
    loop(0, 14, lambda n: sent(red.at[0, 0], s_rs.at[n]))

    @pl.when(extra_src)
    def _():
        sent(extra_r.at[0], s_ex.at[0, 0])

    def sent_cls(k):
        @pl.when(k != mp)
        def _():
            sent(cls.at[0], s_cl.at[k])

    loop(0, CLS_BLOCKS, sent_cls)

    def sent_part(k):
        @pl.when(k != mp)
        def _():
            sent(part.at[0], s_pr.at[k])

    loop(0, 13, sent_part)

    @pl.when(mp < 13)
    def _():
        loop(1, 16, lambda k: sent(part.at[0], s_pf.at[k]))

    @pl.when(mp < CLS_BLOCKS)
    def _():
        loop(1, 16, lambda k: sent(lg.at[0], s_lg.at[k]))
        loop(1, 8, lambda k: sent(ob.at[0], s_ob.at[k]))

    for k in range(CLS_BLOCKS):
        @pl.when(core == k % 2)
        def _(k=k):
            sent(ob.at[0], s_ob2.at[k])


def finish(labels, ob, out, lab_out):
    found = jnp.zeros((4, 128), F32)
    lane = lax.broadcasted_iota(jnp.int32, (4, 128), 1)
    row = lax.broadcasted_iota(jnp.int32, (4, 128), 0)
    label = jnp.full((4, 128), labels[0], jnp.int32)
    for i in range(1, 4):
        label = jnp.where(row == i, labels[i], label)
    for k in range(CLS_BLOCKS):
        vals = ob[k].astype(F32)
        for g in range(16):
            first = (g * CLS_BLOCKS + k) * 128
            piece = vals[4 * g : 4 * g + 4]
            out[:, first : first + 128] = piece
            found = found + jnp.where(lane + first == label, piece, 0.0)
    for i in range(4):
        lab_out[i] = jnp.sum(found[i : i + 1])


def per_device(
    tokens, up_ckpts, up_bias_ckpts, down_ckpts, down_bias_ckpts, norm_ckpts, soup_mask,
    final_gain, projection, class_embed, labels,
):
    vm = pl.BlockSpec(memory_space=pltpu.VMEM)
    sm = pl.BlockSpec(memory_space=pltpu.SMEM)
    hbm = pl.BlockSpec(memory_space=pl.ANY)
    dma = pltpu.SemaphoreType.DMA
    scores = pl.pallas_call(
        kernel,
        out_shape=jax.ShapeDtypeStruct((CLS_BLOCKS, 64, 128), BF16),
        in_specs=[sm, vm, hbm, hbm, vm, vm, vm, vm, hbm, vm],
        out_specs=vm,
        scratch_shapes=[
            pltpu.VMEM((2, CKPT, DB, FFB), BF16),
            pltpu.VMEM((2, CKPT, DB, FFB), BF16),
            pltpu.VMEM((16, 17, 4, DB), BF16),
            pltpu.VMEM((OWN, D), F32),
            pltpu.VMEM((ROWS, D), BF16),
            pltpu.VMEM((ROWS, D), BF16),
            pltpu.VMEM((4, 16, 2 * DB, 256), BF16),
            pltpu.VMEM((D, FFB), BF16),
            pltpu.VMEM((D, FFB), BF16),
            pltpu.VMEM((D, FFB), BF16),
            pltpu.VMEM((D, FFB), BF16),
            pltpu.VMEM((ROWS, FFB), BF16),
            pltpu.VMEM((4, 144, D), BF16),
            pltpu.VMEM((4, 144, D), BF16),
            pltpu.VMEM((4, 144, D), BF16),
            pltpu.VMEM((7, 2, 32, D), BF16),
            pltpu.VMEM((16, D), F32),
            pltpu.VMEM((8, 16, D), BF16),
            pltpu.VMEM((13, 8, 128), F32),
            pltpu.VMEM((16, 8, 128), F32),
            pltpu.VMEM((13, 8, 128), F32),
            pltpu.VMEM((13, 8, 128), F32),
            pltpu.VMEM((D, EMB), BF16),
            pltpu.VMEM((16, 4, EMB), BF16),
            pltpu.VMEM((16, EMBB, 128), BF16),
            pltpu.VMEM((16, 4, 128), F32),
            pltpu.VMEM((16, 4, 128), F32),
            pltpu.VMEM((CLS_BLOCKS, 64, 128), BF16),
            dma((16,)), dma((16,)),
            dma((2, 14)), dma((2, 14)),
            dma((2, 17)), dma((2, 17)),
            dma((4, 15)), dma((4, 15)),
            dma((14,)), dma((14,)),
            dma((4,)), dma((4,)),
            dma((2, 8)), dma((10,)),
            dma((16,)), dma((16,)),
            dma((16,)), dma((16,)),
            dma((16,)), dma((16,)),
            dma((16,)), dma((16,)),
            dma((16,)), dma((16,)),
            dma((16,)), dma((16,)),
            dma((8,)), dma((16,)),
            dma((16,)), dma((16,)),
            dma(()),
            dma((4,)),
        ],
        compiler_params=pltpu.CompilerParams(
            collective_id=0, has_side_effects=True, vmem_limit_bytes=60 * 2**20
        ),
    )(
        soup_mask, jnp.swapaxes(tokens, 0, 1), up_ckpts, jnp.swapaxes(down_ckpts, 2, 3),
        jnp.swapaxes(up_bias_ckpts, 0, 1), jnp.swapaxes(down_bias_ckpts, 0, 1),
        jnp.swapaxes(norm_ckpts, 0, 1), final_gain, projection, class_embed.T,
    )
    return pl.pallas_call(
        finish,
        out_shape=(
            jax.ShapeDtypeStruct((4, 16 * CLS_BLOCKS * 128), F32),
            jax.ShapeDtypeStruct((4,), F32),
        ),
        in_specs=[sm, vm],
        out_specs=(vm, sm),
    )(labels, scores)


def solution(mesh):
    placed = (
        P("dp", None, "mp"),
        P(None, None, "dp", "mp"),
        P(None, None, "mp"),
        P(None, None, "mp", "dp"),
        P(),
        P(),
        P(),
        P(),
        P(),
        P("dp", "mp"),
        P("dp"),
    )
    return jax.shard_map(
        per_device, mesh=mesh, in_specs=placed, out_specs=(P("dp", None), P("dp")), check_vma=False
    )
```

```python
import functools

import jax
import jax.numpy as jnp
from jax import lax
from jax.experimental import pallas as pl
from jax.experimental.pallas import tpu as pltpu
from jax.sharding import PartitionSpec as P

MESH = pl.DeviceIdType.MESH
F32 = jnp.float32
BF16 = jnp.bfloat16

CKPT = 10
D = 1664
DB = 104
FFB = 512
EMB = 1280
EMBB = 80
TOKS = 257
ROWS = 1040
OWN = 80
CHUNK = 208
CLS_BLOCKS = 11
UP1, DOWN1, UP2, DOWN2 = 0, 1, 2, 3
PLACES = ((-1, 0), (1, 0), (0, 1), (-1, 1), (1, 1), (2, 0), (2, 1), (0, 0))
FAR = (0, -1, 1, -2, 2, -3, 3, 4)
STEPS = (2, -1, 1, 0)


def layer_norm(values, gain):
    center = values - jnp.mean(values, axis=-1, keepdims=True)
    spread = jnp.mean(center * center, axis=-1, keepdims=True)
    return center * lax.rsqrt(spread + 1e-05) * gain


def gelu(values):
    return 0.5 * values * (1.0 + lax.erf(values * 0.7071067811865476))


def kernel(
    mask, tok_hbm, up_hbm, down_hbm, up_b_hbm, down_b_hbm, norm_hbm, final_hbm, proj_hbm, cet_hbm,
    ob_out,
    up_ck, down_ck, tok, up_b, down_b, norm_g, final_gain, cet, a2a, state, x1, x2, gath, w_up1, w_dn1, w_up2, w_dn2, hid, p_sib, s_sib, t_own,
    red, extra_r, part, part_r, pair, proj, unit_m, unit_r, cls, lg, lr, ob,
    s_a2a, r_a2a, s_ag, r_ag, s_sb, r_sb, s_ring, r_ring, s_far, r_far, s_rs, r_rs, s_half, r_half, s_ex, r_ex,
    s_pr, r_pr, s_cl, r_cl, s_un, r_un, s_lg, r_lg, s_ob, r_ob,
    ck_sem,
):
    dp = lax.axis_index("dp")
    mp = lax.axis_index("mp")
    yh, z = lax.div(dp, 8), lax.rem(dp, 8)
    core = lax.rem(mp, 2)
    chip = lax.div(mp, 2)
    yl, xc = lax.div(mp, 8), lax.rem(chip, 4)
    other_yh = 1 - yh
    block = core * 8 + xc * 2 + yl
    last = block == 15
    extra_src = jnp.logical_and(core == 1, block != 15)
    sibling = chip * 2 + (1 - core)

    def device(y, dx):
        return y * 8 + lax.rem(xc + dx + 4, 4) * 2 + core

    right, left, across = device(yl, 1), device(yl, -1), device(1 - yl, 0)

    def copy(src, dst, ssem, rsem, to_dp, to_mp):
        return pltpu.make_async_remote_copy(
            src_ref=src, dst_ref=dst, send_sem=ssem, recv_sem=rsem,
            device_id={"dp": to_dp, "mp": to_mp}, device_id_type=MESH,
        )

    def got(ref, rsem):
        copy(ref, ref, s_half.at[0], rsem, dp, sibling).wait_recv()

    def sent(ref, ssem):
        copy(ref, ref, ssem, r_half.at[0], dp, sibling).wait_send()

    def loop(lo, hi, body):
        def step(k, carry):
            body(k)
            return carry

        lax.fori_loop(lo, hi, step, 0)

    loads = [
        pltpu.make_async_copy(src.at[layer], dst.at[layer], ck_sem.at[n])
        for n, (src, dst, layer) in enumerate(
            ((up_hbm, up_ck, 0), (down_hbm, down_ck, 0), (up_hbm, up_ck, 1), (down_hbm, down_ck, 1))
        )
    ]
    tok_load, norm_load, up_b_load, cet_load, down_b_load, final_load, proj_load = (
        pltpu.make_async_copy(src, dst, ck_sem.at[4 + n])
        for n, (src, dst) in enumerate(
            (
                (tok_hbm, tok), (norm_hbm, norm_g), (up_b_hbm, up_b), (cet_hbm, cet),
                (down_b_hbm, down_b), (final_hbm, final_gain), (proj_hbm, proj),
            )
        )
    )
    tok_load.start()
    for load in loads:
        load.start()
    for load in (norm_load, up_b_load, cet_load, down_b_load, final_load, proj_load):
        load.start()

    state[64:80, :] = jnp.zeros((16, D), F32)
    ob[1, 5] = jnp.zeros((64, 128), BF16)
    barrier = pltpu.get_barrier_semaphore()

    def greet(k):
        pl.semaphore_signal(
            barrier, inc=1, device_id={"dp": dp, "mp": lax.rem(mp + k, 16)}, device_id_type=MESH
        )
        pl.semaphore_signal(
            barrier, inc=1, device_id={"dp": lax.rem(dp + k, 16), "mp": mp}, device_id_type=MESH
        )

    loop(1, 16, greet)

    mask_f = [mask[i].astype(F32) for i in range(CKPT)]
    total = mask_f[0]
    for i in range(1, CKPT):
        total = total + mask_f[i]
    total_v = jnp.full((1, 128), total, F32)
    share_v = [jnp.full((1, 128), v, F32) / total_v for v in mask_f]

    def soup_vec(ref, layer, width):
        acc = jnp.zeros((1, width), F32)
        for i in range(CKPT):
            acc = acc + jnp.tile(share_v[i], (1, width // 128)) * ref[i, layer : layer + 1, :]
        return acc

    def soup(ref, layer, cs):
        acc = jnp.zeros((DB, 128), F32)
        for i in range(CKPT):
            acc = acc + share_v[i] * ref[layer, i, :, 128 * cs : 128 * cs + 128].astype(F32)
        return acc

    def own_shard(t, ref, layer):
        loads[t].wait()
        for h in range(2):
            both = jnp.concatenate([soup(ref, layer, h), soup(ref, layer, 2 + h)], axis=0)
            gath[t, dp, :, 128 * h : 128 * h + 128] = both.astype(BF16)

    z_next, z_prev = yh * 8 + lax.rem(z + 1, 8), yh * 8 + lax.rem(z + 7, 8)

    def slot(which_yh, shift):
        return which_yh * 8 + lax.rem(z + shift + 8, 8)

    def ring_push(t, s, n, to):
        copy(gath.at[t, s], gath.at[t, s], s_ring.at[t, n], r_ring.at[t, n], to, mp).start()

    def ring_got(t, s, n):
        got(gath.at[t, s], r_ring.at[t, n])

    def ring(t, step):
        if step == 9:
            ring_push(t, dp, 14, other_yh * 8 + z)
        elif step == 0:
            ring_push(t, dp, 0, z_next)
            ring_push(t, dp, 7, z_prev)
        elif step == 1:
            s = slot(other_yh, 0)
            ring_got(t, s, 14)
            ring_push(t, s, 1, z_next)
            ring_push(t, s, 8, z_prev)
        elif step < 8:
            n = step - 2
            dist = n // 2 + 1
            which = yh if n % 2 == 0 else other_yh
            sl, sr = slot(which, -dist), slot(which, dist)
            ring_got(t, sl, n)
            if n < 5:
                ring_push(t, sl, n + 2, z_next)
            ring_got(t, sr, 7 + n)
            if n < 4:
                ring_push(t, sr, 7 + n + 2, z_prev)
            elif n == 5:
                ring_push(t, sr, 7 + 6, z_prev)
        else:
            ring_got(t, slot(yh, 4), 6)
            ring_got(t, slot(other_yh, 4), 13)

    def far_across(t, k):
        s = slot(yh, FAR[k])
        copy(
            gath.at[t, s], gath.at[t, s], s_far.at[k], r_far.at[k], other_yh * 8 + z, mp
        ).start()

    def far_ring(t, step):
        if step == 0:
            ring_push(t, dp, 0, z_next)
            ring_push(t, dp, 7, z_prev)
        elif step < 4:
            sl, sr = slot(yh, -step), slot(yh, step)
            ring_got(t, sl, step - 1)
            ring_push(t, sl, step, z_next)
            ring_got(t, sr, 7 + step - 1)
            if step < 3:
                ring_push(t, sr, 7 + step, z_prev)
            if step == 1:
                far_across(t, 0)
            far_across(t, 2 * step - 1)
            far_across(t, 2 * step)
        elif step == 4:
            ring_got(t, slot(yh, 4), 3)
            far_across(t, 7)
        else:
            for k in range(8):
                got(gath.at[t, slot(other_yh, FAR[k])], r_far.at[k])

    def compact(t, dst):
        def pair(j):
            g0 = gath[t, 2 * j].astype(F32)
            g1 = gath[t, 2 * j + 1].astype(F32)
            rows = pl.ds(pl.multiple_of(208 * j, 16), 208)
            dst[rows, 0:256] = jnp.concatenate([g0[:DB], g1[:DB]], axis=0).astype(BF16)
            dst[rows, 256:512] = jnp.concatenate([g0[DB:], g1[DB:]], axis=0).astype(BF16)

        loop(0, 8, pair)

    def block_rows(c, dx, y):
        return pl.multiple_of(512 * c + 128 * lax.rem(xc + dx + 4, 4) + 64 * y, 16)

    def half_rows(x, c, idx, h):
        dx, other = PLACES[idx]
        y = 1 - yl if other else yl
        return x.at[pl.ds(block_rows(c, dx, y) + 32 * h, 32)]

    def ag_push(lay, x, idx_here, idx, h, to):
        rows = half_rows(x, core, idx_here, h)
        n = 2 * idx + h
        copy(rows, rows, s_ag.at[lay, n], r_ag.at[lay, n], dp, to).start()

    def ag_sib(lay, x, idx, h):
        rows = half_rows(x, core, idx, h)
        n = 2 * idx + h
        copy(rows, rows, s_sb.at[lay, n], r_sb.at[lay, n], dp, sibling).start()

    def ag_start(lay, x, h):
        ag_push(lay, x, 7, 0, h, right)
        ag_push(lay, x, 7, 1, h, left)
        ag_push(lay, x, 7, 2, h, across)
        ag_sib(lay, x, 7, h)

    def ag_start_extra(lay, x):
        extra = x.at[pl.ds(1024, 16)]

        @pl.when(last)
        def _():
            def push_extra(k):
                copy(
                    extra, extra, s_ex.at[lay, k], r_ex.at[lay], dp, lax.rem(chip + k, 8) * 2 + core
                ).start()

            loop(1, 8, push_extra)
            copy(extra, extra, s_sb.at[lay, 16], r_sb.at[lay, 16], dp, sibling).start()

    def ag_recv(lay, x, idx, h):
        got(half_rows(x, core, idx, h), r_ag.at[lay, 2 * idx + h])
        by_y = lay == 1 and h == 1
        if idx == 0:
            ag_push(lay, x, 0, 5, h, right)
            if by_y:
                ag_push(lay, x, 0, 3, h, across)
        elif idx == 1 and by_y:
            ag_push(lay, x, 1, 4, h, across)
        elif idx == 2 and not by_y:
            ag_push(lay, x, 2, 3, h, right)
            ag_push(lay, x, 2, 4, h, left)
        elif idx == 4:
            ag_push(lay, x, 4, 6, h, left)
        ag_sib(lay, x, idx, h)

    def ag_extra(lay, x):
        extra = x.at[pl.ds(1024, 16)]

        @pl.when(extra_src)
        def _():
            got(extra, r_ex.at[lay])
            copy(extra, extra, s_sb.at[lay, 16], r_sb.at[lay, 16], dp, sibling).start()

    def ag_finish(lay, x):
        for idx in range(8):
            for h in range(2):
                got(half_rows(x, 1 - core, idx, h), r_sb.at[lay, 2 * idx + h])

        @pl.when(core == 0)
        def _():
            got(x.at[pl.ds(1024, 16)], r_sb.at[lay, 16])

    def ag_sent(lay, x):
        rows = x.at[pl.ds(0, 32)]
        extra = x.at[pl.ds(1024, 16)]
        loop(0, 14, lambda n: sent(rows, s_ag.at[lay, n]))
        loop(0, 16, lambda n: sent(rows, s_sb.at[lay, n]))

        @pl.when(last)
        def _():
            loop(1, 8, lambda k: sent(extra, s_ex.at[lay, k]))

        @pl.when(core == 1)
        def _():
            sent(extra, s_sb.at[lay, 16])

    def normed_rows(x, gain):
        rows = layer_norm(state[...], gain).astype(BF16)
        x[pl.ds(block_rows(core, 0, yl), 64), :] = rows[:64]

        @pl.when(last)
        def _():
            x[1024:1040, :] = rows[64:]

    def up_chunk(x, w, bias, ch):
        rows = pl.ds(CHUNK * ch, CHUNK)
        return gelu(jnp.dot(x[rows, :], w[...], preferred_element_type=F32) + bias).astype(BF16)

    def down_product(rows):
        return lax.dot_general(
            rows, w_dn1[...], (((1,), (1,)), ((), ())), preferred_element_type=F32
        )

    def rs_rows(o, y, h):
        return t_own.at[o, pl.ds(pl.multiple_of(64 * y + 32 * h, 16), 32)]

    def rs_push(o, y, kind, h, to):
        n = 2 * kind + h
        copy(rs_rows(o, y, h), red.at[kind, h], s_rs.at[n], r_rs.at[n], dp, to).start()

    def rs_add(o, y, h, *kinds):
        rows = rs_rows(o, y, h)
        acc = rows[...].astype(F32)
        for kind in kinds:
            got(red.at[kind, h], r_rs.at[2 * kind + h])
            acc = acc + red[kind, h].astype(F32)
        rows[...] = acc.astype(BF16)

    own_shard(UP1, up_ck, 0)
    tok_load.wait()
    pl.semaphore_wait(barrier, 30)

    def send_tokens(k):
        m2 = lax.rem(mp + k, 16)
        b2 = lax.rem(m2, 2) * 8 + lax.rem(lax.div(m2, 2), 4) * 2 + lax.div(m2, 8)
        src = tok.at[pl.ds(16 * b2, 17)]
        copy(src, a2a.at[mp], s_a2a.at[k], r_a2a.at[k], dp, m2).start()

    loop(1, 16, send_tokens)
    ring(UP1, 9)
    ring(UP1, 0)
    a2a[mp] = tok[pl.ds(16 * block, 17)]
    own_shard(DOWN1, down_ck, 0)
    far_ring(DOWN1, 0)
    norm_load.wait()
    gain1 = soup_vec(norm_g, 0, D)

    def wait_tokens(k):
        got(a2a.at[lax.rem(mp + 16 - k, 16)], r_a2a.at[k])

    loop(1, 16, wait_tokens)
    for j in range(16):
        state[:68, DB * j : DB * j + DB] = a2a[j].astype(F32).reshape(68, DB)
    normed_rows(x1, gain1)
    ag_start(0, x1, 0)
    ag_start(0, x1, 1)
    ag_start_extra(0, x1)
    ring(UP1, 1)
    ring(UP1, 2)
    own_shard(UP2, up_ck, 1)
    far_ring(DOWN1, 1)
    ring(UP1, 3)
    for idx in range(3):
        ag_recv(0, x1, idx, 0)
    ring(UP1, 4)
    for idx in range(3):
        ag_recv(0, x1, idx, 1)
    far_ring(DOWN1, 2)
    ring(UP1, 5)
    ag_recv(0, x1, 3, 0)
    ag_recv(0, x1, 4, 0)
    ring(UP1, 6)
    far_ring(DOWN1, 3)
    ag_recv(0, x1, 3, 1)
    ag_recv(0, x1, 4, 1)
    ag_recv(0, x1, 5, 0)
    ring(UP1, 7)
    ag_recv(0, x1, 5, 1)
    ag_recv(0, x1, 6, 0)
    far_ring(DOWN1, 4)
    ag_recv(0, x1, 6, 1)
    ag_extra(0, x1)
    own_shard(DOWN2, down_ck, 1)
    ring(UP1, 8)
    ring(UP2, 0)
    compact(UP1, w_up1)
    up_b_load.wait()
    bias_up1 = soup_vec(up_b, 0, FFB)
    ag_finish(0, x1)
    for ch in range(5):
        hid[CHUNK * ch : CHUNK * ch + CHUNK, :] = up_chunk(x1, w_up1, bias_up1, ch)
        if ch == 1:
            ring(UP2, 9)
        if ch == 3:
            ring(UP2, 2)

    def send_cls(k):
        @pl.when(k != mp)
        def _():
            src = cet.at[:, pl.ds(pl.multiple_of(128 * k, 128), 128)]
            copy(src, cls.at[mp], s_cl.at[k], r_cl.at[mp], dp, k).start()

        @pl.when(k == mp)
        def _():
            cls[mp] = cet[:, pl.ds(pl.multiple_of(128 * k, 128), 128)]

    cet_load.wait()
    loop(0, CLS_BLOCKS, send_cls)
    down_b_load.wait()
    gain2 = soup_vec(norm_g, 1, D)
    bias_down1 = soup_vec(down_b, 0, D)
    bias_up2 = soup_vec(up_b, 1, FFB)
    bias_down2 = soup_vec(down_b, 1, D)
    far_ring(DOWN1, 5)
    ring(UP2, 1)
    compact(DOWN1, w_dn1)

    def chunk_product(o, c):
        lhs = hid[pl.ds(block_rows(c, STEPS[o], 0), 128), :]
        if STEPS[o] == 0:
            lhs = jnp.concatenate([lhs, hid[1024:1040, :]], axis=0)
        return down_product(lhs)

    def chunk_rows(o):
        return pl.ds(0, 144 if STEPS[o] == 0 else 128)

    def sib_chunk(o):
        rows = chunk_rows(o)
        p_sib[o, rows, :] = chunk_product(o, 1 - core).astype(BF16)
        copy(p_sib.at[o, rows], s_sib.at[o, rows], s_half.at[o], r_half.at[o], dp, sibling).start()

    def own_chunk(o):
        rows = chunk_rows(o)
        term = chunk_product(o, core)
        got(s_sib.at[o, rows], r_half.at[o])
        t_own[o, rows, :] = (term + s_sib[o, rows, :].astype(F32)).astype(BF16)

    def finish_half(h):
        rs_add(3, yl, h, 4, 5, 6)
        part_rows = slice(32 * h, 32 * h + 32)
        new = state[part_rows, :] + bias_down1 + rs_rows(3, yl, h)[...].astype(F32)
        new = new.astype(BF16).astype(F32)
        state[part_rows, :] = new
        x2[pl.ds(block_rows(core, 0, yl) + 32 * h, 32), :] = layer_norm(new, gain2).astype(BF16)
        ag_start(1, x2, h)

    sib_chunk(0)
    sib_chunk(1)
    own_chunk(0)
    for h in range(2):
        rs_push(0, yl, 0, h, left)
        rs_push(0, 1 - yl, 1, h, right)
    ring(UP2, 3)
    sib_chunk(2)
    own_chunk(1)
    rs_push(1, 1 - yl, 2, 0, left)
    rs_push(1, 1 - yl, 2, 1, left)
    ring(UP2, 4)
    sib_chunk(3)
    own_chunk(2)
    for h in range(2):
        rs_add(2, 1 - yl, h, 1)
        rs_push(2, 1 - yl, 3, h, right)
    ring(UP2, 5)
    for h in range(2):
        rs_add(1, yl, h, 0)
        rs_push(1, yl, 4, h, left)
        rs_push(2, yl, 5, h, right)
    ring(UP2, 6)
    own_chunk(3)

    @pl.when(extra_src)
    def _():
        copy(
            t_own.at[3, pl.ds(128, 16)], extra_r.at[chip], s_ex.at[0, 0], r_ex.at[2 + chip], dp, 15
        ).start()

    rs_add(3, 1 - yl, 0, 3, 2)
    rs_push(3, 1 - yl, 6, 0, across)
    ring(UP2, 7)
    ring(DOWN2, 0)
    rs_add(3, 1 - yl, 1, 3, 2)
    rs_push(3, 1 - yl, 6, 1, across)
    ring(UP2, 8)
    ring(DOWN2, 9)
    finish_half(0)
    ring(DOWN2, 2)
    finish_half(1)

    @pl.when(last)
    def _():
        extra = t_own[3, 128:144, :].astype(F32)
        for q in range(7):
            got(extra_r.at[q], r_ex.at[2 + q])
            extra = extra + extra_r[q].astype(F32)
        extra = (state[64:80, :] + bias_down1 + extra).astype(BF16).astype(F32)
        state[64:80, :] = extra
        x2[1024:1040, :] = layer_norm(extra, gain2).astype(BF16)

    ag_start_extra(1, x2)

    row = lax.broadcasted_iota(jnp.int32, (16, OWN), 1)
    img = lax.broadcasted_iota(jnp.int32, (16, OWN), 0)
    inside = ((row & 3) == img) & (row < jnp.where(last, 68, 64))
    state_sum = jnp.dot(
        jnp.where(inside, 1.0, 0.0).astype(BF16), state[...].astype(BF16), preferred_element_type=F32
    )[:8]
    ring(DOWN2, 1)
    ring(DOWN2, 3)
    for idx in range(3):
        ag_recv(1, x2, idx, 0)
    compact(UP2, w_up2)
    ring(DOWN2, 4)
    for idx in range(3):
        ag_recv(1, x2, idx, 1)
    ring(DOWN2, 5)
    ag_recv(1, x2, 3, 0)
    ag_recv(1, x2, 4, 0)
    ag_recv(1, x2, 5, 0)
    ring(DOWN2, 6)
    ag_recv(1, x2, 3, 1)
    ag_recv(1, x2, 4, 1)
    ag_recv(1, x2, 6, 0)
    ring(DOWN2, 7)
    ag_recv(1, x2, 5, 1)
    ag_recv(1, x2, 6, 1)
    ag_extra(1, x2)
    ag_finish(1, x2)
    hsum = jnp.zeros((16, FFB), F32)
    for ch in range(5):
        h = up_chunk(x2, w_up2, bias_up2, ch)
        row = lax.broadcasted_iota(jnp.int32, (16, CHUNK), 1) + CHUNK * ch
        img = lax.broadcasted_iota(jnp.int32, (16, CHUNK), 0)
        inside = ((row & 3) == img) & (row < 4 * TOKS)
        hsum = hsum + jnp.dot(
            jnp.where(inside, 1.0, 0.0).astype(BF16), h, preferred_element_type=F32
        )
    ring(DOWN2, 8)
    compact(DOWN2, w_dn2)

    hmean = hsum[:8] * (1.0 / TOKS)
    high = hmean.astype(BF16)
    low = (hmean - high.astype(F32)).astype(BF16)
    both = lax.dot_general(
        jnp.concatenate([high.astype(F32), low.astype(F32)], axis=0).astype(BF16), w_dn2[...],
        (((1,), (1,)), ((), ())), preferred_element_type=F32,
    )
    partial = both[:8] + both[8:] + state_sum * (1.0 / TOKS)
    part[...] = partial[:4]
    copy(part, part_r, s_pr.at[0], r_pr.at[0], dp, sibling).start()
    got(part_r, r_pr.at[0])
    pair[chip] = (part[...] + part_r[...]).astype(BF16)

    def send_pair(k):
        copy(
            pair.at[chip], pair.at[chip], s_pr.at[k], r_pr.at[k], dp, lax.rem(chip + k, 8) * 2 + core
        ).start()

    loop(1, 8, send_pair)
    final_load.wait()
    proj_load.wait()
    loop(1, 8, lambda k: got(pair.at[lax.rem(chip + 8 - k, 8)], r_pr.at[k]))
    pooled = pair[0].astype(F32)
    for k in range(1, 8):
        pooled = pooled + pair[k].astype(F32)
    pooled = (pooled + bias_down2).astype(BF16).astype(F32)
    pooled = jnp.concatenate([pooled, jnp.zeros_like(pooled)], axis=0)
    pooled_norm = layer_norm(pooled, final_gain[...].reshape(1, D))
    pooled_norm = jnp.concatenate([pooled_norm, jnp.zeros_like(pooled_norm)], axis=0).astype(BF16)
    embedding = jnp.dot(pooled_norm, proj[...], preferred_element_type=F32)[:8]
    unit = embedding * lax.rsqrt(jnp.sum(embedding * embedding, axis=1, keepdims=True) + 1e-06)
    first_core = core == 0
    unit_m[dp] = jnp.where(first_core, unit[:4, :640], unit[:4, 640:]).astype(BF16)

    def send_unit(k):
        mine = unit_m.at[dp]
        copy(mine, mine, s_un.at[k], r_un.at[k], lax.rem(dp + k, 16), mp).start()

    loop(1, 16, send_unit)

    loop(1, 16, lambda k: sent(tok.at[pl.ds(0, 17)], s_a2a.at[k]))

    def sent_ring(t):
        def step(n):
            sent(gath.at[t, 0], s_ring.at[t, n])

        loop(0, 15, step)

    for t in (UP1, UP2, DOWN2):
        sent_ring(t)
    loop(0, 4, lambda n: sent(gath.at[0, 0], s_ring.at[DOWN1, n]))
    loop(7, 10, lambda n: sent(gath.at[0, 0], s_ring.at[DOWN1, n]))
    loop(0, 8, lambda n: sent(gath.at[0, 0], s_far.at[n]))
    ag_sent(0, x1)
    ag_sent(1, x2)
    for o in range(4):
        sent(p_sib.at[o, pl.ds(0, 144 if o == 3 else 128)], s_half.at[o])
    loop(0, 14, lambda n: sent(red.at[0, 0], s_rs.at[n]))

    @pl.when(extra_src)
    def _():
        sent(extra_r.at[0], s_ex.at[0, 0])

    def sent_cls(k):
        @pl.when(k != mp)
        def _():
            sent(cls.at[0], s_cl.at[k])

    loop(0, CLS_BLOCKS, sent_cls)


    def wait_cls(k):
        @pl.when(k != mp)
        def _():
            got(cls.at[k], r_cl.at[k])

    @pl.when(mp < CLS_BLOCKS)
    def _():
        loop(0, 16, wait_cls)

    loop(1, 16, lambda k: got(unit_m.at[lax.rem(dp + 16 - k, 16)], r_un.at[k]))
    copy(unit_m, unit_r, s_un.at[0], r_un.at[0], dp, sibling).start()
    got(unit_r, r_un.at[0])

    @pl.when(mp < CLS_BLOCKS)
    def _():
        mine = unit_m[...].astype(F32).reshape(64, 640)
        rest = unit_r[...].astype(F32).reshape(64, 640)
        lhs = jnp.concatenate(
            [jnp.where(first_core, mine, rest), jnp.where(first_core, rest, mine)], axis=1
        ).astype(BF16)
        rhs = jnp.concatenate([cls[k] for k in range(16)], axis=0)
        scores = jnp.dot(lhs, rhs, preferred_element_type=F32) * 100.0
        lg[...] = scores.reshape(16, 4, 128)
        lr[dp] = lg[dp]

        def send_logits(k):
            to = lax.rem(dp + k, 16)
            copy(lg.at[to], lr.at[dp], s_lg.at[k], r_lg.at[k], to, mp).start()

        loop(1, 16, send_logits)

        def wait_logits(k):
            got(lr.at[lax.rem(dp + 16 - k, 16)], r_lg.at[k])

        loop(1, 16, wait_logits)
        ob[core, chip] = lr[...].reshape(64, 128).astype(BF16)

        def send_ob(k):
            mine = ob.at[core, chip]
            copy(mine, mine, s_ob.at[k], r_ob.at[chip], dp, lax.rem(chip + k, 8) * 2 + core).start()

        loop(1, 8, send_ob)

    for k in range(6):
        @pl.when(jnp.logical_and(chip != k, 2 * k + core < CLS_BLOCKS))
        def _(k=k):
            got(ob.at[core, k], r_ob.at[k])

    copy(ob.at[core], ob.at[core], s_ob.at[0], r_ob.at[8], dp, sibling).start()
    got(ob.at[1 - core], r_ob.at[8])
    ob_out[...] = ob[...]

    loop(1, 16, lambda k: sent(unit_m.at[0], s_un.at[k]))
    sent(unit_m, s_un.at[0])
    sent(part, s_pr.at[0])
    loop(1, 8, lambda k: sent(pair.at[0], s_pr.at[k]))

    @pl.when(mp < CLS_BLOCKS)
    def _():
        loop(1, 16, lambda k: sent(lg.at[0], s_lg.at[k]))
        loop(1, 8, lambda k: sent(ob.at[0, 0], s_ob.at[k]))

    sent(ob.at[0], s_ob.at[0])


def finish(labels, ob, out, lab_out):
    found = jnp.zeros((4, 128), F32)
    lane = lax.broadcasted_iota(jnp.int32, (4, 128), 1)
    row = lax.broadcasted_iota(jnp.int32, (4, 128), 0)
    label = jnp.full((4, 128), labels[0], jnp.int32)
    for i in range(1, 4):
        label = jnp.where(row == i, labels[i], label)
    for k in range(CLS_BLOCKS):
        vals = ob[k % 2, k // 2].astype(F32)
        for g in range(16):
            first = (g * CLS_BLOCKS + k) * 128
            piece = vals[4 * g : 4 * g + 4]
            out[:, first : first + 128] = piece
            found = found + jnp.where(lane + first == label, piece, 0.0)
    for i in range(4):
        lab_out[i] = jnp.sum(found[i : i + 1])


def per_device(
    tokens, up_ckpts, up_bias_ckpts, down_ckpts, down_bias_ckpts, norm_ckpts, soup_mask,
    final_gain, projection, class_embed, labels,
):
    vm = pl.BlockSpec(memory_space=pltpu.VMEM)
    sm = pl.BlockSpec(memory_space=pltpu.SMEM)
    hbm = pl.BlockSpec(memory_space=pl.ANY)
    dma = pltpu.SemaphoreType.DMA
    scores = pl.pallas_call(
        kernel,
        out_shape=jax.ShapeDtypeStruct((2, 6, 64, 128), BF16),
        in_specs=[sm] + [hbm] * 9,
        out_specs=vm,
        scratch_shapes=[
            pltpu.VMEM((2, CKPT, DB, FFB), BF16),
            pltpu.VMEM((2, CKPT, DB, FFB), BF16),
            pltpu.VMEM((TOKS, 4, DB), BF16),
            pltpu.VMEM((CKPT, 2, FFB), F32),
            pltpu.VMEM((CKPT, 2, D), F32),
            pltpu.VMEM((CKPT, 2, D), F32),
            pltpu.VMEM((D,), F32),
            pltpu.VMEM((EMBB, CLS_BLOCKS * 128), BF16),
            pltpu.VMEM((16, 17, 4, DB), BF16),
            pltpu.VMEM((OWN, D), F32),
            pltpu.VMEM((ROWS, D), BF16),
            pltpu.VMEM((ROWS, D), BF16),
            pltpu.VMEM((4, 16, 2 * DB, 256), BF16),
            pltpu.VMEM((D, FFB), BF16),
            pltpu.VMEM((D, FFB), BF16),
            pltpu.VMEM((D, FFB), BF16),
            pltpu.VMEM((D, FFB), BF16),
            pltpu.VMEM((ROWS, FFB), BF16),
            pltpu.VMEM((4, 144, D), BF16),
            pltpu.VMEM((4, 144, D), BF16),
            pltpu.VMEM((4, 144, D), BF16),
            pltpu.VMEM((7, 2, 32, D), BF16),
            pltpu.VMEM((8, 16, D), BF16),
            pltpu.VMEM((4, D), F32),
            pltpu.VMEM((4, D), F32),
            pltpu.VMEM((8, 4, D), BF16),
            pltpu.VMEM((D, EMB), BF16),
            pltpu.VMEM((16, 4, EMB // 2), BF16),
            pltpu.VMEM((16, 4, EMB // 2), BF16),
            pltpu.VMEM((16, EMBB, 128), BF16),
            pltpu.VMEM((16, 4, 128), F32),
            pltpu.VMEM((16, 4, 128), F32),
            pltpu.VMEM((2, 6, 64, 128), BF16),
            dma((16,)), dma((16,)),
            dma((2, 14)), dma((2, 14)),
            dma((2, 17)), dma((2, 17)),
            dma((4, 15)), dma((4, 15)),
            dma((8,)), dma((8,)),
            dma((14,)), dma((14,)),
            dma((4,)), dma((4,)),
            dma((2, 8)), dma((10,)),
            dma((8,)), dma((8,)),
            dma((16,)), dma((16,)),
            dma((16,)), dma((16,)),
            dma((16,)), dma((16,)),
            dma((8,)), dma((9,)),
            dma((11,)),
        ],
        compiler_params=pltpu.CompilerParams(
            collective_id=0, has_side_effects=True, vmem_limit_bytes=60 * 2**20
        ),
    )(
        soup_mask, jnp.swapaxes(tokens, 0, 1), up_ckpts, jnp.swapaxes(down_ckpts, 2, 3),
        jnp.swapaxes(up_bias_ckpts, 0, 1), jnp.swapaxes(down_bias_ckpts, 0, 1),
        jnp.swapaxes(norm_ckpts, 0, 1), final_gain, projection, class_embed.T,
    )
    return pl.pallas_call(
        finish,
        out_shape=(
            jax.ShapeDtypeStruct((4, 16 * CLS_BLOCKS * 128), F32),
            jax.ShapeDtypeStruct((4,), F32),
        ),
        in_specs=[sm, vm],
        out_specs=(vm, sm),
    )(labels, scores)


def solution(mesh):
    placed = (
        P("dp", None, "mp"),
        P(None, None, "dp", "mp"),
        P(None, None, "mp"),
        P(None, None, "mp", "dp"),
        P(),
        P(),
        P(),
        P(),
        P(),
        P("dp", "mp"),
        P("dp"),
    )
    return jax.shard_map(
        per_device, mesh=mesh, in_specs=placed, out_specs=(P("dp", None), P("dp")), check_vma=False
    )
```

```python
import functools

import jax
import jax.numpy as jnp
from jax import lax
from jax.experimental import pallas as pl
from jax.experimental.pallas import tpu as pltpu
from jax.sharding import PartitionSpec as P

MESH = pl.DeviceIdType.MESH
F32 = jnp.float32
BF16 = jnp.bfloat16

CKPT = 10
D = 1664
DB = 104
FFB = 512
EMB = 1280
EMBB = 80
TOKS = 257
ROWS = 1040
OWN = 80
CHUNK = 208
CLS_BLOCKS = 11
WORKERS = 6
UP1, DOWN1, UP2, DOWN2 = 0, 1, 2, 3
PLACES = ((-1, 0), (1, 0), (0, 1), (-1, 1), (1, 1), (2, 0), (2, 1), (0, 0))
FAR = (0, -1, 1, -2, 2, -3, 3, 4)
STEPS = (2, -1, 1, 0)


def layer_norm(values, gain):
    center = values - jnp.mean(values, axis=-1, keepdims=True)
    spread = jnp.mean(center * center, axis=-1, keepdims=True)
    return center * lax.rsqrt(spread + 1e-05) * gain


def gelu(values):
    return 0.5 * values * (1.0 + lax.erf(values * 0.7071067811865476))


def kernel(
    mask, tok_hbm, up_hbm, down_hbm, up_b_hbm, down_b_hbm, norm_hbm, final_hbm, proj_hbm, cet_hbm,
    ob_out,
    up_ck, down_ck, tok, up_b, down_b, norm_g, final_gain, cet, a2a, state, x1, x2, gath, w_up1, w_dn1, w_up2, w_dn2, hid, p_sib, s_sib, t_own,
    red, extra_r, pair, proj, unit_m, cls, lg, lr, ob,
    s_a2a, r_a2a, s_ag, r_ag, s_sb, r_sb, s_ring, r_ring, s_far, r_far, s_rs, r_rs, s_half, r_half, s_ex, r_ex,
    s_pr, r_pr, s_cl, r_cl, s_un, r_un, s_lg, r_lg, s_ob, r_ob, s_os, r_os,
    ck_sem,
):
    dp = lax.axis_index("dp")
    mp = lax.axis_index("mp")
    yh, z = lax.div(dp, 8), lax.rem(dp, 8)
    core = lax.rem(mp, 2)
    chip = lax.div(mp, 2)
    yl, xc = lax.div(mp, 8), lax.rem(chip, 4)
    other_yh = 1 - yh
    block = core * 8 + xc * 2 + yl
    last = block == 15
    extra_src = jnp.logical_and(core == 1, block != 15)
    sibling = chip * 2 + (1 - core)

    def device(y, dx):
        return y * 8 + lax.rem(xc + dx + 4, 4) * 2 + core

    right, left, across = device(yl, 1), device(yl, -1), device(1 - yl, 0)

    def copy(src, dst, ssem, rsem, to_dp, to_mp):
        return pltpu.make_async_remote_copy(
            src_ref=src, dst_ref=dst, send_sem=ssem, recv_sem=rsem,
            device_id={"dp": to_dp, "mp": to_mp}, device_id_type=MESH,
        )

    def got(ref, rsem):
        copy(ref, ref, s_half.at[0], rsem, dp, sibling).wait_recv()

    def sent(ref, ssem):
        copy(ref, ref, ssem, r_half.at[0], dp, sibling).wait_send()

    def loop(lo, hi, body):
        def step(k, carry):
            body(k)
            return carry

        lax.fori_loop(lo, hi, step, 0)

    loads = [
        pltpu.make_async_copy(src.at[layer], dst.at[layer], ck_sem.at[n])
        for n, (src, dst, layer) in enumerate(
            ((up_hbm, up_ck, 0), (down_hbm, down_ck, 0), (up_hbm, up_ck, 1), (down_hbm, down_ck, 1))
        )
    ]
    tok_load, norm_load, up_b_load, cet_load, down_b_load, final_load, proj_load = (
        pltpu.make_async_copy(src, dst, ck_sem.at[4 + n])
        for n, (src, dst) in enumerate(
            (
                (tok_hbm, tok), (norm_hbm, norm_g), (up_b_hbm, up_b), (cet_hbm, cet),
                (down_b_hbm, down_b), (final_hbm, final_gain), (proj_hbm, proj),
            )
        )
    )
    tok_load.start()
    for load in loads:
        load.start()
    for load in (norm_load, up_b_load, cet_load, down_b_load, final_load, proj_load):
        load.start()

    state[64:80, :] = jnp.zeros((16, D), F32)
    worker = jnp.logical_and(core == 0, chip < WORKERS)

    @pl.when(chip == WORKERS - 1)
    def _():
        cls[1] = jnp.zeros((16, EMBB, 128), BF16)

    barrier = pltpu.get_barrier_semaphore()

    def greet(k):
        pl.semaphore_signal(
            barrier, inc=1, device_id={"dp": dp, "mp": lax.rem(mp + k, 16)}, device_id_type=MESH
        )
        pl.semaphore_signal(
            barrier, inc=1, device_id={"dp": lax.rem(dp + k, 16), "mp": mp}, device_id_type=MESH
        )

    loop(1, 16, greet)

    mask_f = [mask[i].astype(F32) for i in range(CKPT)]
    total = mask_f[0]
    for i in range(1, CKPT):
        total = total + mask_f[i]
    total_v = jnp.full((1, 128), total, F32)
    share_v = [jnp.full((1, 128), v, F32) / total_v for v in mask_f]

    def soup_vec(ref, layer, width):
        acc = jnp.zeros((1, width), F32)
        for i in range(CKPT):
            acc = acc + jnp.tile(share_v[i], (1, width // 128)) * ref[i, layer : layer + 1, :]
        return acc

    def soup(ref, layer, cs):
        acc = jnp.zeros((DB, 128), F32)
        for i in range(CKPT):
            acc = acc + share_v[i] * ref[layer, i, :, 128 * cs : 128 * cs + 128].astype(F32)
        return acc

    def own_shard(t, ref, layer):
        loads[t].wait()
        for h in range(2):
            both = jnp.concatenate([soup(ref, layer, h), soup(ref, layer, 2 + h)], axis=0)
            gath[t, dp, :, 128 * h : 128 * h + 128] = both.astype(BF16)

    z_next, z_prev = yh * 8 + lax.rem(z + 1, 8), yh * 8 + lax.rem(z + 7, 8)

    def slot(which_yh, shift):
        return which_yh * 8 + lax.rem(z + shift + 8, 8)

    def ring_push(t, s, n, to):
        copy(gath.at[t, s], gath.at[t, s], s_ring.at[t, n], r_ring.at[t, n], to, mp).start()

    def ring_got(t, s, n):
        got(gath.at[t, s], r_ring.at[t, n])

    def ring(t, step):
        if step == 9:
            ring_push(t, dp, 14, other_yh * 8 + z)
        elif step == 0:
            ring_push(t, dp, 0, z_next)
            ring_push(t, dp, 7, z_prev)
        elif step == 1:
            s = slot(other_yh, 0)
            ring_got(t, s, 14)
            ring_push(t, s, 1, z_next)
            ring_push(t, s, 8, z_prev)
        elif step < 8:
            n = step - 2
            dist = n // 2 + 1
            which = yh if n % 2 == 0 else other_yh
            sl, sr = slot(which, -dist), slot(which, dist)
            ring_got(t, sl, n)
            if n < 5:
                ring_push(t, sl, n + 2, z_next)
            ring_got(t, sr, 7 + n)
            if n < 4:
                ring_push(t, sr, 7 + n + 2, z_prev)
            elif n == 5:
                ring_push(t, sr, 7 + 6, z_prev)
        else:
            ring_got(t, slot(yh, 4), 6)
            ring_got(t, slot(other_yh, 4), 13)

    def far_across(t, k):
        s = slot(yh, FAR[k])
        copy(
            gath.at[t, s], gath.at[t, s], s_far.at[k], r_far.at[k], other_yh * 8 + z, mp
        ).start()

    def far_ring(t, step):
        if step == 0:
            ring_push(t, dp, 0, z_next)
            ring_push(t, dp, 7, z_prev)
        elif step == 9:
            far_across(t, 0)
        elif step < 4:
            sl, sr = slot(yh, -step), slot(yh, step)
            ring_got(t, sl, step - 1)
            ring_push(t, sl, step, z_next)
            ring_got(t, sr, 7 + step - 1)
            if step < 3:
                ring_push(t, sr, 7 + step, z_prev)
            far_across(t, 2 * step - 1)
            far_across(t, 2 * step)
        elif step == 4:
            ring_got(t, slot(yh, 4), 3)
            far_across(t, 7)
        else:
            for k in range(8):
                got(gath.at[t, slot(other_yh, FAR[k])], r_far.at[k])

    def compact(t, dst):
        def pair(j):
            g0 = gath[t, 2 * j].astype(F32)
            g1 = gath[t, 2 * j + 1].astype(F32)
            rows = pl.ds(pl.multiple_of(208 * j, 16), 208)
            dst[rows, 0:256] = jnp.concatenate([g0[:DB], g1[:DB]], axis=0).astype(BF16)
            dst[rows, 256:512] = jnp.concatenate([g0[DB:], g1[DB:]], axis=0).astype(BF16)

        loop(0, 8, pair)

    def block_rows(c, dx, y):
        return pl.multiple_of(512 * c + 128 * lax.rem(xc + dx + 4, 4) + 64 * y, 16)

    def half_rows(x, c, idx, h):
        dx, other = PLACES[idx]
        y = 1 - yl if other else yl
        return x.at[pl.ds(block_rows(c, dx, y) + 32 * h, 32)]

    def ag_push(lay, x, idx_here, idx, h, to):
        rows = half_rows(x, core, idx_here, h)
        n = 2 * idx + h
        copy(rows, rows, s_ag.at[lay, n], r_ag.at[lay, n], dp, to).start()

    def ag_sib(lay, x, idx, h):
        rows = half_rows(x, core, idx, h)
        n = 2 * idx + h
        copy(rows, rows, s_sb.at[lay, n], r_sb.at[lay, n], dp, sibling).start()

    def ag_start(lay, x, h):
        ag_push(lay, x, 7, 0, h, right)
        ag_push(lay, x, 7, 1, h, left)
        ag_push(lay, x, 7, 2, h, across)
        ag_sib(lay, x, 7, h)

    def ag_start_extra(lay, x):
        extra = x.at[pl.ds(1024, 16)]

        @pl.when(last)
        def _():
            def push_extra(k):
                copy(
                    extra, extra, s_ex.at[lay, k], r_ex.at[lay], dp, lax.rem(chip + k, 8) * 2 + core
                ).start()

            loop(1, 8, push_extra)
            copy(extra, extra, s_sb.at[lay, 16], r_sb.at[lay, 16], dp, sibling).start()

    def ag_recv(lay, x, idx, h):
        got(half_rows(x, core, idx, h), r_ag.at[lay, 2 * idx + h])
        by_y = lay == 1 and h == 1
        if idx == 0:
            ag_push(lay, x, 0, 5, h, right)
            if by_y:
                ag_push(lay, x, 0, 3, h, across)
        elif idx == 1 and by_y:
            ag_push(lay, x, 1, 4, h, across)
        elif idx == 2 and not by_y:
            ag_push(lay, x, 2, 3, h, right)
            ag_push(lay, x, 2, 4, h, left)
        elif idx == 4:
            ag_push(lay, x, 4, 6, h, left)
        ag_sib(lay, x, idx, h)

    def ag_extra(lay, x):
        extra = x.at[pl.ds(1024, 16)]

        @pl.when(extra_src)
        def _():
            got(extra, r_ex.at[lay])
            copy(extra, extra, s_sb.at[lay, 16], r_sb.at[lay, 16], dp, sibling).start()

    def ag_finish(lay, x):
        for idx in range(8):
            for h in range(2):
                got(half_rows(x, 1 - core, idx, h), r_sb.at[lay, 2 * idx + h])

        @pl.when(core == 0)
        def _():
            got(x.at[pl.ds(1024, 16)], r_sb.at[lay, 16])

    def ag_sent(lay, x):
        rows = x.at[pl.ds(0, 32)]
        extra = x.at[pl.ds(1024, 16)]
        loop(0, 14, lambda n: sent(rows, s_ag.at[lay, n]))
        loop(0, 16, lambda n: sent(rows, s_sb.at[lay, n]))

        @pl.when(last)
        def _():
            loop(1, 8, lambda k: sent(extra, s_ex.at[lay, k]))

        @pl.when(core == 1)
        def _():
            sent(extra, s_sb.at[lay, 16])

    def normed_rows(x, gain):
        rows = layer_norm(state[...], gain).astype(BF16)
        x[pl.ds(block_rows(core, 0, yl), 64), :] = rows[:64]

        @pl.when(last)
        def _():
            x[1024:1040, :] = rows[64:]

    def up_chunk(x, w, bias, ch):
        rows = pl.ds(CHUNK * ch, CHUNK)
        return gelu(jnp.dot(x[rows, :], w[...], preferred_element_type=F32) + bias).astype(BF16)

    def down_product(rows):
        return lax.dot_general(
            rows, w_dn1[...], (((1,), (1,)), ((), ())), preferred_element_type=F32
        )

    def rs_rows(o, y, h):
        return t_own.at[o, pl.ds(pl.multiple_of(64 * y + 32 * h, 16), 32)]

    def rs_push(o, y, kind, h, to):
        n = 2 * kind + h
        copy(rs_rows(o, y, h), red.at[kind, h], s_rs.at[n], r_rs.at[n], dp, to).start()

    def rs_add(o, y, h, *kinds):
        rows = rs_rows(o, y, h)
        acc = rows[...].astype(F32)
        for kind in kinds:
            got(red.at[kind, h], r_rs.at[2 * kind + h])
            acc = acc + red[kind, h].astype(F32)
        rows[...] = acc.astype(BF16)

    own_shard(UP1, up_ck, 0)
    tok_load.wait()
    pl.semaphore_wait(barrier, 30)

    def send_tokens(k):
        m2 = lax.rem(mp + k, 16)
        b2 = lax.rem(m2, 2) * 8 + lax.rem(lax.div(m2, 2), 4) * 2 + lax.div(m2, 8)
        src = tok.at[pl.ds(16 * b2, 17)]
        copy(src, a2a.at[mp], s_a2a.at[k], r_a2a.at[k], dp, m2).start()

    loop(1, 16, send_tokens)
    ring(UP1, 9)
    ring(UP1, 0)
    a2a[mp] = tok[pl.ds(16 * block, 17)]
    own_shard(DOWN1, down_ck, 0)
    far_ring(DOWN1, 0)
    norm_load.wait()
    gain1 = soup_vec(norm_g, 0, D)

    def wait_tokens(k):
        got(a2a.at[lax.rem(mp + 16 - k, 16)], r_a2a.at[k])

    loop(1, 16, wait_tokens)
    for j in range(16):
        state[:68, DB * j : DB * j + DB] = a2a[j].astype(F32).reshape(68, DB)
    normed_rows(x1, gain1)
    ag_start(0, x1, 0)
    ag_start(0, x1, 1)
    ag_start_extra(0, x1)
    ring(UP1, 1)
    far_ring(DOWN1, 9)
    ring(UP1, 2)
    own_shard(UP2, up_ck, 1)
    own_shard(DOWN2, down_ck, 1)
    ring(UP1, 3)
    for idx in range(3):
        ag_recv(0, x1, idx, 0)
    ring(UP1, 4)
    far_ring(DOWN1, 1)
    for idx in range(3):
        ag_recv(0, x1, idx, 1)
    ring(UP1, 5)
    ag_recv(0, x1, 3, 0)
    ag_recv(0, x1, 4, 0)
    far_ring(DOWN1, 2)
    ring(UP1, 6)
    ag_recv(0, x1, 5, 0)
    ag_recv(0, x1, 3, 1)
    ag_recv(0, x1, 4, 1)
    ring(UP1, 7)
    far_ring(DOWN1, 3)
    ag_recv(0, x1, 5, 1)
    ag_recv(0, x1, 6, 0)
    ag_recv(0, x1, 6, 1)
    ag_extra(0, x1)
    ring(UP1, 8)
    far_ring(DOWN1, 4)
    ring(UP2, 0)
    compact(UP1, w_up1)
    up_b_load.wait()
    bias_up1 = soup_vec(up_b, 0, FFB)
    ag_finish(0, x1)
    for ch in range(5):
        hid[CHUNK * ch : CHUNK * ch + CHUNK, :] = up_chunk(x1, w_up1, bias_up1, ch)

    def send_cls(k):
        to = lax.div(k, 2) * 2
        src = cet.at[:, pl.ds(pl.multiple_of(128 * k, 128), 128)]
        n = lax.rem(k, 2)

        @pl.when(to != mp)
        def _():
            copy(src, cls.at[n, mp], s_cl.at[k], r_cl.at[n, mp], dp, to).start()

        @pl.when(to == mp)
        def _():
            cls[n, mp] = cet[:, pl.ds(pl.multiple_of(128 * k, 128), 128)]

    cet_load.wait()
    loop(0, CLS_BLOCKS, send_cls)
    down_b_load.wait()
    gain2 = soup_vec(norm_g, 1, D)
    bias_down1 = soup_vec(down_b, 0, D)
    bias_up2 = soup_vec(up_b, 1, FFB)
    bias_down2 = soup_vec(down_b, 1, D)
    ring(UP2, 9)
    far_ring(DOWN1, 5)
    ring(UP2, 2)
    compact(DOWN1, w_dn1)

    def chunk_product(o, c):
        lhs = hid[pl.ds(block_rows(c, STEPS[o], 0), 128), :]
        if STEPS[o] == 0:
            lhs = jnp.concatenate([lhs, hid[1024:1040, :]], axis=0)
        return down_product(lhs)

    def chunk_rows(o):
        return pl.ds(0, 144 if STEPS[o] == 0 else 128)

    def sib_chunk(o):
        p_sib[o, chunk_rows(o), :] = chunk_product(o, 1 - core).astype(BF16)

    def sib_send(o):
        rows = chunk_rows(o)
        copy(p_sib.at[o, rows], s_sib.at[o, rows], s_half.at[o], r_half.at[o], dp, sibling).start()

    def own_chunk(o):
        rows = chunk_rows(o)
        term = chunk_product(o, core)
        got(s_sib.at[o, rows], r_half.at[o])
        t_own[o, rows, :] = (term + s_sib[o, rows, :].astype(F32)).astype(BF16)

    def finish_half(h):
        rs_add(3, yl, h, 4, 5, 6)
        part_rows = slice(32 * h, 32 * h + 32)
        new = state[part_rows, :] + bias_down1 + rs_rows(3, yl, h)[...].astype(F32)
        new = new.astype(BF16).astype(F32)
        state[part_rows, :] = new
        x2[pl.ds(block_rows(core, 0, yl) + 32 * h, 32), :] = layer_norm(new, gain2).astype(BF16)
        ag_start(1, x2, h)

    sib_chunk(0)
    sib_send(0)
    sib_chunk(1)
    ring(UP2, 1)
    own_chunk(0)
    for h in range(2):
        rs_push(0, yl, 0, h, left)
        rs_push(0, 1 - yl, 1, h, right)
    sib_send(1)
    sib_chunk(2)
    sib_send(2)
    own_chunk(1)
    rs_push(1, 1 - yl, 2, 0, left)
    rs_push(1, 1 - yl, 2, 1, left)
    ring(UP2, 4)
    ring(UP2, 3)
    sib_chunk(3)
    sib_send(3)
    own_chunk(2)
    for h in range(2):
        rs_add(2, 1 - yl, h, 1)
        rs_push(2, 1 - yl, 3, h, right)
    for h in range(2):
        rs_add(1, yl, h, 0)
        rs_push(1, yl, 4, h, left)
        rs_push(2, yl, 5, h, right)
    ring(UP2, 6)
    own_chunk(3)
    ring(UP2, 5)
    ring(DOWN2, 9)
    ring(DOWN2, 0)

    @pl.when(extra_src)
    def _():
        copy(
            t_own.at[3, pl.ds(128, 16)], extra_r.at[chip], s_ex.at[0, 0], r_ex.at[2 + chip], dp, 15
        ).start()

    rs_add(3, 1 - yl, 0, 3, 2)
    rs_push(3, 1 - yl, 6, 0, across)
    rs_add(3, 1 - yl, 1, 3, 2)
    rs_push(3, 1 - yl, 6, 1, across)
    ring(UP2, 7)
    finish_half(0)
    ring(DOWN2, 2)
    finish_half(1)

    @pl.when(last)
    def _():
        extra = t_own[3, 128:144, :].astype(F32)
        for q in range(7):
            got(extra_r.at[q], r_ex.at[2 + q])
            extra = extra + extra_r[q].astype(F32)
        extra = (state[64:80, :] + bias_down1 + extra).astype(BF16).astype(F32)
        state[64:80, :] = extra
        x2[1024:1040, :] = layer_norm(extra, gain2).astype(BF16)

    ag_start_extra(1, x2)

    row = lax.broadcasted_iota(jnp.int32, (16, OWN), 1)
    img = lax.broadcasted_iota(jnp.int32, (16, OWN), 0)
    inside = ((row & 3) == img) & (row < jnp.where(last, 68, 64))
    state_sum = jnp.dot(
        jnp.where(inside, 1.0, 0.0).astype(BF16), state[...].astype(BF16), preferred_element_type=F32
    )[:8]
    hsum = jnp.zeros((16, FFB), F32)

    def pair_sum(c, dx, idxs, with_extra=False):
        if c is not core:
            for idx in idxs:
                for h in range(2):
                    got(half_rows(x2, 1 - core, idx, h), r_sb.at[1, 2 * idx + h])
        x = x2[pl.ds(block_rows(c, dx, 0), 128), :]
        size = 128
        if with_extra:
            x = jnp.concatenate([x, x2[1024:1040, :]], axis=0)
            size = 144
        h = gelu(jnp.dot(x, w_up2[...], preferred_element_type=F32) + bias_up2).astype(BF16)
        row = lax.broadcasted_iota(jnp.int32, (16, size), 1)
        img = lax.broadcasted_iota(jnp.int32, (16, size), 0)
        inside = ((row & 3) == img) & (row < 132)
        return jnp.dot(jnp.where(inside, 1.0, 0.0).astype(BF16), h, preferred_element_type=F32)

    other = 1 - core
    ring(DOWN2, 1)
    ring(UP2, 8)
    compact(UP2, w_up2)
    for idx in range(3):
        ag_recv(1, x2, idx, 0)
    ring(DOWN2, 4)
    for idx in range(3):
        ag_recv(1, x2, idx, 1)
    ring(DOWN2, 3)
    hsum = hsum + pair_sum(core, 0, (7, 2))
    ring(DOWN2, 6)
    ag_recv(1, x2, 3, 0)
    ag_recv(1, x2, 4, 0)
    ag_recv(1, x2, 5, 0)
    ring(DOWN2, 5)
    ag_recv(1, x2, 3, 1)
    ag_recv(1, x2, 4, 1)
    hsum = hsum + pair_sum(core, -1, (0, 3))
    hsum = hsum + pair_sum(other, 0, (7, 2))
    ring(DOWN2, 7)
    ag_recv(1, x2, 6, 0)
    ag_recv(1, x2, 5, 1)
    hsum = hsum + pair_sum(core, 1, (1, 4))
    ag_recv(1, x2, 6, 1)
    ag_extra(1, x2)
    hsum = hsum + pair_sum(other, -1, (0, 3))
    hsum = hsum + pair_sum(core, 2, (5, 6))
    ring(DOWN2, 8)
    compact(DOWN2, w_dn2)
    hsum = hsum + pair_sum(other, 1, (1, 4))

    @pl.when(core == 0)
    def _():
        got(x2.at[pl.ds(1024, 16)], r_sb.at[1, 16])

    hsum = hsum + pair_sum(other, 2, (5, 6), True)

    hmean = hsum[:8] * (1.0 / TOKS)
    high = hmean.astype(BF16)
    low = (hmean - high.astype(F32)).astype(BF16)
    both = lax.dot_general(
        jnp.concatenate([high.astype(F32), low.astype(F32)], axis=0).astype(BF16), w_dn2[...],
        (((1,), (1,)), ((), ())), preferred_element_type=F32,
    )
    partial = both[:8] + both[8:] + state_sum * (1.0 / TOKS)
    pair[mp] = partial[:4].astype(BF16)

    def send_pair(q):
        @pl.when(2 * q != mp)
        def _():
            copy(pair.at[mp], pair.at[mp], s_pr.at[q], r_pr.at[mp], dp, 2 * q).start()

    loop(0, WORKERS, send_pair)
    final_load.wait()
    proj_load.wait()

    @pl.when(worker)
    def _():
        def wait_pair(k):
            @pl.when(k != mp)
            def _():
                got(pair.at[k], r_pr.at[k])

        loop(0, 16, wait_pair)
        pooled = pair[0].astype(F32)
        for k in range(1, 16):
            pooled = pooled + pair[k].astype(F32)
        pooled = (pooled + bias_down2).astype(BF16).astype(F32)
        pooled = jnp.concatenate([pooled, jnp.zeros_like(pooled)], axis=0)
        normed = layer_norm(pooled, final_gain[...].reshape(1, D))
        normed = jnp.concatenate([normed, jnp.zeros_like(normed)], axis=0).astype(BF16)
        embedding = jnp.dot(normed, proj[...], preferred_element_type=F32)[:8]
        unit = embedding * lax.rsqrt(jnp.sum(embedding * embedding, axis=1, keepdims=True) + 1e-06)
        unit_m[dp] = unit[:4].astype(BF16)

        def send_unit(k):
            mine = unit_m.at[dp]
            copy(mine, mine, s_un.at[k], r_un.at[k], lax.rem(dp + k, 16), mp).start()

        loop(1, 16, send_unit)

    loop(1, 16, lambda k: sent(tok.at[pl.ds(0, 17)], s_a2a.at[k]))

    def sent_ring(t):
        def step(n):
            sent(gath.at[t, 0], s_ring.at[t, n])

        loop(0, 15, step)

    for t in (UP1, UP2, DOWN2):
        sent_ring(t)
    loop(0, 4, lambda n: sent(gath.at[0, 0], s_ring.at[DOWN1, n]))
    loop(7, 10, lambda n: sent(gath.at[0, 0], s_ring.at[DOWN1, n]))
    loop(0, 8, lambda n: sent(gath.at[0, 0], s_far.at[n]))
    ag_sent(0, x1)
    ag_sent(1, x2)
    for o in range(4):
        sent(p_sib.at[o, pl.ds(0, 144 if o == 3 else 128)], s_half.at[o])
    loop(0, 14, lambda n: sent(red.at[0, 0], s_rs.at[n]))

    @pl.when(extra_src)
    def _():
        sent(extra_r.at[0], s_ex.at[0, 0])

    def sent_cls(k):
        @pl.when(lax.div(k, 2) * 2 != mp)
        def _():
            sent(cls.at[0, 0], s_cl.at[k])

    loop(0, CLS_BLOCKS, sent_cls)

    def sent_pair(q):
        @pl.when(2 * q != mp)
        def _():
            sent(pair.at[0], s_pr.at[q])

    loop(0, WORKERS, sent_pair)

    def ob_forward(k):
        copy(ob.at[k], ob.at[k], s_os.at[k], r_os.at[k], dp, sibling).start()

    @pl.when(worker)
    def _():
        def wait_cls(k):
            @pl.when(k != mp)
            def _():
                got(cls.at[0, k], r_cl.at[0, k])

                @pl.when(chip < WORKERS - 1)
                def _():
                    got(cls.at[1, k], r_cl.at[1, k])

        loop(0, 16, wait_cls)
        rhs = jnp.concatenate(
            [jnp.concatenate([cls[n, k] for k in range(16)], axis=0) for n in range(2)], axis=1
        )
        loop(1, 16, lambda k: got(unit_m.at[lax.rem(dp + 16 - k, 16)], r_un.at[k]))
        lhs = unit_m[...].astype(F32).reshape(64, EMB).astype(BF16)
        scores = jnp.dot(lhs, rhs, preferred_element_type=F32) * 100.0
        lg[...] = scores.reshape(16, 4, 256)
        lr[dp] = lg[dp]

        def send_logits(k):
            to = lax.rem(dp + k, 16)
            copy(lg.at[to], lr.at[dp], s_lg.at[k], r_lg.at[k], to, mp).start()

        loop(1, 16, send_logits)

        def wait_logits(k):
            got(lr.at[lax.rem(dp + 16 - k, 16)], r_lg.at[k])

        loop(1, 16, wait_logits)
        ob[chip] = lr[...].reshape(64, 256).astype(BF16)

        def send_ob(k):
            mine = ob.at[chip]
            copy(mine, mine, s_ob.at[k], r_ob.at[chip], dp, lax.rem(chip + k, 8) * 2).start()

        loop(1, 8, send_ob)
        ob_forward(chip)

    @pl.when(core == 0)
    def _():
        for k in range(WORKERS):
            @pl.when(chip != k)
            def _(k=k):
                got(ob.at[k], r_ob.at[k])
                ob_forward(k)

    @pl.when(core == 1)
    def _():
        for k in range(WORKERS):
            got(ob.at[k], r_os.at[k])

    ob_out[...] = ob[...]

    @pl.when(worker)
    def _():
        loop(1, 16, lambda k: sent(unit_m.at[0], s_un.at[k]))
        loop(1, 16, lambda k: sent(lg.at[0], s_lg.at[k]))
        loop(1, 8, lambda k: sent(ob.at[0], s_ob.at[k]))

    @pl.when(core == 0)
    def _():
        loop(0, WORKERS, lambda k: sent(ob.at[0], s_os.at[k]))


def finish(labels, ob, out, lab_out):
    found = jnp.zeros((4, 128), F32)
    lane = lax.broadcasted_iota(jnp.int32, (4, 128), 1)
    row = lax.broadcasted_iota(jnp.int32, (4, 128), 0)
    label = jnp.full((4, 128), labels[0], jnp.int32)
    for i in range(1, 4):
        label = jnp.where(row == i, labels[i], label)
    for k in range(CLS_BLOCKS):
        vals = ob[k // 2, :, 128 * (k % 2) : 128 * (k % 2) + 128].astype(F32)
        for g in range(16):
            first = (g * CLS_BLOCKS + k) * 128
            piece = vals[4 * g : 4 * g + 4]
            out[:, first : first + 128] = piece
            found = found + jnp.where(lane + first == label, piece, 0.0)
    for i in range(4):
        lab_out[i] = jnp.sum(found[i : i + 1])


def per_device(
    tokens, up_ckpts, up_bias_ckpts, down_ckpts, down_bias_ckpts, norm_ckpts, soup_mask,
    final_gain, projection, class_embed, labels,
):
    vm = pl.BlockSpec(memory_space=pltpu.VMEM)
    sm = pl.BlockSpec(memory_space=pltpu.SMEM)
    hbm = pl.BlockSpec(memory_space=pl.ANY)
    dma = pltpu.SemaphoreType.DMA
    scores = pl.pallas_call(
        kernel,
        out_shape=jax.ShapeDtypeStruct((WORKERS, 64, 256), BF16),
        in_specs=[sm] + [hbm] * 9,
        out_specs=vm,
        scratch_shapes=[
            pltpu.VMEM((2, CKPT, DB, FFB), BF16),
            pltpu.VMEM((2, CKPT, DB, FFB), BF16),
            pltpu.VMEM((TOKS, 4, DB), BF16),
            pltpu.VMEM((CKPT, 2, FFB), F32),
            pltpu.VMEM((CKPT, 2, D), F32),
            pltpu.VMEM((CKPT, 2, D), F32),
            pltpu.VMEM((D,), F32),
            pltpu.VMEM((EMBB, CLS_BLOCKS * 128), BF16),
            pltpu.VMEM((16, 17, 4, DB), BF16),
            pltpu.VMEM((OWN, D), F32),
            pltpu.VMEM((ROWS, D), BF16),
            pltpu.VMEM((ROWS, D), BF16),
            pltpu.VMEM((4, 16, 2 * DB, 256), BF16),
            pltpu.VMEM((D, FFB), BF16),
            pltpu.VMEM((D, FFB), BF16),
            pltpu.VMEM((D, FFB), BF16),
            pltpu.VMEM((D, FFB), BF16),
            pltpu.VMEM((ROWS, FFB), BF16),
            pltpu.VMEM((4, 144, D), BF16),
            pltpu.VMEM((4, 144, D), BF16),
            pltpu.VMEM((4, 144, D), BF16),
            pltpu.VMEM((7, 2, 32, D), BF16),
            pltpu.VMEM((8, 16, D), BF16),
            pltpu.VMEM((16, 4, D), BF16),
            pltpu.VMEM((D, EMB), BF16),
            pltpu.VMEM((16, 4, EMB), BF16),
            pltpu.VMEM((2, 16, EMBB, 128), BF16),
            pltpu.VMEM((16, 4, 256), F32),
            pltpu.VMEM((16, 4, 256), F32),
            pltpu.VMEM((WORKERS, 64, 256), BF16),
            dma((16,)), dma((16,)),
            dma((2, 14)), dma((2, 14)),
            dma((2, 17)), dma((2, 17)),
            dma((4, 15)), dma((4, 15)),
            dma((8,)), dma((8,)),
            dma((14,)), dma((14,)),
            dma((4,)), dma((4,)),
            dma((2, 8)), dma((10,)),
            dma((8,)), dma((16,)),
            dma((16,)), dma((2, 16)),
            dma((16,)), dma((16,)),
            dma((16,)), dma((16,)),
            dma((8,)), dma((8,)),
            dma((8,)), dma((8,)),
            dma((11,)),
        ],
        compiler_params=pltpu.CompilerParams(
            collective_id=0, has_side_effects=True, vmem_limit_bytes=60 * 2**20
        ),
    )(
        soup_mask, jnp.swapaxes(tokens, 0, 1), up_ckpts, jnp.swapaxes(down_ckpts, 2, 3),
        jnp.swapaxes(up_bias_ckpts, 0, 1), jnp.swapaxes(down_bias_ckpts, 0, 1),
        jnp.swapaxes(norm_ckpts, 0, 1), final_gain, projection, class_embed.T,
    )
    return pl.pallas_call(
        finish,
        out_shape=(
            jax.ShapeDtypeStruct((4, 16 * CLS_BLOCKS * 128), F32),
            jax.ShapeDtypeStruct((4,), F32),
        ),
        in_specs=[sm, vm],
        out_specs=(vm, sm),
    )(labels, scores)


def solution(mesh):
    placed = (
        P("dp", None, "mp"),
        P(None, None, "dp", "mp"),
        P(None, None, "mp"),
        P(None, None, "mp", "dp"),
        P(),
        P(),
        P(),
        P(),
        P(),
        P("dp", "mp"),
        P("dp"),
    )
    return jax.shard_map(
        per_device, mesh=mesh, in_specs=placed, out_specs=(P("dp", None), P("dp")), check_vma=False
    )
```

```python
import functools

import jax
import jax.numpy as jnp
from jax import lax
from jax.experimental import pallas as pl
from jax.experimental.pallas import tpu as pltpu
from jax.sharding import PartitionSpec as P

MESH = pl.DeviceIdType.MESH
F32 = jnp.float32
BF16 = jnp.bfloat16

CKPT = 10
D = 1664
DB = 104
FFB = 512
EMB = 1280
EMBB = 80
TOKS = 257
ROWS = 1040
OWN = 80
CHUNK = 208
CLS_BLOCKS = 11
WORKERS = 6
UP1, DOWN1, UP2, DOWN2 = 0, 1, 2, 3
PLACES = ((-1, 0), (1, 0), (0, 1), (-1, 1), (1, 1), (2, 0), (2, 1), (0, 0))
FAR = (0, -1, 1, -2, 2, -3, 3, 4)
STEPS = (2, -1, 1, 0)


def layer_norm(values, gain):
    center = values - jnp.mean(values, axis=-1, keepdims=True)
    spread = jnp.mean(center * center, axis=-1, keepdims=True)
    return center * lax.rsqrt(spread + 1e-05) * gain


def gelu(values):
    return 0.5 * values * (1.0 + lax.erf(values * 0.7071067811865476))


def kernel(
    mask, tok_hbm, up_hbm, down_hbm, up_b_hbm, down_b_hbm, norm_hbm, final_hbm, proj_hbm, cet_hbm,
    ob_out,
    up_ck, down_ck, tok, up_b, down_b, norm_g, final_gain, cet, a2a, state, x1, x2, gath, w_up1, w_dn1, w_up2, w_dn2, hid, p_sib, s_sib, t_own,
    red, extra_r, pair, proj, unit_m, cls, lg, lr, ob,
    s_a2a, r_a2a, s_ag, r_ag, s_sb, r_sb, s_ring, r_ring, s_far, r_far, s_rs, r_rs, s_half, r_half, s_ex, r_ex,
    s_pr, r_pr, s_cl, r_cl, s_un, r_un, s_lg, r_lg, s_ob, r_ob, s_os, r_os,
    ck_sem,
):
    dp = lax.axis_index("dp")
    mp = lax.axis_index("mp")
    yh, z = lax.div(dp, 8), lax.rem(dp, 8)
    core = lax.rem(mp, 2)
    chip = lax.div(mp, 2)
    yl, xc = lax.div(mp, 8), lax.rem(chip, 4)
    other_yh = 1 - yh
    block = core * 8 + xc * 2 + yl
    last = block == 15
    extra_src = jnp.logical_and(core == 1, block != 15)
    sibling = chip * 2 + (1 - core)

    def device(y, dx):
        return y * 8 + lax.rem(xc + dx + 4, 4) * 2 + core

    right, left, across = device(yl, 1), device(yl, -1), device(1 - yl, 0)

    def copy(src, dst, ssem, rsem, to_dp, to_mp):
        return pltpu.make_async_remote_copy(
            src_ref=src, dst_ref=dst, send_sem=ssem, recv_sem=rsem,
            device_id={"dp": to_dp, "mp": to_mp}, device_id_type=MESH,
        )

    def got(ref, rsem):
        copy(ref, ref, s_half.at[0], rsem, dp, sibling).wait_recv()

    def sent(ref, ssem):
        copy(ref, ref, ssem, r_half.at[0], dp, sibling).wait_send()

    def loop(lo, hi, body):
        def step(k, carry):
            body(k)
            return carry

        lax.fori_loop(lo, hi, step, 0)

    loads = [
        pltpu.make_async_copy(src.at[layer], dst.at[layer], ck_sem.at[n])
        for n, (src, dst, layer) in enumerate(
            ((up_hbm, up_ck, 0), (down_hbm, down_ck, 0), (up_hbm, up_ck, 1), (down_hbm, down_ck, 1))
        )
    ]
    tok_load, norm_load, up_b_load, cet_load, down_b_load, final_load, proj_load = (
        pltpu.make_async_copy(src, dst, ck_sem.at[4 + n])
        for n, (src, dst) in enumerate(
            (
                (tok_hbm, tok), (norm_hbm, norm_g), (up_b_hbm, up_b), (cet_hbm, cet),
                (down_b_hbm, down_b), (final_hbm, final_gain), (proj_hbm, proj),
            )
        )
    )
    tok_load.start()
    for load in loads:
        load.start()
    for load in (norm_load, up_b_load, cet_load, down_b_load, final_load, proj_load):
        load.start()

    state[64:80, :] = jnp.zeros((16, D), F32)
    worker = jnp.logical_and(core == 0, chip < WORKERS)

    @pl.when(chip == WORKERS - 1)
    def _():
        cls[1] = jnp.zeros((16, EMBB, 128), BF16)

    barrier = pltpu.get_barrier_semaphore()

    def greet(k):
        pl.semaphore_signal(
            barrier, inc=1, device_id={"dp": dp, "mp": lax.rem(mp + k, 16)}, device_id_type=MESH
        )
        pl.semaphore_signal(
            barrier, inc=1, device_id={"dp": lax.rem(dp + k, 16), "mp": mp}, device_id_type=MESH
        )

    loop(1, 16, greet)

    mask_f = [mask[i].astype(F32) for i in range(CKPT)]
    total = mask_f[0]
    for i in range(1, CKPT):
        total = total + mask_f[i]
    total_v = jnp.full((1, 128), total, F32)
    share_v = [jnp.full((1, 128), v, F32) / total_v for v in mask_f]

    def soup_vec(ref, layer, width):
        acc = jnp.zeros((1, width), F32)
        for i in range(CKPT):
            acc = acc + jnp.tile(share_v[i], (1, width // 128)) * ref[i, layer : layer + 1, :]
        return acc

    def soup(ref, layer, cs):
        acc = jnp.zeros((DB, 128), F32)
        for i in range(CKPT):
            acc = acc + share_v[i] * ref[layer, i, :, 128 * cs : 128 * cs + 128].astype(F32)
        return acc

    def own_shard(t, ref, layer):
        loads[t].wait()
        for h in range(2):
            both = jnp.concatenate([soup(ref, layer, h), soup(ref, layer, 2 + h)], axis=0)
            gath[t, dp, :, 128 * h : 128 * h + 128] = both.astype(BF16)

    z_next, z_prev = yh * 8 + lax.rem(z + 1, 8), yh * 8 + lax.rem(z + 7, 8)

    def slot(which_yh, shift):
        return which_yh * 8 + lax.rem(z + shift + 8, 8)

    def ring_push(t, s, n, to):
        copy(gath.at[t, s], gath.at[t, s], s_ring.at[t, n], r_ring.at[t, n], to, mp).start()

    def ring_got(t, s, n):
        got(gath.at[t, s], r_ring.at[t, n])

    def ring(t, step):
        if step == 9:
            ring_push(t, dp, 14, other_yh * 8 + z)
        elif step == 0:
            ring_push(t, dp, 0, z_next)
            ring_push(t, dp, 7, z_prev)
        elif step == 1:
            s = slot(other_yh, 0)
            ring_got(t, s, 14)
            ring_push(t, s, 1, z_next)
            ring_push(t, s, 8, z_prev)
        elif step < 8:
            n = step - 2
            dist = n // 2 + 1
            which = yh if n % 2 == 0 else other_yh
            sl, sr = slot(which, -dist), slot(which, dist)
            ring_got(t, sl, n)
            if n < 5:
                ring_push(t, sl, n + 2, z_next)
            ring_got(t, sr, 7 + n)
            if n < 4:
                ring_push(t, sr, 7 + n + 2, z_prev)
            elif n == 5:
                ring_push(t, sr, 7 + 6, z_prev)
        else:
            ring_got(t, slot(yh, 4), 6)
            ring_got(t, slot(other_yh, 4), 13)

    def far_across(t, k):
        s = slot(yh, FAR[k])
        copy(
            gath.at[t, s], gath.at[t, s], s_far.at[k], r_far.at[k], other_yh * 8 + z, mp
        ).start()

    def far_ring(t, step):
        if step == 0:
            ring_push(t, dp, 0, z_next)
            ring_push(t, dp, 7, z_prev)
        elif step == 9:
            far_across(t, 0)
        elif step < 4:
            sl, sr = slot(yh, -step), slot(yh, step)
            ring_got(t, sl, step - 1)
            if step < 3:
                ring_push(t, sl, step, z_next)
            else:
                rows = gath.at[t, sl, pl.ds(0, 112)]
                copy(rows, rows, s_ring.at[t, 3], r_ring.at[t, 3], z_next, mp).start()
            ring_got(t, sr, 7 + step - 1)
            if step < 3:
                ring_push(t, sr, 7 + step, z_prev)
            else:
                rows = gath.at[t, sr, pl.ds(112, 96)]
                copy(rows, rows, s_ring.at[t, 10], r_ring.at[t, 10], z_prev, mp).start()
            far_across(t, 2 * step - 1)
            far_across(t, 2 * step)
        elif step == 4:
            got(gath.at[t, slot(yh, 4), pl.ds(0, 112)], r_ring.at[t, 3])
            got(gath.at[t, slot(yh, 4), pl.ds(112, 96)], r_ring.at[t, 10])
            far_across(t, 7)
        else:
            for k in range(8):
                got(gath.at[t, slot(other_yh, FAR[k])], r_far.at[k])

    def compact(t, dst):
        def pair(j):
            g0 = gath[t, 2 * j].astype(F32)
            g1 = gath[t, 2 * j + 1].astype(F32)
            rows = pl.ds(pl.multiple_of(208 * j, 16), 208)
            dst[rows, 0:256] = jnp.concatenate([g0[:DB], g1[:DB]], axis=0).astype(BF16)
            dst[rows, 256:512] = jnp.concatenate([g0[DB:], g1[DB:]], axis=0).astype(BF16)

        loop(0, 8, pair)

    def block_rows(c, dx, y):
        return pl.multiple_of(512 * c + 128 * lax.rem(xc + dx + 4, 4) + 64 * y, 16)

    def half_rows(x, c, idx, h):
        dx, other = PLACES[idx]
        y = 1 - yl if other else yl
        return x.at[pl.ds(block_rows(c, dx, y) + 32 * h, 32)]

    def ag_push(lay, x, idx_here, idx, h, to):
        rows = half_rows(x, core, idx_here, h)
        n = 2 * idx + h
        copy(rows, rows, s_ag.at[lay, n], r_ag.at[lay, n], dp, to).start()

    def ag_sib(lay, x, idx, h):
        rows = half_rows(x, core, idx, h)
        n = 2 * idx + h
        copy(rows, rows, s_sb.at[lay, n], r_sb.at[lay, n], dp, sibling).start()

    def ag_start(lay, x, h):
        ag_push(lay, x, 7, 0, h, right)
        ag_push(lay, x, 7, 1, h, left)
        ag_push(lay, x, 7, 2, h, across)
        ag_sib(lay, x, 7, h)

    def ag_start_extra(lay, x):
        extra = x.at[pl.ds(1024, 16)]

        @pl.when(last)
        def _():
            def push_extra(k):
                copy(
                    extra, extra, s_ex.at[lay, k], r_ex.at[lay], dp, lax.rem(chip + k, 8) * 2 + core
                ).start()

            loop(1, 8, push_extra)
            copy(extra, extra, s_sb.at[lay, 16], r_sb.at[lay, 16], dp, sibling).start()

    def ag_recv(lay, x, idx, h):
        got(half_rows(x, core, idx, h), r_ag.at[lay, 2 * idx + h])
        by_y = lay == 1 and h == 1
        if idx == 0:
            ag_push(lay, x, 0, 5, h, right)
            if by_y:
                ag_push(lay, x, 0, 3, h, across)
        elif idx == 1 and by_y:
            ag_push(lay, x, 1, 4, h, across)
        elif idx == 2 and not by_y:
            ag_push(lay, x, 2, 3, h, right)
            ag_push(lay, x, 2, 4, h, left)
        elif idx == 4:
            ag_push(lay, x, 4, 6, h, left)
        ag_sib(lay, x, idx, h)

    def ag_extra(lay, x):
        extra = x.at[pl.ds(1024, 16)]

        @pl.when(extra_src)
        def _():
            got(extra, r_ex.at[lay])
            copy(extra, extra, s_sb.at[lay, 16], r_sb.at[lay, 16], dp, sibling).start()

    def ag_finish(lay, x):
        for idx in range(8):
            for h in range(2):
                got(half_rows(x, 1 - core, idx, h), r_sb.at[lay, 2 * idx + h])

        @pl.when(core == 0)
        def _():
            got(x.at[pl.ds(1024, 16)], r_sb.at[lay, 16])

    def ag_sent(lay, x):
        rows = x.at[pl.ds(0, 32)]
        extra = x.at[pl.ds(1024, 16)]
        loop(0, 14, lambda n: sent(rows, s_ag.at[lay, n]))
        loop(0, 16, lambda n: sent(rows, s_sb.at[lay, n]))

        @pl.when(last)
        def _():
            loop(1, 8, lambda k: sent(extra, s_ex.at[lay, k]))

        @pl.when(core == 1)
        def _():
            sent(extra, s_sb.at[lay, 16])

    def normed_rows(x, gain):
        rows = layer_norm(state[...], gain).astype(BF16)
        x[pl.ds(block_rows(core, 0, yl), 64), :] = rows[:64]

        @pl.when(last)
        def _():
            x[1024:1040, :] = rows[64:]

    def up_chunk(x, w, bias, ch):
        rows = pl.ds(CHUNK * ch, CHUNK)
        return gelu(jnp.dot(x[rows, :], w[...], preferred_element_type=F32) + bias).astype(BF16)

    def down_product(rows):
        return lax.dot_general(
            rows, w_dn1[...], (((1,), (1,)), ((), ())), preferred_element_type=F32
        )

    def rs_rows(o, y, h):
        return t_own.at[o, pl.ds(pl.multiple_of(64 * y + 32 * h, 16), 32)]

    def rs_push(o, y, kind, h, to):
        n = 2 * kind + h
        copy(rs_rows(o, y, h), red.at[kind, h], s_rs.at[n], r_rs.at[n], dp, to).start()

    def rs_add(o, y, h, *kinds):
        rows = rs_rows(o, y, h)
        acc = rows[...].astype(F32)
        for kind in kinds:
            got(red.at[kind, h], r_rs.at[2 * kind + h])
            acc = acc + red[kind, h].astype(F32)
        rows[...] = acc.astype(BF16)

    own_shard(UP1, up_ck, 0)
    tok_load.wait()
    pl.semaphore_wait(barrier, 30)

    def send_tokens(k):
        m2 = lax.rem(mp + k, 16)
        b2 = lax.rem(m2, 2) * 8 + lax.rem(lax.div(m2, 2), 4) * 2 + lax.div(m2, 8)
        src = tok.at[pl.ds(16 * b2, 17)]
        copy(src, a2a.at[mp], s_a2a.at[k], r_a2a.at[k], dp, m2).start()

    loop(1, 16, send_tokens)
    ring(UP1, 9)
    ring(UP1, 0)
    a2a[mp] = tok[pl.ds(16 * block, 17)]
    own_shard(DOWN1, down_ck, 0)
    far_ring(DOWN1, 0)
    norm_load.wait()
    gain1 = soup_vec(norm_g, 0, D)

    def wait_tokens(k):
        got(a2a.at[lax.rem(mp + 16 - k, 16)], r_a2a.at[k])

    loop(1, 16, wait_tokens)
    for j in range(16):
        state[:68, DB * j : DB * j + DB] = a2a[j].astype(F32).reshape(68, DB)
    normed_rows(x1, gain1)
    ag_start(0, x1, 0)
    ag_start(0, x1, 1)
    ag_start_extra(0, x1)
    ring(UP1, 1)
    far_ring(DOWN1, 9)
    ring(UP1, 2)
    own_shard(UP2, up_ck, 1)
    own_shard(DOWN2, down_ck, 1)
    far_ring(DOWN1, 1)
    ring(UP1, 3)
    for idx in range(3):
        ag_recv(0, x1, idx, 0)
    far_ring(DOWN1, 2)
    ring(UP1, 4)
    for idx in range(3):
        ag_recv(0, x1, idx, 1)
    ring(UP1, 5)
    ag_recv(0, x1, 3, 0)
    ag_recv(0, x1, 4, 0)
    far_ring(DOWN1, 3)
    ag_recv(0, x1, 5, 0)
    ag_recv(0, x1, 3, 1)
    ag_recv(0, x1, 4, 1)
    ring(UP1, 6)
    far_ring(DOWN1, 4)
    ag_recv(0, x1, 5, 1)
    ag_recv(0, x1, 6, 0)
    ag_recv(0, x1, 6, 1)
    ag_extra(0, x1)
    ring(UP1, 7)
    ring(UP2, 0)
    ring(UP1, 8)
    ring(UP2, 9)
    compact(UP1, w_up1)
    up_b_load.wait()
    bias_up1 = soup_vec(up_b, 0, FFB)
    ag_finish(0, x1)
    for ch in range(5):
        hid[CHUNK * ch : CHUNK * ch + CHUNK, :] = up_chunk(x1, w_up1, bias_up1, ch)

    def send_cls(k):
        to = lax.div(k, 2) * 2
        src = cet.at[:, pl.ds(pl.multiple_of(128 * k, 128), 128)]
        n = lax.rem(k, 2)

        @pl.when(to != mp)
        def _():
            copy(src, cls.at[n, mp], s_cl.at[k], r_cl.at[n, mp], dp, to).start()

        @pl.when(to == mp)
        def _():
            cls[n, mp] = cet[:, pl.ds(pl.multiple_of(128 * k, 128), 128)]

    cet_load.wait()
    loop(0, CLS_BLOCKS, send_cls)
    down_b_load.wait()
    gain2 = soup_vec(norm_g, 1, D)
    bias_down1 = soup_vec(down_b, 0, D)
    bias_up2 = soup_vec(up_b, 1, FFB)
    bias_down2 = soup_vec(down_b, 1, D)
    far_ring(DOWN1, 5)
    ring(UP2, 2)
    compact(DOWN1, w_dn1)

    def chunk_product(o, c):
        lhs = hid[pl.ds(block_rows(c, STEPS[o], 0), 128), :]
        if STEPS[o] == 0:
            lhs = jnp.concatenate([lhs, hid[1024:1040, :]], axis=0)
        return down_product(lhs)

    def chunk_rows(o):
        return pl.ds(0, 144 if STEPS[o] == 0 else 128)

    def sib_chunk(o):
        p_sib[o, chunk_rows(o), :] = chunk_product(o, 1 - core).astype(BF16)

    def sib_send(o):
        rows = chunk_rows(o)
        copy(p_sib.at[o, rows], s_sib.at[o, rows], s_half.at[o], r_half.at[o], dp, sibling).start()

    def own_chunk(o):
        rows = chunk_rows(o)
        term = chunk_product(o, core)
        got(s_sib.at[o, rows], r_half.at[o])
        t_own[o, rows, :] = (term + s_sib[o, rows, :].astype(F32)).astype(BF16)

    def finish_half(h):
        rs_add(3, yl, h, 4, 5, 6)
        part_rows = slice(32 * h, 32 * h + 32)
        new = state[part_rows, :] + bias_down1 + rs_rows(3, yl, h)[...].astype(F32)
        new = new.astype(BF16).astype(F32)
        state[part_rows, :] = new
        x2[pl.ds(block_rows(core, 0, yl) + 32 * h, 32), :] = layer_norm(new, gain2).astype(BF16)
        ag_start(1, x2, h)

    sib_chunk(0)
    sib_send(0)
    sib_chunk(1)
    own_chunk(0)
    for h in range(2):
        rs_push(0, yl, 0, h, left)
        rs_push(0, 1 - yl, 1, h, right)
    sib_send(1)
    sib_chunk(2)
    sib_send(2)
    ring(UP2, 1)
    own_chunk(1)
    rs_push(1, 1 - yl, 2, 0, left)
    rs_push(1, 1 - yl, 2, 1, left)
    ring(UP2, 4)
    ring(DOWN2, 9)
    ring(DOWN2, 0)
    sib_chunk(3)
    sib_send(3)
    own_chunk(2)
    for h in range(2):
        rs_add(2, 1 - yl, h, 1)
        rs_push(2, 1 - yl, 3, h, right)
    for h in range(2):
        rs_add(1, yl, h, 0)
        rs_push(1, yl, 4, h, left)
        rs_push(2, yl, 5, h, right)
    ring(UP2, 3)
    own_chunk(3)
    ring(UP2, 6)

    @pl.when(extra_src)
    def _():
        copy(
            t_own.at[3, pl.ds(128, 16)], extra_r.at[chip], s_ex.at[0, 0], r_ex.at[2 + chip], dp, 15
        ).start()

    rs_add(3, 1 - yl, 0, 3, 2)
    rs_push(3, 1 - yl, 6, 0, across)
    ring(DOWN2, 2)
    rs_add(3, 1 - yl, 1, 3, 2)
    rs_push(3, 1 - yl, 6, 1, across)
    ring(UP2, 5)
    ring(DOWN2, 1)
    finish_half(0)
    ring(DOWN2, 4)
    finish_half(1)
    ring(UP2, 7)

    @pl.when(last)
    def _():
        extra = t_own[3, 128:144, :].astype(F32)
        for q in range(7):
            got(extra_r.at[q], r_ex.at[2 + q])
            extra = extra + extra_r[q].astype(F32)
        extra = (state[64:80, :] + bias_down1 + extra).astype(BF16).astype(F32)
        state[64:80, :] = extra
        x2[1024:1040, :] = layer_norm(extra, gain2).astype(BF16)

    ag_start_extra(1, x2)

    row = lax.broadcasted_iota(jnp.int32, (16, OWN), 1)
    img = lax.broadcasted_iota(jnp.int32, (16, OWN), 0)
    inside = ((row & 3) == img) & (row < jnp.where(last, 68, 64))
    state_sum = jnp.dot(
        jnp.where(inside, 1.0, 0.0).astype(BF16), state[...].astype(BF16), preferred_element_type=F32
    )[:8]
    hsum = jnp.zeros((16, FFB), F32)

    def pair_sum(c, dx, idxs, with_extra=False):
        if c is not core:
            for idx in idxs:
                for h in range(2):
                    got(half_rows(x2, 1 - core, idx, h), r_sb.at[1, 2 * idx + h])
        x = x2[pl.ds(block_rows(c, dx, 0), 128), :]
        size = 128
        if with_extra:
            x = jnp.concatenate([x, x2[1024:1040, :]], axis=0)
            size = 144
        h = gelu(jnp.dot(x, w_up2[...], preferred_element_type=F32) + bias_up2).astype(BF16)
        row = lax.broadcasted_iota(jnp.int32, (16, size), 1)
        img = lax.broadcasted_iota(jnp.int32, (16, size), 0)
        inside = ((row & 3) == img) & (row < 132)
        return jnp.dot(jnp.where(inside, 1.0, 0.0).astype(BF16), h, preferred_element_type=F32)

    other = 1 - core
    for idx in range(3):
        ag_recv(1, x2, idx, 0)
    ring(DOWN2, 3)
    for idx in range(3):
        ag_recv(1, x2, idx, 1)
    ring(UP2, 8)
    compact(UP2, w_up2)
    ring(DOWN2, 6)
    ag_recv(1, x2, 3, 0)
    ag_recv(1, x2, 4, 0)
    ag_recv(1, x2, 5, 0)
    hsum = hsum + pair_sum(core, 0, (7, 2))
    ring(DOWN2, 5)
    ag_recv(1, x2, 3, 1)
    ag_recv(1, x2, 4, 1)
    ring(DOWN2, 7)
    hsum = hsum + pair_sum(core, -1, (0, 3))
    hsum = hsum + pair_sum(other, 0, (7, 2))
    ag_recv(1, x2, 6, 0)
    ag_recv(1, x2, 5, 1)
    hsum = hsum + pair_sum(core, 1, (1, 4))
    ag_recv(1, x2, 6, 1)
    ag_extra(1, x2)
    hsum = hsum + pair_sum(other, -1, (0, 3))
    hsum = hsum + pair_sum(core, 2, (5, 6))
    ring(DOWN2, 8)
    compact(DOWN2, w_dn2)
    hsum = hsum + pair_sum(other, 1, (1, 4))

    @pl.when(core == 0)
    def _():
        got(x2.at[pl.ds(1024, 16)], r_sb.at[1, 16])

    hsum = hsum + pair_sum(other, 2, (5, 6), True)

    hmean = hsum[:8] * (1.0 / TOKS)
    high = hmean.astype(BF16)
    low = (hmean - high.astype(F32)).astype(BF16)
    both = lax.dot_general(
        jnp.concatenate([high.astype(F32), low.astype(F32)], axis=0).astype(BF16), w_dn2[...],
        (((1,), (1,)), ((), ())), preferred_element_type=F32,
    )
    partial = both[:8] + both[8:] + state_sum * (1.0 / TOKS)
    pair[mp] = partial[:4].astype(BF16)

    def send_pair(q):
        @pl.when(2 * q != mp)
        def _():
            copy(pair.at[mp], pair.at[mp], s_pr.at[q], r_pr.at[mp], dp, 2 * q).start()

    loop(0, WORKERS, send_pair)
    final_load.wait()
    proj_load.wait()

    @pl.when(worker)
    def _():
        def wait_pair(k):
            @pl.when(k != mp)
            def _():
                got(pair.at[k], r_pr.at[k])

        loop(0, 16, wait_pair)
        pooled = pair[0].astype(F32)
        for k in range(1, 16):
            pooled = pooled + pair[k].astype(F32)
        pooled = (pooled + bias_down2).astype(BF16).astype(F32)
        pooled = jnp.concatenate([pooled, jnp.zeros_like(pooled)], axis=0)
        normed = layer_norm(pooled, final_gain[...].reshape(1, D))
        normed = jnp.concatenate([normed, jnp.zeros_like(normed)], axis=0).astype(BF16)
        embedding = jnp.dot(normed, proj[...], preferred_element_type=F32)[:8]
        unit = embedding * lax.rsqrt(jnp.sum(embedding * embedding, axis=1, keepdims=True) + 1e-06)
        unit_m[dp] = unit[:4].astype(BF16)

        def send_unit(k):
            mine = unit_m.at[dp]
            copy(mine, mine, s_un.at[k], r_un.at[k], lax.rem(dp + k, 16), mp).start()

        loop(1, 16, send_unit)

    loop(1, 16, lambda k: sent(tok.at[pl.ds(0, 17)], s_a2a.at[k]))

    def sent_ring(t):
        def step(n):
            sent(gath.at[t, 0], s_ring.at[t, n])

        loop(0, 15, step)

    for t in (UP1, UP2, DOWN2):
        sent_ring(t)
    loop(0, 3, lambda n: sent(gath.at[0, 0], s_ring.at[DOWN1, n]))
    sent(gath.at[0, 0, pl.ds(0, 112)], s_ring.at[DOWN1, 3])
    sent(gath.at[0, 0, pl.ds(0, 96)], s_ring.at[DOWN1, 10])
    loop(7, 10, lambda n: sent(gath.at[0, 0], s_ring.at[DOWN1, n]))
    loop(0, 8, lambda n: sent(gath.at[0, 0], s_far.at[n]))
    ag_sent(0, x1)
    ag_sent(1, x2)
    for o in range(4):
        sent(p_sib.at[o, pl.ds(0, 144 if o == 3 else 128)], s_half.at[o])
    loop(0, 14, lambda n: sent(red.at[0, 0], s_rs.at[n]))

    @pl.when(extra_src)
    def _():
        sent(extra_r.at[0], s_ex.at[0, 0])

    def sent_cls(k):
        @pl.when(lax.div(k, 2) * 2 != mp)
        def _():
            sent(cls.at[0, 0], s_cl.at[k])

    loop(0, CLS_BLOCKS, sent_cls)

    def sent_pair(q):
        @pl.when(2 * q != mp)
        def _():
            sent(pair.at[0], s_pr.at[q])

    loop(0, WORKERS, sent_pair)

    def ob_forward(k):
        copy(ob.at[k], ob.at[k], s_os.at[k], r_os.at[k], dp, sibling).start()

    @pl.when(worker)
    def _():
        def wait_cls(k):
            @pl.when(k != mp)
            def _():
                got(cls.at[0, k], r_cl.at[0, k])

                @pl.when(chip < WORKERS - 1)
                def _():
                    got(cls.at[1, k], r_cl.at[1, k])

        loop(0, 16, wait_cls)
        rhs = jnp.concatenate(
            [jnp.concatenate([cls[n, k] for k in range(16)], axis=0) for n in range(2)], axis=1
        )
        loop(1, 16, lambda k: got(unit_m.at[lax.rem(dp + 16 - k, 16)], r_un.at[k]))
        lhs = unit_m[...].astype(F32).reshape(64, EMB).astype(BF16)
        scores = jnp.dot(lhs, rhs, preferred_element_type=F32) * 100.0
        lg[...] = scores.reshape(16, 4, 256)
        lr[dp] = lg[dp]

        def send_logits(k):
            to = lax.rem(dp + k, 16)
            copy(lg.at[to], lr.at[dp], s_lg.at[k], r_lg.at[k], to, mp).start()

        loop(1, 16, send_logits)

        def wait_logits(k):
            got(lr.at[lax.rem(dp + 16 - k, 16)], r_lg.at[k])

        loop(1, 16, wait_logits)
        ob[chip] = lr[...].reshape(64, 256).astype(BF16)

        def send_ob(k):
            mine = ob.at[chip]
            copy(mine, mine, s_ob.at[k], r_ob.at[chip], dp, lax.rem(chip + k, 8) * 2).start()

        loop(1, 8, send_ob)
        ob_forward(chip)

    @pl.when(core == 0)
    def _():
        for k in range(WORKERS):
            @pl.when(chip != k)
            def _(k=k):
                got(ob.at[k], r_ob.at[k])
                ob_forward(k)

    @pl.when(core == 1)
    def _():
        for k in range(WORKERS):
            got(ob.at[k], r_os.at[k])

    ob_out[...] = ob[...]

    @pl.when(worker)
    def _():
        loop(1, 16, lambda k: sent(unit_m.at[0], s_un.at[k]))
        loop(1, 16, lambda k: sent(lg.at[0], s_lg.at[k]))
        loop(1, 8, lambda k: sent(ob.at[0], s_ob.at[k]))

    @pl.when(core == 0)
    def _():
        loop(0, WORKERS, lambda k: sent(ob.at[0], s_os.at[k]))


def finish(labels, ob, out, lab_out):
    found = jnp.zeros((4, 128), F32)
    lane = lax.broadcasted_iota(jnp.int32, (4, 128), 1)
    row = lax.broadcasted_iota(jnp.int32, (4, 128), 0)
    label = jnp.full((4, 128), labels[0], jnp.int32)
    for i in range(1, 4):
        label = jnp.where(row == i, labels[i], label)
    for k in range(CLS_BLOCKS):
        vals = ob[k // 2, :, 128 * (k % 2) : 128 * (k % 2) + 128].astype(F32)
        for g in range(16):
            first = (g * CLS_BLOCKS + k) * 128
            piece = vals[4 * g : 4 * g + 4]
            out[:, first : first + 128] = piece
            found = found + jnp.where(lane + first == label, piece, 0.0)
    for i in range(4):
        lab_out[i] = jnp.sum(found[i : i + 1])


def per_device(
    tokens, up_ckpts, up_bias_ckpts, down_ckpts, down_bias_ckpts, norm_ckpts, soup_mask,
    final_gain, projection, class_embed, labels,
):
    vm = pl.BlockSpec(memory_space=pltpu.VMEM)
    sm = pl.BlockSpec(memory_space=pltpu.SMEM)
    hbm = pl.BlockSpec(memory_space=pl.ANY)
    dma = pltpu.SemaphoreType.DMA
    scores = pl.pallas_call(
        kernel,
        out_shape=jax.ShapeDtypeStruct((WORKERS, 64, 256), BF16),
        in_specs=[sm] + [hbm] * 9,
        out_specs=vm,
        scratch_shapes=[
            pltpu.VMEM((2, CKPT, DB, FFB), BF16),
            pltpu.VMEM((2, CKPT, DB, FFB), BF16),
            pltpu.VMEM((TOKS, 4, DB), BF16),
            pltpu.VMEM((CKPT, 2, FFB), F32),
            pltpu.VMEM((CKPT, 2, D), F32),
            pltpu.VMEM((CKPT, 2, D), F32),
            pltpu.VMEM((D,), F32),
            pltpu.VMEM((EMBB, CLS_BLOCKS * 128), BF16),
            pltpu.VMEM((16, 17, 4, DB), BF16),
            pltpu.VMEM((OWN, D), F32),
            pltpu.VMEM((ROWS, D), BF16),
            pltpu.VMEM((ROWS, D), BF16),
            pltpu.VMEM((4, 16, 2 * DB, 256), BF16),
            pltpu.VMEM((D, FFB), BF16),
            pltpu.VMEM((D, FFB), BF16),
            pltpu.VMEM((D, FFB), BF16),
            pltpu.VMEM((D, FFB), BF16),
            pltpu.VMEM((ROWS, FFB), BF16),
            pltpu.VMEM((4, 144, D), BF16),
            pltpu.VMEM((4, 144, D), BF16),
            pltpu.VMEM((4, 144, D), BF16),
            pltpu.VMEM((7, 2, 32, D), BF16),
            pltpu.VMEM((8, 16, D), BF16),
            pltpu.VMEM((16, 4, D), BF16),
            pltpu.VMEM((D, EMB), BF16),
            pltpu.VMEM((16, 4, EMB), BF16),
            pltpu.VMEM((2, 16, EMBB, 128), BF16),
            pltpu.VMEM((16, 4, 256), F32),
            pltpu.VMEM((16, 4, 256), F32),
            pltpu.VMEM((WORKERS, 64, 256), BF16),
            dma((16,)), dma((16,)),
            dma((2, 14)), dma((2, 14)),
            dma((2, 17)), dma((2, 17)),
            dma((4, 15)), dma((4, 15)),
            dma((8,)), dma((8,)),
            dma((14,)), dma((14,)),
            dma((4,)), dma((4,)),
            dma((2, 8)), dma((10,)),
            dma((8,)), dma((16,)),
            dma((16,)), dma((2, 16)),
            dma((16,)), dma((16,)),
            dma((16,)), dma((16,)),
            dma((8,)), dma((8,)),
            dma((8,)), dma((8,)),
            dma((11,)),
        ],
        compiler_params=pltpu.CompilerParams(
            collective_id=0, has_side_effects=True, vmem_limit_bytes=60 * 2**20
        ),
    )(
        soup_mask, jnp.swapaxes(tokens, 0, 1), up_ckpts, jnp.swapaxes(down_ckpts, 2, 3),
        jnp.swapaxes(up_bias_ckpts, 0, 1), jnp.swapaxes(down_bias_ckpts, 0, 1),
        jnp.swapaxes(norm_ckpts, 0, 1), final_gain, projection, class_embed.T,
    )
    return pl.pallas_call(
        finish,
        out_shape=(
            jax.ShapeDtypeStruct((4, 16 * CLS_BLOCKS * 128), F32),
            jax.ShapeDtypeStruct((4,), F32),
        ),
        in_specs=[sm, vm],
        out_specs=(vm, sm),
    )(labels, scores)


def solution(mesh):
    placed = (
        P("dp", None, "mp"),
        P(None, None, "dp", "mp"),
        P(None, None, "mp"),
        P(None, None, "mp", "dp"),
        P(),
        P(),
        P(),
        P(),
        P(),
        P("dp", "mp"),
        P("dp"),
    )
    return jax.shard_map(
        per_device, mesh=mesh, in_specs=placed, out_specs=(P("dp", None), P("dp")), check_vma=False
    )
```

```python
import functools

import jax
import jax.numpy as jnp
from jax import lax
from jax.experimental import pallas as pl
from jax.experimental.pallas import tpu as pltpu
from jax.sharding import PartitionSpec as P

MESH = pl.DeviceIdType.MESH
F32 = jnp.float32
BF16 = jnp.bfloat16

CKPT = 10
D = 1664
DB = 104
FFB = 512
EMB = 1280
EMBB = 80
TOKS = 257
ROWS = 1040
OWN = 80
CHUNK = 208
CLS_BLOCKS = 11
WORKERS = 6
UP1, DOWN1, UP2, DOWN2 = 0, 1, 2, 3
PLACES = ((-1, 0), (1, 0), (0, 1), (-1, 1), (1, 1), (2, 0), (2, 1), (0, 0))
FAR = (0, -1, 1, -2, 2, -3, 3, 4)
STEPS = (2, -1, 1, 0)


def layer_norm(values, gain):
    center = values - jnp.mean(values, axis=-1, keepdims=True)
    spread = jnp.mean(center * center, axis=-1, keepdims=True)
    return center * lax.rsqrt(spread + 1e-05) * gain


def gelu(values):
    return 0.5 * values * (1.0 + lax.erf(values * 0.7071067811865476))


def kernel(
    mask, tok_hbm, up_hbm, down_hbm, up_b_hbm, down_b_hbm, norm_hbm, final_hbm, proj_hbm, cet_hbm,
    ob_out,
    up_ck, down_ck, tok, up_b, down_b, norm_g, final_gain, cet, a2a, state, x1, x2, gath, w_up1, w_dn1, w_up2, w_dn2, hid, p_sib, s_sib, t_own,
    red, extra_r, pair, proj, unit_m, cls, lg, lr, ob,
    s_a2a, r_a2a, s_ag, r_ag, s_sb, r_sb, s_ring, r_ring, s_far, r_far, s_rs, r_rs, s_half, r_half, s_ex, r_ex,
    s_pr, r_pr, s_cl, r_cl, s_un, r_un, s_lg, r_lg, s_ob, r_ob, s_os, r_os,
    ck_sem,
):
    dp = lax.axis_index("dp")
    mp = lax.axis_index("mp")
    yh, z = lax.div(dp, 8), lax.rem(dp, 8)
    core = lax.rem(mp, 2)
    chip = lax.div(mp, 2)
    yl, xc = lax.div(mp, 8), lax.rem(chip, 4)
    other_yh = 1 - yh
    block = core * 8 + xc * 2 + yl
    last = block == 15
    extra_src = jnp.logical_and(core == 1, block != 15)
    sibling = chip * 2 + (1 - core)

    def device(y, dx):
        return y * 8 + lax.rem(xc + dx + 4, 4) * 2 + core

    right, left, across = device(yl, 1), device(yl, -1), device(1 - yl, 0)

    def copy(src, dst, ssem, rsem, to_dp, to_mp):
        return pltpu.make_async_remote_copy(
            src_ref=src, dst_ref=dst, send_sem=ssem, recv_sem=rsem,
            device_id={"dp": to_dp, "mp": to_mp}, device_id_type=MESH,
        )

    def got(ref, rsem):
        copy(ref, ref, s_half.at[0], rsem, dp, sibling).wait_recv()

    def sent(ref, ssem):
        copy(ref, ref, ssem, r_half.at[0], dp, sibling).wait_send()

    def loop(lo, hi, body):
        def step(k, carry):
            body(k)
            return carry

        lax.fori_loop(lo, hi, step, 0)

    barrier = pltpu.get_barrier_semaphore()

    def greet(k):
        pl.semaphore_signal(
            barrier, inc=1, device_id={"dp": dp, "mp": lax.rem(mp + k, 16)}, device_id_type=MESH
        )
        pl.semaphore_signal(
            barrier, inc=1, device_id={"dp": lax.rem(dp + k, 16), "mp": mp}, device_id_type=MESH
        )

    loop(1, 16, greet)

    loads = [
        pltpu.make_async_copy(src.at[layer], dst.at[layer], ck_sem.at[n])
        for n, (src, dst, layer) in enumerate(
            ((up_hbm, up_ck, 0), (down_hbm, down_ck, 0), (up_hbm, up_ck, 1), (down_hbm, down_ck, 1))
        )
    ]
    tok_load, norm_load, up_b_load, cet_load, down_b_load, final_load, proj_load = (
        pltpu.make_async_copy(src, dst, ck_sem.at[4 + n])
        for n, (src, dst) in enumerate(
            (
                (tok_hbm, tok), (norm_hbm, norm_g), (up_b_hbm, up_b), (cet_hbm, cet),
                (down_b_hbm, down_b), (final_hbm, final_gain), (proj_hbm, proj),
            )
        )
    )
    loads[0].start()
    tok_load.start()
    for load in loads[1:]:
        load.start()
    for load in (norm_load, up_b_load, cet_load, down_b_load, final_load, proj_load):
        load.start()

    state[64:80, :] = jnp.zeros((16, D), F32)
    worker = jnp.logical_and(core == 0, chip < WORKERS)

    @pl.when(chip == WORKERS - 1)
    def _():
        cls[1] = jnp.zeros((16, EMBB, 128), BF16)

    mask_f = [mask[i].astype(F32) for i in range(CKPT)]
    total = mask_f[0]
    for i in range(1, CKPT):
        total = total + mask_f[i]
    total_v = jnp.full((1, 128), total, F32)
    share_v = [jnp.full((1, 128), v, F32) / total_v for v in mask_f]

    def soup_vec(ref, layer, width):
        acc = jnp.zeros((1, width), F32)
        for i in range(CKPT):
            acc = acc + jnp.tile(share_v[i], (1, width // 128)) * ref[i, layer : layer + 1, :]
        return acc

    def soup(ref, layer, cs):
        acc = jnp.zeros((DB, 128), F32)
        for i in range(CKPT):
            acc = acc + share_v[i] * ref[layer, i, :, 128 * cs : 128 * cs + 128].astype(F32)
        return acc

    def own_shard(t, ref, layer):
        loads[t].wait()
        for h in range(2):
            both = jnp.concatenate([soup(ref, layer, h), soup(ref, layer, 2 + h)], axis=0)
            gath[t, dp, :, 128 * h : 128 * h + 128] = both.astype(BF16)

    z_next, z_prev = yh * 8 + lax.rem(z + 1, 8), yh * 8 + lax.rem(z + 7, 8)

    def slot(which_yh, shift):
        return which_yh * 8 + lax.rem(z + shift + 8, 8)

    def ring_rows(t, s):
        return gath.at[t, s, pl.ds(0, 144)] if t == DOWN2 else gath.at[t, s]

    def ring_push(t, s, n, to):
        rows = ring_rows(t, s)
        copy(rows, rows, s_ring.at[t, n], r_ring.at[t, n], to, mp).start()

    def ring_got(t, s, n):
        got(ring_rows(t, s), r_ring.at[t, n])

    def ring(t, step):
        if step == 9:
            ring_push(t, dp, 14, other_yh * 8 + z)
        elif step == 0:
            ring_push(t, dp, 0, z_next)
            ring_push(t, dp, 7, z_prev)
        elif step == 1:
            s = slot(other_yh, 0)
            ring_got(t, s, 14)
            ring_push(t, s, 1, z_next)
            ring_push(t, s, 8, z_prev)
        elif step < 8:
            n = step - 2
            dist = n // 2 + 1
            which = yh if n % 2 == 0 else other_yh
            sl, sr = slot(which, -dist), slot(which, dist)
            ring_got(t, sl, n)
            if n < 5:
                ring_push(t, sl, n + 2, z_next)
            ring_got(t, sr, 7 + n)
            if n < 4:
                ring_push(t, sr, 7 + n + 2, z_prev)
            elif n == 5:
                ring_push(t, sr, 7 + 6, z_prev)
        else:
            ring_got(t, slot(yh, 4), 6)
            ring_got(t, slot(other_yh, 4), 13)

    def far_part(t):
        return (0, 208, 112) if t == DOWN1 else (144, 64, 32)

    def far_rows(t, s):
        first, size, _ = far_part(t)
        return gath.at[t, s, pl.ds(first, size)]

    def far_halves(t, s):
        first, size, half = far_part(t)
        return gath.at[t, s, pl.ds(first, half)], gath.at[t, s, pl.ds(first + half, size - half)]

    def far_across(t, k):
        rows = far_rows(t, slot(yh, FAR[k]))
        copy(rows, rows, s_far.at[t // 2, k], r_far.at[t // 2, k], other_yh * 8 + z, mp).start()

    def far_ring(t, step):
        f = 4 + t // 2

        def push(rows, n, to):
            copy(rows, rows, s_ring.at[f, n], r_ring.at[f, n], to, mp).start()

        if step == 0:
            push(far_rows(t, dp), 0, z_next)
            push(far_rows(t, dp), 7, z_prev)
        elif step == 9:
            far_across(t, 0)
        elif step < 4:
            sl, sr = slot(yh, -step), slot(yh, step)
            got(far_rows(t, sl), r_ring.at[f, step - 1])
            push(far_rows(t, sl) if step < 3 else far_halves(t, sl)[0], step, z_next)
            got(far_rows(t, sr), r_ring.at[f, 7 + step - 1])
            push(far_rows(t, sr) if step < 3 else far_halves(t, sr)[1], 7 + step, z_prev)
            far_across(t, 2 * step - 1)
            far_across(t, 2 * step)
        elif step == 4:
            first, second = far_halves(t, slot(yh, 4))
            got(first, r_ring.at[f, 3])
            got(second, r_ring.at[f, 10])
            far_across(t, 7)
        else:
            for k in range(8):
                got(far_rows(t, slot(other_yh, FAR[k])), r_far.at[t // 2, k])

    def far_sent(t):
        f = 4 + t // 2
        rows = far_rows(t, 0)
        loop(0, 3, lambda n: sent(rows, s_ring.at[f, n]))
        loop(7, 10, lambda n: sent(rows, s_ring.at[f, n]))
        first, second = far_halves(t, 0)
        sent(first, s_ring.at[f, 3])
        sent(second, s_ring.at[f, 10])
        loop(0, 8, lambda n: sent(rows, s_far.at[t // 2, n]))

    def compact(t, dst):
        def pair(j):
            g0 = gath[t, 2 * j].astype(F32)
            g1 = gath[t, 2 * j + 1].astype(F32)
            rows = pl.ds(pl.multiple_of(208 * j, 16), 208)
            dst[rows, 0:256] = jnp.concatenate([g0[:DB], g1[:DB]], axis=0).astype(BF16)
            dst[rows, 256:512] = jnp.concatenate([g0[DB:], g1[DB:]], axis=0).astype(BF16)

        loop(0, 8, pair)

    def block_rows(c, dx, y):
        return pl.multiple_of(512 * c + 128 * lax.rem(xc + dx + 4, 4) + 64 * y, 16)

    def half_rows(x, c, idx, h):
        dx, other = PLACES[idx]
        y = 1 - yl if other else yl
        return x.at[pl.ds(block_rows(c, dx, y) + 32 * h, 32)]

    def ag_push(lay, x, idx_here, idx, h, to):
        rows = half_rows(x, core, idx_here, h)
        n = 2 * idx + h
        copy(rows, rows, s_ag.at[lay, n], r_ag.at[lay, n], dp, to).start()

    def ag_sib(lay, x, idx, h):
        rows = half_rows(x, core, idx, h)
        n = 2 * idx + h
        copy(rows, rows, s_sb.at[lay, n], r_sb.at[lay, n], dp, sibling).start()

    def ag_start(lay, x, h):
        ag_push(lay, x, 7, 0, h, right)
        ag_push(lay, x, 7, 1, h, left)
        ag_push(lay, x, 7, 2, h, across)
        ag_sib(lay, x, 7, h)

    def ag_start_extra(lay, x):
        extra = x.at[pl.ds(1024, 16)]

        @pl.when(last)
        def _():
            def push_extra(k):
                copy(
                    extra, extra, s_ex.at[lay, k], r_ex.at[lay], dp, lax.rem(chip + k, 8) * 2 + core
                ).start()

            loop(1, 8, push_extra)
            copy(extra, extra, s_sb.at[lay, 16], r_sb.at[lay, 16], dp, sibling).start()

    def ag_recv(lay, x, idx, h):
        got(half_rows(x, core, idx, h), r_ag.at[lay, 2 * idx + h])
        by_y = lay == 1 and h == 1
        if idx == 0:
            ag_push(lay, x, 0, 5, h, right)
            if by_y:
                ag_push(lay, x, 0, 3, h, across)
        elif idx == 1 and by_y:
            ag_push(lay, x, 1, 4, h, across)
        elif idx == 2 and not by_y:
            ag_push(lay, x, 2, 3, h, right)
            ag_push(lay, x, 2, 4, h, left)
        elif idx == 4:
            ag_push(lay, x, 4, 6, h, left)
        ag_sib(lay, x, idx, h)

    def ag_extra(lay, x):
        extra = x.at[pl.ds(1024, 16)]

        @pl.when(extra_src)
        def _():
            got(extra, r_ex.at[lay])
            copy(extra, extra, s_sb.at[lay, 16], r_sb.at[lay, 16], dp, sibling).start()

    def ag_finish(lay, x):
        for idx in range(8):
            for h in range(2):
                got(half_rows(x, 1 - core, idx, h), r_sb.at[lay, 2 * idx + h])

        @pl.when(core == 0)
        def _():
            got(x.at[pl.ds(1024, 16)], r_sb.at[lay, 16])

    def ag_sent(lay, x):
        rows = x.at[pl.ds(0, 32)]
        extra = x.at[pl.ds(1024, 16)]
        loop(0, 14, lambda n: sent(rows, s_ag.at[lay, n]))
        loop(0, 16, lambda n: sent(rows, s_sb.at[lay, n]))

        @pl.when(last)
        def _():
            loop(1, 8, lambda k: sent(extra, s_ex.at[lay, k]))

        @pl.when(core == 1)
        def _():
            sent(extra, s_sb.at[lay, 16])

    def normed_rows(x, gain):
        rows = layer_norm(state[...], gain).astype(BF16)
        x[pl.ds(block_rows(core, 0, yl), 64), :] = rows[:64]

        @pl.when(last)
        def _():
            x[1024:1040, :] = rows[64:]

    def up_chunk(x, w, bias, ch):
        rows = pl.ds(CHUNK * ch, CHUNK)
        return gelu(jnp.dot(x[rows, :], w[...], preferred_element_type=F32) + bias).astype(BF16)

    def down_product(rows):
        return lax.dot_general(
            rows, w_dn1[...], (((1,), (1,)), ((), ())), preferred_element_type=F32
        )

    def rs_rows(o, y, h):
        return t_own.at[o, pl.ds(pl.multiple_of(64 * y + 32 * h, 16), 32)]

    def rs_push(o, y, kind, h, to):
        n = 2 * kind + h
        copy(rs_rows(o, y, h), red.at[kind, h], s_rs.at[n], r_rs.at[n], dp, to).start()

    def rs_add(o, y, h, *kinds):
        rows = rs_rows(o, y, h)
        acc = rows[...].astype(F32)
        for kind in kinds:
            got(red.at[kind, h], r_rs.at[2 * kind + h])
            acc = acc + red[kind, h].astype(F32)
        rows[...] = acc.astype(BF16)

    own_shard(UP1, up_ck, 0)
    tok_load.wait()
    pl.semaphore_wait(barrier, 30)

    def send_tokens(k):
        m2 = lax.rem(mp + k, 16)
        b2 = lax.rem(m2, 2) * 8 + lax.rem(lax.div(m2, 2), 4) * 2 + lax.div(m2, 8)
        src = tok.at[pl.ds(16 * b2, 17)]
        copy(src, a2a.at[mp], s_a2a.at[k], r_a2a.at[k], dp, m2).start()

    loop(1, 16, send_tokens)
    ring(UP1, 9)
    ring(UP1, 0)
    a2a[mp] = tok[pl.ds(16 * block, 17)]
    own_shard(DOWN1, down_ck, 0)
    far_ring(DOWN1, 0)
    norm_load.wait()
    gain1 = soup_vec(norm_g, 0, D)

    def wait_tokens(k):
        got(a2a.at[lax.rem(mp + 16 - k, 16)], r_a2a.at[k])

    loop(1, 16, wait_tokens)
    for j in range(16):
        state[:68, DB * j : DB * j + DB] = a2a[j].astype(F32).reshape(68, DB)
    normed_rows(x1, gain1)
    ag_start(0, x1, 0)
    ag_start(0, x1, 1)
    ag_start_extra(0, x1)
    ring(UP1, 1)
    far_ring(DOWN1, 9)
    ring(UP1, 2)
    own_shard(UP2, up_ck, 1)
    own_shard(DOWN2, down_ck, 1)
    far_ring(DOWN1, 1)
    ring(UP1, 3)
    for idx in range(3):
        ag_recv(0, x1, idx, 0)
    far_ring(DOWN1, 2)
    ring(UP1, 4)
    for idx in range(3):
        ag_recv(0, x1, idx, 1)
    ring(UP1, 5)
    ag_recv(0, x1, 3, 0)
    ag_recv(0, x1, 4, 0)
    far_ring(DOWN1, 3)
    ag_recv(0, x1, 5, 0)
    ag_recv(0, x1, 3, 1)
    ag_recv(0, x1, 4, 1)
    ring(UP1, 6)
    far_ring(DOWN1, 4)
    ag_recv(0, x1, 5, 1)
    ag_recv(0, x1, 6, 0)
    ag_recv(0, x1, 6, 1)
    ag_extra(0, x1)
    ring(UP1, 7)
    ring(UP2, 0)
    ring(UP1, 8)
    ring(UP2, 9)
    compact(UP1, w_up1)
    up_b_load.wait()
    bias_up1 = soup_vec(up_b, 0, FFB)
    ag_finish(0, x1)
    for ch in range(5):
        hid[CHUNK * ch : CHUNK * ch + CHUNK, :] = up_chunk(x1, w_up1, bias_up1, ch)

    def send_cls(k):
        to = lax.div(k, 2) * 2
        src = cet.at[:, pl.ds(pl.multiple_of(128 * k, 128), 128)]
        n = lax.rem(k, 2)

        @pl.when(to != mp)
        def _():
            copy(src, cls.at[n, mp], s_cl.at[k], r_cl.at[n, mp], dp, to).start()

        @pl.when(to == mp)
        def _():
            cls[n, mp] = cet[:, pl.ds(pl.multiple_of(128 * k, 128), 128)]

    cet_load.wait()
    loop(0, CLS_BLOCKS, send_cls)
    down_b_load.wait()
    gain2 = soup_vec(norm_g, 1, D)
    bias_down1 = soup_vec(down_b, 0, D)
    bias_up2 = soup_vec(up_b, 1, FFB)
    bias_down2 = soup_vec(down_b, 1, D)
    far_ring(DOWN1, 5)
    ring(UP2, 2)
    compact(DOWN1, w_dn1)

    def chunk_product(o, c):
        lhs = hid[pl.ds(block_rows(c, STEPS[o], 0), 128), :]
        if STEPS[o] == 0:
            lhs = jnp.concatenate([lhs, hid[1024:1040, :]], axis=0)
        return down_product(lhs)

    def chunk_rows(o):
        return pl.ds(0, 144 if STEPS[o] == 0 else 128)

    def sib_chunk(o):
        p_sib[o, chunk_rows(o), :] = chunk_product(o, 1 - core).astype(BF16)

    def sib_send(o):
        rows = chunk_rows(o)
        copy(p_sib.at[o, rows], s_sib.at[o, rows], s_half.at[o], r_half.at[o], dp, sibling).start()

    def own_chunk(o):
        rows = chunk_rows(o)
        term = chunk_product(o, core)
        got(s_sib.at[o, rows], r_half.at[o])
        t_own[o, rows, :] = (term + s_sib[o, rows, :].astype(F32)).astype(BF16)

    def finish_half(h):
        rs_add(3, yl, h, 4, 5, 6)
        part_rows = slice(32 * h, 32 * h + 32)
        new = state[part_rows, :] + bias_down1 + rs_rows(3, yl, h)[...].astype(F32)
        new = new.astype(BF16).astype(F32)
        state[part_rows, :] = new
        x2[pl.ds(block_rows(core, 0, yl) + 32 * h, 32), :] = layer_norm(new, gain2).astype(BF16)
        ag_start(1, x2, h)

    sib_chunk(0)
    sib_send(0)
    sib_chunk(1)
    own_chunk(0)
    for h in range(2):
        rs_push(0, yl, 0, h, left)
        rs_push(0, 1 - yl, 1, h, right)
    sib_send(1)
    far_ring(DOWN2, 0)
    far_ring(DOWN2, 9)
    sib_chunk(2)
    sib_send(2)
    ring(UP2, 1)
    own_chunk(1)
    rs_push(1, 1 - yl, 2, 0, left)
    rs_push(1, 1 - yl, 2, 1, left)
    ring(UP2, 4)
    ring(DOWN2, 9)
    ring(DOWN2, 0)
    sib_chunk(3)
    sib_send(3)
    own_chunk(2)
    for h in range(2):
        rs_add(2, 1 - yl, h, 1)
        rs_push(2, 1 - yl, 3, h, right)
    for h in range(2):
        rs_add(1, yl, h, 0)
        rs_push(1, yl, 4, h, left)
        rs_push(2, yl, 5, h, right)
    ring(UP2, 3)
    far_ring(DOWN2, 1)
    own_chunk(3)
    ring(UP2, 6)

    @pl.when(extra_src)
    def _():
        copy(
            t_own.at[3, pl.ds(128, 16)], extra_r.at[chip], s_ex.at[0, 0], r_ex.at[2 + chip], dp, 15
        ).start()

    rs_add(3, 1 - yl, 0, 3, 2)
    rs_push(3, 1 - yl, 6, 0, across)
    ring(DOWN2, 2)
    rs_add(3, 1 - yl, 1, 3, 2)
    rs_push(3, 1 - yl, 6, 1, across)
    ring(UP2, 5)
    ring(DOWN2, 1)
    far_ring(DOWN2, 2)
    finish_half(0)
    finish_half(1)
    ring(DOWN2, 4)
    ring(UP2, 7)

    @pl.when(last)
    def _():
        extra = t_own[3, 128:144, :].astype(F32)
        for q in range(7):
            got(extra_r.at[q], r_ex.at[2 + q])
            extra = extra + extra_r[q].astype(F32)
        extra = (state[64:80, :] + bias_down1 + extra).astype(BF16).astype(F32)
        state[64:80, :] = extra
        x2[1024:1040, :] = layer_norm(extra, gain2).astype(BF16)

    ag_start_extra(1, x2)

    row = lax.broadcasted_iota(jnp.int32, (16, OWN), 1)
    img = lax.broadcasted_iota(jnp.int32, (16, OWN), 0)
    inside = ((row & 3) == img) & (row < jnp.where(last, 68, 64))
    state_sum = jnp.dot(
        jnp.where(inside, 1.0, 0.0).astype(BF16), state[...].astype(BF16), preferred_element_type=F32
    )[:8]
    hsum = jnp.zeros((16, FFB), F32)

    def pair_sum(c, dx, idxs, with_extra=False):
        if c is not core:
            for idx in idxs:
                for h in range(2):
                    got(half_rows(x2, 1 - core, idx, h), r_sb.at[1, 2 * idx + h])
        x = x2[pl.ds(block_rows(c, dx, 0), 128), :]
        size = 128
        if with_extra:
            x = jnp.concatenate([x, x2[1024:1040, :]], axis=0)
            size = 144
        h = gelu(jnp.dot(x, w_up2[...], preferred_element_type=F32) + bias_up2).astype(BF16)
        row = lax.broadcasted_iota(jnp.int32, (16, size), 1)
        img = lax.broadcasted_iota(jnp.int32, (16, size), 0)
        inside = ((row & 3) == img) & (row < 132)
        return jnp.dot(jnp.where(inside, 1.0, 0.0).astype(BF16), h, preferred_element_type=F32)

    other = 1 - core
    for idx in range(3):
        ag_recv(1, x2, idx, 0)
    ring(DOWN2, 3)
    for idx in range(3):
        ag_recv(1, x2, idx, 1)
    far_ring(DOWN2, 3)
    ring(UP2, 8)
    compact(UP2, w_up2)
    ring(DOWN2, 6)
    ring(DOWN2, 5)
    ag_recv(1, x2, 3, 0)
    ag_recv(1, x2, 4, 0)
    ag_recv(1, x2, 5, 0)
    hsum = hsum + pair_sum(core, 0, (7, 2))
    ag_recv(1, x2, 3, 1)
    ag_recv(1, x2, 4, 1)
    far_ring(DOWN2, 4)
    ring(DOWN2, 7)
    hsum = hsum + pair_sum(core, -1, (0, 3))
    hsum = hsum + pair_sum(other, 0, (7, 2))
    ag_recv(1, x2, 6, 0)
    ag_recv(1, x2, 5, 1)
    hsum = hsum + pair_sum(core, 1, (1, 4))
    ag_recv(1, x2, 6, 1)
    ag_extra(1, x2)
    hsum = hsum + pair_sum(other, -1, (0, 3))
    hsum = hsum + pair_sum(core, 2, (5, 6))
    ring(DOWN2, 8)
    far_ring(DOWN2, 5)
    compact(DOWN2, w_dn2)
    hsum = hsum + pair_sum(other, 1, (1, 4))

    @pl.when(core == 0)
    def _():
        got(x2.at[pl.ds(1024, 16)], r_sb.at[1, 16])

    hsum = hsum + pair_sum(other, 2, (5, 6), True)

    hmean = hsum[:8] * (1.0 / TOKS)
    high = hmean.astype(BF16)
    low = (hmean - high.astype(F32)).astype(BF16)
    both = lax.dot_general(
        jnp.concatenate([high.astype(F32), low.astype(F32)], axis=0).astype(BF16), w_dn2[...],
        (((1,), (1,)), ((), ())), preferred_element_type=F32,
    )
    partial = both[:8] + both[8:] + state_sum * (1.0 / TOKS)
    pair[mp] = partial[:4].astype(BF16)

    def send_pair(q):
        @pl.when(2 * q != mp)
        def _():
            copy(pair.at[mp], pair.at[mp], s_pr.at[q], r_pr.at[mp], dp, 2 * q).start()

    loop(0, WORKERS, send_pair)
    final_load.wait()
    proj_load.wait()

    @pl.when(worker)
    def _():
        def wait_pair(k):
            @pl.when(k != mp)
            def _():
                got(pair.at[k], r_pr.at[k])

        loop(0, 16, wait_pair)
        pooled = pair[0].astype(F32)
        for k in range(1, 16):
            pooled = pooled + pair[k].astype(F32)
        pooled = (pooled + bias_down2).astype(BF16).astype(F32)
        pooled = jnp.concatenate([pooled, jnp.zeros_like(pooled)], axis=0)
        normed = layer_norm(pooled, final_gain[...].reshape(1, D))
        normed = jnp.concatenate([normed, jnp.zeros_like(normed)], axis=0).astype(BF16)
        embedding = jnp.dot(normed, proj[...], preferred_element_type=F32)[:8]
        unit = embedding * lax.rsqrt(jnp.sum(embedding * embedding, axis=1, keepdims=True) + 1e-06)
        unit_m[dp] = unit[:4].astype(BF16)

        def send_unit(k):
            mine = unit_m.at[dp]
            copy(mine, mine, s_un.at[k], r_un.at[k], lax.rem(dp + k, 16), mp).start()

        loop(1, 16, send_unit)

    loop(1, 16, lambda k: sent(tok.at[pl.ds(0, 17)], s_a2a.at[k]))

    for t in (UP1, UP2, DOWN2):
        loop(0, 15, lambda n, t=t: sent(ring_rows(t, 0), s_ring.at[t, n]))
    far_sent(DOWN1)
    far_sent(DOWN2)
    ag_sent(0, x1)
    ag_sent(1, x2)
    for o in range(4):
        sent(p_sib.at[o, pl.ds(0, 144 if o == 3 else 128)], s_half.at[o])
    loop(0, 14, lambda n: sent(red.at[0, 0], s_rs.at[n]))

    @pl.when(extra_src)
    def _():
        sent(extra_r.at[0], s_ex.at[0, 0])

    def sent_cls(k):
        @pl.when(lax.div(k, 2) * 2 != mp)
        def _():
            sent(cls.at[0, 0], s_cl.at[k])

    loop(0, CLS_BLOCKS, sent_cls)

    def sent_pair(q):
        @pl.when(2 * q != mp)
        def _():
            sent(pair.at[0], s_pr.at[q])

    loop(0, WORKERS, sent_pair)

    def ob_forward(k):
        copy(ob.at[k], ob.at[k], s_os.at[k], r_os.at[k], dp, sibling).start()

    @pl.when(worker)
    def _():
        def wait_cls(k):
            @pl.when(k != mp)
            def _():
                got(cls.at[0, k], r_cl.at[0, k])

                @pl.when(chip < WORKERS - 1)
                def _():
                    got(cls.at[1, k], r_cl.at[1, k])

        loop(0, 16, wait_cls)
        rhs = jnp.concatenate(
            [jnp.concatenate([cls[n, k] for k in range(16)], axis=0) for n in range(2)], axis=1
        )
        loop(1, 16, lambda k: got(unit_m.at[lax.rem(dp + 16 - k, 16)], r_un.at[k]))
        lhs = unit_m[...].astype(F32).reshape(64, EMB).astype(BF16)
        scores = jnp.dot(lhs, rhs, preferred_element_type=F32) * 100.0
        lg[...] = scores.reshape(16, 4, 256)
        lr[dp] = lg[dp]

        def send_logits(k):
            to = lax.rem(dp + k, 16)
            copy(lg.at[to], lr.at[dp], s_lg.at[k], r_lg.at[k], to, mp).start()

        loop(1, 16, send_logits)

        def wait_logits(k):
            got(lr.at[lax.rem(dp + 16 - k, 16)], r_lg.at[k])

        loop(1, 16, wait_logits)
        ob[chip] = lr[...].reshape(64, 256).astype(BF16)

        def send_ob(k):
            mine = ob.at[chip]
            copy(mine, mine, s_ob.at[k], r_ob.at[chip], dp, lax.rem(chip + k, 8) * 2).start()

        loop(1, 8, send_ob)
        ob_forward(chip)
        loop(1, 16, lambda k: sent(unit_m.at[0], s_un.at[k]))
        loop(1, 16, lambda k: sent(lg.at[0], s_lg.at[k]))

    @pl.when(core == 0)
    def _():
        for k in range(WORKERS):
            @pl.when(chip != k)
            def _(k=k):
                got(ob.at[k], r_ob.at[k])
                ob_forward(k)

    @pl.when(core == 1)
    def _():
        for k in range(WORKERS):
            got(ob.at[k], r_os.at[k])

    ob_out[...] = ob[...]

    @pl.when(worker)
    def _():
        loop(1, 8, lambda k: sent(ob.at[0], s_ob.at[k]))

    @pl.when(core == 0)
    def _():
        loop(0, WORKERS, lambda k: sent(ob.at[0], s_os.at[k]))


def finish(labels, ob, out, lab_out):
    found = jnp.zeros((4, 128), F32)
    lane = lax.broadcasted_iota(jnp.int32, (4, 128), 1)
    row = lax.broadcasted_iota(jnp.int32, (4, 128), 0)
    label = jnp.full((4, 128), labels[0], jnp.int32)
    for i in range(1, 4):
        label = jnp.where(row == i, labels[i], label)
    for k in range(CLS_BLOCKS):
        vals = ob[k // 2, :, 128 * (k % 2) : 128 * (k % 2) + 128].astype(F32)
        for g in range(16):
            first = (g * CLS_BLOCKS + k) * 128
            piece = vals[4 * g : 4 * g + 4]
            out[:, first : first + 128] = piece
            found = found + jnp.where(lane + first == label, piece, 0.0)
    for i in range(4):
        lab_out[i] = jnp.sum(found[i : i + 1])


def per_device(
    tokens, up_ckpts, up_bias_ckpts, down_ckpts, down_bias_ckpts, norm_ckpts, soup_mask,
    final_gain, projection, class_embed, labels,
):
    vm = pl.BlockSpec(memory_space=pltpu.VMEM)
    sm = pl.BlockSpec(memory_space=pltpu.SMEM)
    hbm = pl.BlockSpec(memory_space=pl.ANY)
    dma = pltpu.SemaphoreType.DMA
    scores = pl.pallas_call(
        kernel,
        out_shape=jax.ShapeDtypeStruct((WORKERS, 64, 256), BF16),
        in_specs=[sm] + [hbm] * 9,
        out_specs=vm,
        scratch_shapes=[
            pltpu.VMEM((2, CKPT, DB, FFB), BF16),
            pltpu.VMEM((2, CKPT, DB, FFB), BF16),
            pltpu.VMEM((TOKS, 4, DB), BF16),
            pltpu.VMEM((CKPT, 2, FFB), F32),
            pltpu.VMEM((CKPT, 2, D), F32),
            pltpu.VMEM((CKPT, 2, D), F32),
            pltpu.VMEM((D,), F32),
            pltpu.VMEM((EMBB, CLS_BLOCKS * 128), BF16),
            pltpu.VMEM((16, 17, 4, DB), BF16),
            pltpu.VMEM((OWN, D), F32),
            pltpu.VMEM((ROWS, D), BF16),
            pltpu.VMEM((ROWS, D), BF16),
            pltpu.VMEM((4, 16, 2 * DB, 256), BF16),
            pltpu.VMEM((D, FFB), BF16),
            pltpu.VMEM((D, FFB), BF16),
            pltpu.VMEM((D, FFB), BF16),
            pltpu.VMEM((D, FFB), BF16),
            pltpu.VMEM((ROWS, FFB), BF16),
            pltpu.VMEM((4, 144, D), BF16),
            pltpu.VMEM((4, 144, D), BF16),
            pltpu.VMEM((4, 144, D), BF16),
            pltpu.VMEM((7, 2, 32, D), BF16),
            pltpu.VMEM((8, 16, D), BF16),
            pltpu.VMEM((16, 4, D), BF16),
            pltpu.VMEM((D, EMB), BF16),
            pltpu.VMEM((16, 4, EMB), BF16),
            pltpu.VMEM((2, 16, EMBB, 128), BF16),
            pltpu.VMEM((16, 4, 256), F32),
            pltpu.VMEM((16, 4, 256), F32),
            pltpu.VMEM((WORKERS, 64, 256), BF16),
            dma((16,)), dma((16,)),
            dma((2, 14)), dma((2, 14)),
            dma((2, 17)), dma((2, 17)),
            dma((6, 15)), dma((6, 15)),
            dma((2, 8)), dma((2, 8)),
            dma((14,)), dma((14,)),
            dma((4,)), dma((4,)),
            dma((2, 8)), dma((10,)),
            dma((8,)), dma((16,)),
            dma((16,)), dma((2, 16)),
            dma((16,)), dma((16,)),
            dma((16,)), dma((16,)),
            dma((8,)), dma((8,)),
            dma((8,)), dma((8,)),
            dma((11,)),
        ],
        compiler_params=pltpu.CompilerParams(
            collective_id=0, has_side_effects=True, vmem_limit_bytes=60 * 2**20
        ),
    )(
        soup_mask, jnp.swapaxes(tokens, 0, 1), up_ckpts, jnp.swapaxes(down_ckpts, 2, 3),
        jnp.swapaxes(up_bias_ckpts, 0, 1), jnp.swapaxes(down_bias_ckpts, 0, 1),
        jnp.swapaxes(norm_ckpts, 0, 1), final_gain, projection, class_embed.T,
    )
    return pl.pallas_call(
        finish,
        out_shape=(
            jax.ShapeDtypeStruct((4, 16 * CLS_BLOCKS * 128), F32),
            jax.ShapeDtypeStruct((4,), F32),
        ),
        in_specs=[sm, vm],
        out_specs=(vm, sm),
    )(labels, scores)


def solution(mesh):
    placed = (
        P("dp", None, "mp"),
        P(None, None, "dp", "mp"),
        P(None, None, "mp"),
        P(None, None, "mp", "dp"),
        P(),
        P(),
        P(),
        P(),
        P(),
        P("dp", "mp"),
        P("dp"),
    )
    return jax.shard_map(
        per_device, mesh=mesh, in_specs=placed, out_specs=(P("dp", None), P("dp")), check_vma=False
    )
```
